128 devices in a mesh: fsdp: 128 (over z, y, x, core).
Axes of the slice: x: 4, y: 4, z: 4, core: 2. Of those that a mesh axis runs over, the one named last changes fastest.
Arguments:
- tokens: bfloat16 [32768, 640], P('fsdp'), may hold values from -6 to 6
- out_grad: bfloat16 [32768, 640], P('fsdp'), may hold values from -6 to 6
- seq_start: int32 [25], replicated, may hold values from 0 to 31744, as said below
- seq_len: int32 [25], replicated, may hold values from 384 to 1024, as said below
- w_query: bfloat16 [640, 1024], P('fsdp'), may hold values from -0.25 to 0.25
- w_key_value: bfloat16 [640, 512], P('fsdp'), may hold values from -0.25 to 0.25
- w_output: bfloat16 [1024, 640], P('fsdp'), may hold values from -0.1875 to 0.1875
- w_gate_up: bfloat16 [640, 4096], P('fsdp'), may hold values from -0.25 to 0.25
- w_down: bfloat16 [2048, 640], P('fsdp'), may hold values from -0.125 to 0.125
- norm_attn_in: bfloat16 [640], P('fsdp'), may hold values from 0.099609375 to 1.8984375
- norm_attn_out: bfloat16 [640], P('fsdp'), may hold values from 0.099609375 to 1.8984375
- norm_mlp_in: bfloat16 [640], P('fsdp'), may hold values from 0.099609375 to 1.8984375
- norm_mlp_out: bfloat16 [640], P('fsdp'), may hold values from 0.099609375 to 1.8984375
- norm_query: bfloat16 [256], P('fsdp'), may hold values from 0.099609375 to 1.8984375
- norm_key: bfloat16 [256], P('fsdp'), may hold values from 0.099609375 to 1.8984375
Outputs:
- mixed: bfloat16 [32768, 640], P('fsdp')
- tokens_grad: bfloat16 [32768, 640], P('fsdp')
- grad_w_query: float32 [640, 1024], P('fsdp')
- grad_w_key_value: float32 [640, 512], P('fsdp')
- grad_w_output: float32 [1024, 640], P('fsdp')
- grad_w_gate_up: float32 [640, 4096], P('fsdp')
- grad_w_down: float32 [2048, 640], P('fsdp')
- grad_norm_attn_in: float32 [640], P('fsdp')
- grad_norm_attn_out: float32 [640], P('fsdp')
- grad_norm_mlp_in: float32 [640], P('fsdp')
- grad_norm_mlp_out: float32 [640], P('fsdp')
- grad_norm_query: float32 [256], P('fsdp')
- grad_norm_key: float32 [256], P('fsdp')
The draws below stay inside these ranges and needn't reach their ends.
Inputs may be any that keep to these rules, and one draw needn't show every extreme that they name: `seq_start`: sequence s starts at a multiple of 128 and lies within the blocks of 128 slots numbered s * 256 // 25 to (s + 1) * 256 // 25 - 1; the first sequence starts at slot 0 and the last one ends at the last slot. `seq_len`: the last sequence has exactly 1024 tokens and another exactly 384.
All inputs are finite; a program needn't handle non-finite values.
Results may differ from the reference program's by a relative error of at most 0.035.
Values may be sent and summed in bfloat16 or wider, within the bound.
No kernel may reach another device: no remote copies, remote signals or barrier semaphores. Data moves between devices by JAX's collectives and lax.ppermute only.
A program may use at most 128 MiB of HBM per device.

```python
import math
import jax
import jax.numpy as jnp
from jax import lax

D = 640
FF = 2048
H = 4
HD = 256
WINDOW = 512
BLOCK = 128
MAXLEN = 1024
MINLEN = 384
TOKENS = 32768
NBLK = 256
NSEQ = 25


def sequence_plan(key):
    key_len, key_short, key_place = jax.random.split(key, 3)
    order = jnp.arange(NSEQ, dtype=jnp.int32)
    lengths = jax.random.randint(key_len, (NSEQ,), MINLEN, MAXLEN + 1)
    long_one = NSEQ - 1
    short_one = jax.random.randint(key_short, (), 0, NSEQ - 1)
    lengths = jnp.where(order == long_one, MAXLEN, jnp.where(order == short_one, MINLEN, lengths))
    blocks = (lengths + BLOCK - 1) // BLOCK
    region_low = order * NBLK // NSEQ
    region_high = (order + 1) * NBLK // NSEQ
    spare_room = region_high - region_low - blocks
    offsets = jax.random.randint(key_place, (NSEQ,), 0, spare_room + 1)
    offsets = jnp.where(order == 0, 0, jnp.where(order == NSEQ - 1, spare_room, offsets))
    starts = (region_low + offsets) * BLOCK
    return (starts.astype(jnp.int32), lengths.astype(jnp.int32))


def draw_seq_start(key, part):
    return sequence_plan(key)[0]


def draw_seq_len(key, part):
    return sequence_plan(key)[1]


def level_of(stream_key, extent, pieces, smallest, largest):
    def one(dim, blocks):
        heights = jax.random.uniform(jax.random.fold_in(jax.random.fold_in(stream_key, 6), dim), (blocks,), jnp.float32, smallest / len(pieces), largest / len(pieces))
        return jnp.repeat(jnp.exp(heights), extent[dim] // blocks).reshape((-1,) + (1,) * (len(extent) - dim - 1))

    level = one(*pieces[0])
    for cut in pieces[1:]:
        level = level * one(*cut)
    return level


def gaussian(own_key, shape, scale, reach, cuts=(), kind=jnp.bfloat16):
    loudness = level_of(own_key, shape, cuts, -0.22, 0.18) if cuts else 1.0
    values = jax.random.normal(own_key, shape, jnp.float32) * scale * loudness
    return jnp.minimum(jnp.maximum(values, -reach), reach).astype(kind)


def setup_inputs(seed: int = 0) -> dict:
    key_list = jax.random.split(jax.random.key(seed), 16)
    return {
        "tokens": gaussian(key_list[0], (TOKENS, D), 1.0, 6.0, ((0, 128),)),
        "out_grad": gaussian(key_list[1], (TOKENS, D), 1.0, 6.0, ((0, 128),)),
        "seq_start": draw_seq_start(jax.random.fold_in(key_list[15], 71), 0),
        "seq_len": draw_seq_len(jax.random.fold_in(key_list[15], 71), 0),
        "w_query": gaussian(key_list[4], (D, H * HD), D ** -0.5, 0.25, ((0, 128),)),
        "w_key_value": gaussian(key_list[5], (D, 2 * HD), D ** -0.5, 0.25, ((0, 128),)),
        "w_output": gaussian(key_list[6], (H * HD, D), (H * HD) ** -0.5, 0.1875, ((0, 128),)),
        "w_gate_up": gaussian(key_list[7], (D, 2 * FF), D ** -0.5, 0.25, ((0, 128),)),
        "w_down": gaussian(key_list[8], (FF, D), FF ** -0.5, 0.125, ((0, 128),)),
        "norm_attn_in": jnp.clip(1.0 + 0.18 * jax.random.normal(key_list[9], (D,), jnp.float32), 0.099609375, 1.8984375).astype(jnp.bfloat16),
        "norm_attn_out": jnp.clip(1.0 + 0.18 * jax.random.normal(key_list[10], (D,), jnp.float32), 0.099609375, 1.8984375).astype(jnp.bfloat16),
        "norm_mlp_in": jnp.clip(1.0 + 0.18 * jax.random.normal(key_list[11], (D,), jnp.float32), 0.099609375, 1.8984375).astype(jnp.bfloat16),
        "norm_mlp_out": jnp.clip(1.0 + 0.18 * jax.random.normal(key_list[12], (D,), jnp.float32), 0.099609375, 1.8984375).astype(jnp.bfloat16),
        "norm_query": jnp.clip(1.0 + 0.18 * jax.random.normal(key_list[13], (HD,), jnp.float32), 0.099609375, 1.8984375).astype(jnp.bfloat16),
        "norm_key": jnp.clip(1.0 + 0.18 * jax.random.normal(key_list[14], (HD,), jnp.float32), 0.099609375, 1.8984375).astype(jnp.bfloat16),
    }


@jax.custom_vjp
def low(v):
    return lax.optimization_barrier(v.astype(jnp.bfloat16)).astype(jnp.float32)

@jax.custom_vjp
def low_back(v):
    return v

def low_keep(v):
    return (low(v), None)

def low_pass(kept, grad):
    return (grad,)

def back_keep(v):
    return (v, None)

def back_low(kept, grad):
    return (low(grad),)
low.defvjp(low_keep, low_pass)
low_back.defvjp(back_keep, back_low)
epsilon = 1e-06
theta_base = 10000.0
query_scale = 0.0625

def matmul(left, right):
    return jnp.dot(left, right, precision=lax.Precision.HIGHEST, preferred_element_type=jnp.float32)

def rms_scale(values, norm_gain):
    mean_sq = lax.optimization_barrier(jnp.mean(values * values, axis=-1, keepdims=True))
    return values * lax.rsqrt(mean_sq + epsilon) * norm_gain

def apply_rope(values, positions):
    half_size = values.shape[-1] // 2
    inv_freq = theta_base ** (-2.0 * jnp.arange(half_size, dtype=jnp.float32) / values.shape[-1])
    angles = positions.astype(jnp.float32)[:, None] * inv_freq[None, :]
    cos_vals = jnp.cos(angles)[:, None, :]
    sin_vals = jnp.sin(angles)[:, None, :]
    first_half = values[..., :half_size]
    second_half = values[..., half_size:]
    return jnp.concatenate([first_half * cos_vals - second_half * sin_vals, second_half * cos_vals + first_half * sin_vals], axis=-1)

def token_layout(seq_start, seq_len, first_token, token_count):
    indices = first_token + jnp.arange(token_count, dtype=jnp.int32)
    offsets = indices[:, None] - seq_start[None, :]
    inside = (offsets >= 0) & (offsets < seq_len[None, :])
    live_mask = jnp.any(inside, axis=1)
    seq_numbers = jnp.arange(seq_start.shape[0], dtype=jnp.int32)
    seq_id = lax.optimization_barrier(jnp.sum(jnp.where(inside, seq_numbers[None, :], 0), axis=1)).astype(jnp.int32)
    seq_id = jnp.where(live_mask, seq_id, -1).astype(jnp.int32)
    positions = lax.optimization_barrier(jnp.sum(jnp.where(inside, offsets, 0), axis=1)).astype(jnp.int32)
    return (indices, seq_id, positions, live_mask)

def allowed_mask(q_index, q_seq, k_index, k_seq):
    distance = q_index[:, None] - k_index[None, :]
    same_seq = (q_seq[:, None] == k_seq[None, :]) & (q_seq[:, None] >= 0) & (distance >= 0) & (distance < WINDOW)
    return same_seq | (distance == 0)

def reference(tokens, out_grad, seq_start, seq_len, w_query, w_key_value, w_output, w_gate_up, w_down, norm_attn_in, norm_attn_out, norm_mlp_in, norm_mlp_out, norm_query, norm_key):
    indices, seq_id, positions, live_mask = token_layout(seq_start, seq_len, jnp.int32(0), TOKENS)
    live = live_mask.astype(jnp.float32)[:, None]
    block_rows = math.gcd(TOKENS, 512)
    pad_index = jnp.arange(-WINDOW, TOKENS, dtype=jnp.int32)
    pad_seq = jnp.concatenate([jnp.full((WINDOW,), -1, jnp.int32), seq_id]).astype(jnp.int32)
    starts = (jnp.arange(TOKENS // block_rows, dtype=jnp.int32) * block_rows).astype(jnp.int32)

    def attention(query_rot, key_rot, value_low):
        key_pad = jnp.concatenate([jnp.zeros((WINDOW, HD), jnp.float32), key_rot], axis=0)
        value_pad = jnp.concatenate([jnp.zeros((WINDOW, HD), jnp.float32), value_low], axis=0)

        def one_block(start):
            query_part = lax.dynamic_slice_in_dim(query_rot, start, block_rows, 0)
            key_part = lax.dynamic_slice_in_dim(key_pad, start, block_rows + WINDOW, 0)
            value_part = lax.dynamic_slice_in_dim(value_pad, start, block_rows + WINDOW, 0)
            q_index = lax.dynamic_slice_in_dim(indices, start, block_rows, 0)
            q_seq = lax.dynamic_slice_in_dim(seq_id, start, block_rows, 0)
            k_index = lax.dynamic_slice_in_dim(pad_index, start, block_rows + WINDOW, 0)
            k_seq = lax.dynamic_slice_in_dim(pad_seq, start, block_rows + WINDOW, 0)
            allowed = allowed_mask(q_index, q_seq, k_index, k_seq)
            scores = jnp.einsum('thd,kd->htk', query_part, key_part, precision=lax.Precision.HIGHEST) * query_scale
            scores = low_back(scores)
            masked = jnp.where(allowed[None], scores, -jnp.inf)
            weights = low(jax.nn.softmax(masked, axis=-1))
            return jnp.einsum('htk,kd->thd', weights, value_part, precision=lax.Precision.HIGHEST)
        parts = lax.map(jax.checkpoint(one_block), starts)
        return parts.reshape(TOKENS, H * HD)

    def forward(inputs, wq_full, wkv_full, wo_full, wgu_full, wd_full, gain_ai, gain_ao, gain_mi, gain_mo, gain_q, gain_k):
        attn_in = low(rms_scale(inputs, gain_ai))
        query_raw = low_back(matmul(attn_in, wq_full)).reshape(TOKENS, H, HD)
        key_value = low_back(matmul(attn_in, wkv_full))
        key_raw = key_value[:, None, :HD]
        query_rot = low(apply_rope(rms_scale(query_raw, gain_q), positions))
        key_rot = low(apply_rope(rms_scale(key_raw, gain_k), positions))[:, 0, :]
        value_low = low(key_value[:, HD:])
        heads_out = low(low_back(attention(query_rot, key_rot, value_low)))
        attn_proj = low_back(matmul(heads_out, wo_full))
        state = inputs + rms_scale(attn_proj, gain_ao)
        mlp_in = low(rms_scale(state, gain_mi))
        gate_up = low_back(matmul(mlp_in, wgu_full))
        hidden = low(jax.nn.gelu(gate_up[:, :FF], approximate=True) * gate_up[:, FF:])
        branch = low_back(matmul(hidden, wd_full))
        return live * (state + rms_scale(branch, gain_mo))
    floats = [item.astype(jnp.float32) for item in (tokens, w_query, w_key_value, w_output, w_gate_up, w_down, norm_attn_in, norm_attn_out, norm_mlp_in, norm_mlp_out, norm_query, norm_key)]
    mixed, pullback = jax.vjp(forward, *floats)
    grads = pullback(out_grad.astype(jnp.float32))
    return (mixed.astype(jnp.bfloat16), grads[0].astype(jnp.bfloat16), grads[1], grads[2], grads[3], grads[4], grads[5], grads[6], grads[7], grads[8], grads[9], grads[10], grads[11])
```

```python
import jax
import jax.numpy as jnp
from jax import lax
from jax.sharding import PartitionSpec as P

WINDOW = 512


epsilon = 1e-06
theta_base = 10000.0
query_scale = 0.0625


def shifted(block, axis, distance):
    devices = range(lax.axis_size(axis))
    route = [(i - distance, i) for i in devices if i - distance in devices]
    return lax.ppermute(block, axis, route)


def rms_scale(values, norm_gain):
    mean_sq = jnp.mean(values * values, axis=-1, keepdims=True)
    return values * lax.rsqrt(mean_sq + epsilon) * norm_gain


def apply_rope(values, positions):
    half_size = values.shape[-1] // 2
    inv_freq = theta_base ** (-2.0 * jnp.arange(half_size, dtype=jnp.float32) / values.shape[-1])
    angles = positions.astype(jnp.float32)[:, None] * inv_freq[None, :]
    cos_vals = jnp.cos(angles)[:, None, :]
    sin_vals = jnp.sin(angles)[:, None, :]
    first_half = values[..., :half_size]
    second_half = values[..., half_size:]
    return jnp.concatenate(
        [
            first_half * cos_vals - second_half * sin_vals,
            second_half * cos_vals + first_half * sin_vals,
        ],
        axis=-1,
    )


def token_layout(seq_start, seq_len, first_token, token_count):
    indices = first_token + jnp.arange(token_count, dtype=jnp.int32)
    offsets = indices[:, None] - seq_start[None, :]
    inside = (offsets >= 0) & (offsets < seq_len[None, :])
    live_mask = jnp.any(inside, axis=1)
    seq_numbers = jnp.arange(seq_start.shape[0], dtype=jnp.int32)
    seq_id = jnp.sum(jnp.where(inside, seq_numbers[None, :], 0), axis=1)
    seq_id = jnp.where(live_mask, seq_id, -1)
    positions = jnp.sum(jnp.where(inside, offsets, 0), axis=1)
    return (indices, seq_id, positions, live_mask)


def allowed_mask(q_index, q_seq, k_index, k_seq):
    distance = q_index[:, None] - k_index[None, :]
    same_seq = (
        (q_seq[:, None] == k_seq[None, :])
        & (q_seq[:, None] >= 0)
        & (distance >= 0)
        & (distance < WINDOW)
    )
    return same_seq | (distance == 0)


def matmul(left, right):
    return jnp.dot(left, right, preferred_element_type=jnp.float32)


SHARD_ROWS = 8


def same_core_groups(size):
    return [[2 * chip + core for chip in range(size // 2)] for core in range(2)]


def swap_cores(block):
    size = lax.axis_size("fsdp")
    return lax.ppermute(block, "fsdp", [(i, i ^ 1) for i in range(size)])


def exchange(blocks):
    size = lax.axis_size("fsdp")
    return lax.all_to_all(
        blocks, "fsdp", split_axis=0, concat_axis=0, tiled=True,
        axis_index_groups=same_core_groups(size),
    )


def spread(block):
    chips = lax.axis_size("fsdp") // 2
    return exchange(jnp.broadcast_to(block[None], (chips,) + block.shape))


def in_core_order(own, peer, core):
    return jnp.where(core == 0, jnp.stack([own, peer], 1), jnp.stack([peer, own], 1))


def summed(parts):
    own, other = parts
    both = own.astype(jnp.float32) + swap_cores(other).astype(jnp.float32)
    return jnp.sum(exchange(both.astype(jnp.bfloat16)).astype(jnp.float32), axis=0)


def unpermute(values, selector):
    high = values.astype(jnp.bfloat16)
    low = (values - high.astype(jnp.float32)).astype(jnp.bfloat16)
    return matmul(high, selector.T) + matmul(low, selector.T)


def on_device(
    tokens,
    out_grad,
    seq_start,
    seq_len,
    w_query,
    w_key_value,
    w_output,
    w_gate_up,
    w_down,
    norm_attn_in,
    norm_attn_out,
    norm_mlp_in,
    norm_mlp_out,
    norm_query,
    norm_key,
):
    bf16 = jnp.bfloat16
    size = lax.axis_size("fsdp")
    chips = size // 2
    me = lax.axis_index("fsdp")
    core = me % 2
    tok_rows, width = tokens.shape
    shard = w_query.shape[0]
    q_cols, kv_cols = w_query.shape[1], w_key_value.shape[1]
    gu_cols = w_gate_up.shape[1]
    out_rows, down_rows = w_output.shape[0], w_down.shape[0]
    head_size = kv_cols // 2
    num_heads = q_cols // head_size
    ff_width = gu_cols // 2
    hshard = norm_query.shape[0]

    pad = SHARD_ROWS - shard
    pack_mlp = jnp.concatenate(
        [jnp.pad(w_gate_up, ((0, pad), (0, 0))), w_down[:SHARD_ROWS], w_down[SHARD_ROWS:]], axis=1
    )
    mlp_full = lax.all_gather(pack_mlp, "fsdp", axis=0, tiled=True)

    gains = jnp.concatenate(
        [norm_attn_in, norm_attn_out, norm_mlp_in, norm_mlp_out, norm_query, norm_key]
    )
    gain_count = gains.shape[0]
    pack_attn = jnp.concatenate(
        [
            jnp.concatenate([w_query, w_key_value], axis=1),
            jnp.pad(gains, (0, q_cols + kv_cols - gain_count))[None],
            jnp.zeros((pad - 1, q_cols + kv_cols), bf16),
        ],
        axis=0,
    )
    own_attn = spread(pack_attn)
    peer_attn = swap_cores(own_attn)
    qkv_rel = jnp.concatenate([own_attn, peer_attn], axis=0).reshape(-1, q_cols + kv_cols)
    own_out = spread(w_output)
    peer_out = swap_cores(own_out)
    output_full = in_core_order(own_out, peer_out, core).reshape(-1, width)
    all_gains = in_core_order(
        own_attn[:, shard, :gain_count], peer_attn[:, shard, :gain_count], core
    ).reshape(size, gain_count).astype(jnp.float32)
    gain_in, gain_out, gain_mlp_in, gain_mlp_out = [
        all_gains[:, i * shard : (i + 1) * shard].reshape(-1) for i in range(4)
    ]
    gain_query, gain_key = [
        all_gains[:, 4 * shard + i * hshard : 4 * shard + (i + 1) * hshard].reshape(-1)
        for i in range(2)
    ]

    place = jnp.arange(size * SHARD_ROWS, dtype=jnp.int32)
    row_in = place % SHARD_ROWS
    rel_core = place // (chips * SHARD_ROWS)
    rel_chip = (place // SHARD_ROWS) % chips
    rel_source = jnp.where(
        row_in < shard, (rel_chip * 2 + (rel_core ^ core)) * shard + row_in, -1
    )
    flat_source = jnp.where(row_in < shard, (place // SHARD_ROWS) * shard + row_in, -1)
    natural = jnp.arange(width, dtype=jnp.int32)[:, None]
    to_rel = (natural == rel_source[None]).astype(bf16)
    to_flat = (natural == flat_source[None]).astype(bf16)

    key_reach = (WINDOW + tok_rows - 2) // tok_rows
    first_token = me * tok_rows
    q_index, q_seq, q_pos, q_live = token_layout(seq_start, seq_len, first_token, tok_rows)
    k_index, k_seq, k_pos, k_live = token_layout(
        seq_start, seq_len, first_token - key_reach * tok_rows, (key_reach + 1) * tok_rows
    )
    allowed = allowed_mask(q_index, q_seq, k_index, k_seq)[None]
    live = q_live.astype(jnp.float32)[:, None]
    inputs = tokens.astype(jnp.float32)
    attn_in, attn_in_back = jax.vjp(rms_scale, inputs, gain_in)
    attn_in_low = attn_in.astype(bf16)
    attn_in_rel = matmul(attn_in_low, to_rel).astype(bf16)
    qkv_raw = matmul(attn_in_rel, qkv_rel)
    query_raw = qkv_raw[:, :q_cols].reshape(tok_rows, num_heads, head_size)
    keyval_raw = qkv_raw[:, q_cols:]

    def prepare(query_part, key_part, gain_q, gain_k):
        return (
            apply_rope(rms_scale(query_part, gain_q), q_pos),
            apply_rope(rms_scale(key_part, gain_k), q_pos),
        )

    (query_rot, key_rot), prepare_back = jax.vjp(
        prepare, query_raw, keyval_raw[:, None, :head_size], gain_query, gain_key
    )
    query_low = query_rot.astype(bf16)
    own_keys = jnp.concatenate([key_rot[:, 0, :], keyval_raw[:, head_size:]], axis=1).astype(bf16)
    key_parts = []
    for shift_by in range(key_reach, 0, -1):
        key_parts.append(shifted(own_keys, "fsdp", shift_by))
    all_keys = jnp.concatenate(key_parts + [own_keys], axis=0)
    key_low = all_keys[:, :head_size]
    value_low = all_keys[:, head_size:]
    scores = (
        jnp.einsum("thd,kd->htk", query_low, key_low, preferred_element_type=jnp.float32)
        * query_scale
    )
    masked = jnp.where(allowed, scores, -jnp.inf)
    row_max = jnp.max(masked, axis=-1, keepdims=True)
    exp_terms = jnp.exp(masked - row_max)
    row_total = jnp.sum(exp_terms, axis=-1, keepdims=True)
    probs = exp_terms / row_total
    probs_low = probs.astype(bf16)
    heads_out = jnp.einsum("htk,kd->thd", probs_low, value_low, preferred_element_type=jnp.float32)
    heads_low = heads_out.reshape(tok_rows, num_heads * head_size).astype(bf16)
    attn_proj = matmul(heads_low, output_full)
    state, residual_back = jax.vjp(
        lambda projected, gain_vec: inputs + rms_scale(projected, gain_vec), attn_proj, gain_out
    )
    gateup_flat = mlp_full[:, :gu_cols]
    down_full = jnp.concatenate(
        [
            mlp_full[:, gu_cols : gu_cols + width].reshape(size, SHARD_ROWS, width),
            mlp_full[:, gu_cols + width :].reshape(size, SHARD_ROWS, width),
        ],
        axis=1,
    ).reshape(-1, width)
    mlp_in, mlp_in_back = jax.vjp(rms_scale, state, gain_mlp_in)
    mlp_in_low = mlp_in.astype(bf16)
    mlp_in_flat = matmul(mlp_in_low, to_flat).astype(bf16)
    mlp_in_rel = matmul(mlp_in_low, to_rel).astype(bf16)
    gate_up = matmul(mlp_in_flat, gateup_flat)

    def activate(both):
        return jax.nn.gelu(both[:, :ff_width], approximate=True) * both[:, ff_width:]

    hidden, activate_back = jax.vjp(activate, gate_up)
    hidden_low = hidden.astype(bf16)
    branch = matmul(hidden_low, down_full)
    final, final_back = jax.vjp(
        lambda state_in, branch_in, gain_vec: state_in + rms_scale(branch_in, gain_vec),
        state,
        branch,
        gain_mlp_out,
    )
    mixed = (final * live).astype(bf16)
    cotangent = out_grad.astype(jnp.float32) * live
    d_state_top, d_branch, grad_mlp_out = final_back(cotangent)
    branch_low = d_branch.astype(bf16)
    d_hidden = matmul(branch_low, down_full.T)
    (d_gate_up,) = activate_back(d_hidden)
    gate_up_low = d_gate_up.astype(bf16)
    grad_down = matmul(hidden_low.T, branch_low).astype(bf16)
    down_parts = grad_down.reshape(chips, 2, down_rows, width)
    share_down = summed(
        (
            lax.dynamic_index_in_dim(down_parts, core, 1, keepdims=False),
            lax.dynamic_index_in_dim(down_parts, 1 - core, 1, keepdims=False),
        )
    )
    grad_gate_up = matmul(mlp_in_rel.T, gate_up_low).astype(bf16)
    gu_parts = grad_gate_up.reshape(2, chips, SHARD_ROWS, gu_cols)
    share_gate_up = summed((gu_parts[0], gu_parts[1]))[:shard]
    d_mlp_in = unpermute(matmul(gate_up_low, gateup_flat.T), to_flat)
    d_state_norm, grad_mlp_in = mlp_in_back(d_mlp_in)
    d_state = d_state_top + d_state_norm
    d_proj, grad_attn_out = residual_back(d_state)
    proj_low = d_proj.astype(bf16)
    d_heads = matmul(proj_low, output_full.T).astype(bf16).reshape(tok_rows, num_heads, head_size)
    grad_output = matmul(heads_low.T, proj_low).astype(bf16)
    output_parts = grad_output.reshape(chips, 2, out_rows, width)
    share_output = summed(
        (
            lax.dynamic_index_in_dim(output_parts, core, 1, keepdims=False),
            lax.dynamic_index_in_dim(output_parts, 1 - core, 1, keepdims=False),
        )
    )
    d_probs = jnp.einsum("thd,kd->htk", d_heads, value_low, preferred_element_type=jnp.float32)
    row_dot = jnp.sum(probs * d_probs, axis=-1, keepdims=True)
    d_scores = (probs * (d_probs - row_dot)).astype(bf16)
    d_query_rot = (
        jnp.einsum("htk,kd->thd", d_scores, key_low, preferred_element_type=jnp.float32)
        * query_scale
    )
    d_keys = (
        jnp.einsum("htk,thd->kd", d_scores, query_low, preferred_element_type=jnp.float32)
        * query_scale
    )
    d_values = jnp.einsum("htk,thd->kd", probs_low, d_heads, preferred_element_type=jnp.float32)
    key_grads = jnp.concatenate([d_keys, d_values], axis=1)
    own_grads = key_grads[key_reach * tok_rows :]
    for shift_by in range(1, key_reach + 1):
        lower = (key_reach - shift_by) * tok_rows
        own_grads = own_grads + shifted(
            key_grads[lower : lower + tok_rows].astype(bf16), "fsdp", -shift_by
        ).astype(jnp.float32)
    d_query_raw, d_key_raw, grad_query_gain, grad_key_gain = prepare_back(
        (d_query_rot, own_grads[:, None, :head_size])
    )
    qkv_grad_low = jnp.concatenate(
        [
            d_query_raw.reshape(tok_rows, num_heads * head_size),
            d_key_raw[:, 0, :],
            own_grads[:, head_size:],
        ],
        axis=1,
    ).astype(bf16)
    grad_qkv = matmul(attn_in_rel.T, qkv_grad_low).astype(bf16)
    d_attn_in = unpermute(matmul(qkv_grad_low, qkv_rel.T), to_rel)
    d_inputs, grad_attn_in = attn_in_back(d_attn_in)
    tokens_grad = (d_state + d_inputs).astype(bf16)
    gain_grads = jnp.concatenate(
        [
            vector.reshape(size, -1)
            for vector in (
                grad_attn_in, grad_attn_out, grad_mlp_in, grad_mlp_out,
                grad_query_gain, grad_key_gain,
            )
        ],
        axis=1,
    ).reshape(chips, 2, gain_count)
    gain_grads = jnp.stack(
        [
            lax.dynamic_index_in_dim(gain_grads, core, 1, keepdims=False),
            lax.dynamic_index_in_dim(gain_grads, 1 - core, 1, keepdims=False),
        ]
    ).astype(bf16)
    qkv_parts = grad_qkv.reshape(2, chips, SHARD_ROWS, q_cols + kv_cols)
    qkv_parts = qkv_parts.at[:, :, shard, :gain_count].set(gain_grads)
    share_attn = summed((qkv_parts[0], qkv_parts[1]))
    share_gains = share_attn[shard, :gain_count]
    return (
        mixed,
        tokens_grad,
        share_attn[:shard, :q_cols],
        share_attn[:shard, q_cols:],
        share_output,
        share_gate_up,
        share_down,
        share_gains[:shard],
        share_gains[shard : 2 * shard],
        share_gains[2 * shard : 3 * shard],
        share_gains[3 * shard : 4 * shard],
        share_gains[4 * shard : 4 * shard + hshard],
        share_gains[4 * shard + hshard :],
    )


def solution(mesh):
    placed = (
        P("fsdp", None),
        P("fsdp", None),
        P(),
        P(),
        P("fsdp", None),
        P("fsdp", None),
        P("fsdp", None),
        P("fsdp", None),
        P("fsdp", None),
        P("fsdp"),
        P("fsdp"),
        P("fsdp"),
        P("fsdp"),
        P("fsdp"),
        P("fsdp"),
    )
    return jax.shard_map(
        on_device,
        mesh=mesh,
        in_specs=placed,
        out_specs=(
            P("fsdp", None),
            P("fsdp", None),
            P("fsdp", None),
            P("fsdp", None),
            P("fsdp", None),
            P("fsdp", None),
            P("fsdp", None),
            P("fsdp"),
            P("fsdp"),
            P("fsdp"),
            P("fsdp"),
            P("fsdp"),
            P("fsdp"),
        ),
        check_vma=False,
    )
```

```python
import jax
import jax.numpy as jnp
from jax import lax
from jax.experimental import pallas as pl
from jax.experimental.pallas import tpu as pltpu
from jax.sharding import PartitionSpec as P

WINDOW = 512


epsilon = 1e-06
theta_base = 10000.0
query_scale = 0.0625


def shifted(block, axis, distance):
    devices = range(lax.axis_size(axis))
    route = [(i - distance, i) for i in devices if i - distance in devices]
    return lax.ppermute(block, axis, route)


def token_layout(seq_start, seq_len, first_token, token_count):
    indices = first_token + jnp.arange(token_count, dtype=jnp.int32)
    offsets = indices[:, None] - seq_start[None, :]
    inside = (offsets >= 0) & (offsets < seq_len[None, :])
    live_mask = jnp.any(inside, axis=1)
    seq_numbers = jnp.arange(seq_start.shape[0], dtype=jnp.int32)
    seq_id = jnp.sum(jnp.where(inside, seq_numbers[None, :], 0), axis=1)
    seq_id = jnp.where(live_mask, seq_id, -1)
    positions = jnp.sum(jnp.where(inside, offsets, 0), axis=1)
    return (indices, seq_id, positions, live_mask)


BF16 = jnp.bfloat16
F32 = jnp.float32
SLOTS = 8
GAIN_SLOT = 5
MASKED = -1e30
VMEM_BYTES = 56 * 1024 * 1024
LANES = 128


def same_core_groups(size):
    return [[2 * chip + core for chip in range(size // 2)] for core in range(2)]


def swap_cores(block):
    size = lax.axis_size("fsdp")
    return lax.ppermute(block, "fsdp", [(i, i ^ 1) for i in range(size)])


def exchange(blocks):
    return lax.all_to_all(
        blocks,
        "fsdp",
        split_axis=0,
        concat_axis=0,
        tiled=True,
        axis_index_groups=same_core_groups(lax.axis_size("fsdp")),
    )


def spread(block):
    chips = lax.axis_size("fsdp") // 2
    return exchange(jnp.broadcast_to(block[None], (chips,) + block.shape))


def call(kernel, outs, ins, scratch=(), specs=None, flops=4e9):
    return pl.pallas_call(
        kernel,
        out_shape=outs,
        in_specs=specs,
        scratch_shapes=list(scratch),
        compiler_params=pltpu.CompilerParams(vmem_limit_bytes=VMEM_BYTES),
        cost_estimate=pl.CostEstimate(
            flops=int(flops), bytes_accessed=8_000_000, transcendentals=0
        ),
    )(*ins)


SCALAR = pl.BlockSpec(memory_space=pltpu.SMEM)
WHOLE = pl.BlockSpec(memory_space=pltpu.VMEM)
AWAY = pl.BlockSpec(memory_space=pl.ANY)


def shape(dims, kind):
    return jax.ShapeDtypeStruct(dims, kind)


def dot(left, right):
    return jnp.dot(left, right, preferred_element_type=F32)


def dot_nt(left, right):
    return lax.dot_general(left, right, (((1,), (1,)), ((), ())), preferred_element_type=F32)


def dot_tn(left, right):
    return lax.dot_general(left, right, (((0,), (0,)), ((), ())), preferred_element_type=F32)


def normed(values):
    scale = lax.rsqrt(jnp.mean(values * values, axis=-1, keepdims=True) + epsilon)
    return values * scale, scale


def normed_back(cot, unit, scale, gain):
    weighted = cot * gain
    inner = jnp.mean(weighted * unit, axis=-1, keepdims=True)
    return scale * (weighted - unit * inner), jnp.sum(cot * unit, axis=0, keepdims=True)


def ones_where(mask):
    return jnp.where(mask, 1.0, 0.0).astype(BF16)


def places(count):
    place = lax.broadcasted_iota(jnp.int32, (1, count), 1)
    return lax.shift_right_logical(place, 3), place & (SLOTS - 1)


def pick_rows(rows, count, per, core):
    block, slot = places(count)
    device = block if core is None else 2 * block + core
    source = jnp.where(slot < per, device * per + slot, -1)
    return ones_where(lax.broadcasted_iota(jnp.int32, (rows, count), 0) == source)


def pick_slot(rows, count, per, core):
    block, slot = places(count)
    low = jnp.where(slot == GAIN_SLOT, (2 * block + core) * per, -2 * rows)
    natural = lax.broadcasted_iota(jnp.int32, (rows, count), 0)
    return ones_where((natural >= low) & (natural < low + per))


def gain_mask(first, per, rows, columns):
    row = lax.broadcasted_iota(jnp.int32, (rows, columns), 0)
    column = lax.broadcasted_iota(jnp.int32, (rows, columns), 1)
    return row == first + lax.rem(column, per)


def turned(values, cos, sin):
    half = values.shape[-1] // 2
    first, second = values[:, :half], values[:, half:]
    return jnp.concatenate([first * cos - second * sin, second * cos + first * sin], axis=1)


def before_attention(
    core_ref, tok, own, peer, cos, sin, attn_rel, raw, query_low, own_kv, gains, head_gains
):
    core = core_ref[0]
    width, rows = tok.shape[1], own.shape[0]
    kv_cols = own_kv.shape[1]
    head = kv_cols // 2
    q_cols = query_low.shape[1]
    per, per_head = width // LANES, head // LANES

    def gather(natural, count):
        mine = dot(pick_slot(natural, rows, count, core), own[:, :LANES])
        theirs = dot(pick_slot(natural, rows, count, 1 - core), peer[:, :LANES])
        return jnp.transpose(mine + theirs)[:32]

    wide = gather(width, per)
    for which in range(4):
        mask = gain_mask(which * per, per, 32, width)
        gains[which : which + 1, :] = jnp.sum(jnp.where(mask, wide, 0.0), 0, keepdims=True)
    narrow = gather(head, per_head)
    for which in range(2):
        mask = gain_mask(4 * per + which * per_head, per_head, 32, head)
        head_gains[which : which + 1, :] = jnp.sum(jnp.where(mask, narrow, 0.0), 0, keepdims=True)
    unit, _ = normed(tok[...].astype(F32))
    low = (unit * gains[0:1, :]).astype(BF16)
    attn_rel[:, :rows] = dot(low, pick_rows(width, rows, per, core)).astype(BF16)
    attn_rel[:, rows:] = dot(low, pick_rows(width, rows, per, 1 - core)).astype(BF16)
    columns = q_cols + kv_cols
    raw[...] = dot(attn_rel[:, :rows], own[:, :columns]) + dot(attn_rel[:, rows:], peer[:, :columns])
    for index in range(q_cols // head):
        span = slice(index * head, (index + 1) * head)
        unit, _ = normed(raw[:, span])
        query_low[:, span] = turned(unit * head_gains[0:1, :], cos[...], sin[...]).astype(BF16)
    unit, _ = normed(raw[:, q_cols : q_cols + head])
    own_kv[:, :head] = turned(unit * head_gains[1:2, :], cos[...], sin[...]).astype(BF16)
    own_kv[:, head:] = raw[:, q_cols + head :].astype(BF16)


def visible(q_seq, k_seq):
    queries, keys = q_seq.shape[0], k_seq.shape[1]
    row = lax.broadcasted_iota(jnp.int32, (queries, keys), 0)
    column = lax.broadcasted_iota(jnp.int32, (queries, keys), 1)
    distance = row - column + (keys - queries)
    same = (q_seq[...] == k_seq[...]) & (q_seq[...] >= 0)
    return (same & (distance >= 0) & (distance < WINDOW)) | (distance == 0)


def attention(
    core_ref, query_low, kv_far, kv_near, kv_own, q_seq, k_seq, own, peer, tok, gains,
    heads_low, log_total, proj, state,
):
    core = core_ref[0]
    head = kv_own.shape[1] // 2
    width, rows = tok.shape[1], own.shape[0]
    q_cols = query_low.shape[1]
    parts = (kv_far, kv_near, kv_own)
    keys = jnp.concatenate([part[:, :head] for part in parts], axis=0)
    values = jnp.concatenate([part[:, head:] for part in parts], axis=0)
    allowed = visible(q_seq, k_seq)
    for index in range(q_cols // head):
        span = slice(index * head, (index + 1) * head)
        scores = dot_nt(query_low[:, span], keys) * query_scale
        scores = jnp.where(allowed, scores, MASKED)
        top = jnp.max(scores, axis=-1, keepdims=True)
        terms = jnp.exp(scores - top)
        total = jnp.sum(terms, axis=-1, keepdims=True)
        probs = (terms * (1.0 / total)).astype(BF16)
        heads_low[:, span] = dot(probs, values).astype(BF16)
        log_total[:, index : index + 1] = top + jnp.log(total)
    offset = own.shape[1] - width
    heads = heads_low[...]
    first = dot(heads, pick_rows(q_cols, rows, SLOTS, core)).astype(BF16)
    second = dot(heads, pick_rows(q_cols, rows, SLOTS, 1 - core)).astype(BF16)
    proj[...] = dot(first, own[:, offset:]) + dot(second, peer[:, offset:])
    unit, _ = normed(proj[...])
    state[...] = tok[...].astype(F32) + unit * gains[1:2, :]


def feed_forward(
    core_ref, state, proj, out_grad, live, gains, heads_low, own, peer, gate_up, own_down, peer_down,
    mixed, d_state, d_heads, gain_grads, keep, send,
    weights, down, act, act_slope, hidden, total, back, low_flat, low, low_branch, turn, turn_down,
    turn_out, weight_sem, down_sem,
):
    core = core_ref[0]
    tiles, tile = weights.shape[0], weights.shape[2]
    half = tiles // 2
    width = state.shape[1]
    rows = own.shape[0]
    q_cols = heads_low.shape[1]
    per = width // LANES
    down_rows = own_down.shape[1]
    blocks, strips = keep.shape[0], keep.shape[1]
    block_rows = width // blocks
    tile_chips = tile // (2 * down_rows)

    def weight_copy(index):
        return pltpu.make_async_copy(
            gate_up.at[:, pl.ds(pl.multiple_of(index * tile, tile), tile)],
            weights.at[index],
            weight_sem.at[index],
        )

    down_copies = (
        pltpu.make_async_copy(own_down, down.at[:, core], down_sem.at[0]),
        pltpu.make_async_copy(peer_down, down.at[:, 1 - core], down_sem.at[1]),
    )
    for index in range(half):
        weight_copy(index).start()
        weight_copy(half + index).start()
        if index == 0:
            for copy in down_copies:
                copy.start()

    spread_flat = pick_rows(width, weights.shape[1], per, None)
    unit, scale = normed(state[...])
    low[...] = (unit * gains[2:3, :]).astype(BF16)
    low_flat[...] = dot(low[...], spread_flat).astype(BF16)
    total[...] = jnp.zeros_like(total)
    for copy in down_copies:
        copy.wait()

    def down_tile(index):
        chunk = down[pl.ds(index * tile_chips, tile_chips)]
        return chunk.reshape(tile, width)

    def forward(index, carry):
        columns = pl.ds(pl.multiple_of(index * tile, tile), tile)
        weight_copy(index).wait()
        weight_copy(half + index).wait()
        gate = dot(low_flat[...], weights[index])
        up = dot(low_flat[...], weights[half + index])
        square = gate * gate
        bend = jnp.tanh(gate * (0.7978845608028654 * (1.0 + 0.044715 * square)))
        rise = 0.5 * (1.0 + bend)
        gelu = gate * rise
        slope = rise + 0.5 * gate * (1.0 - bend * bend) * (
            0.7978845608028654 * (1.0 + 0.134145 * square)
        )
        act[:, columns] = gelu
        act_slope[:, columns] = up * slope
        hidden[:, columns] = (gelu * up).astype(BF16)
        total[...] += dot(hidden[:, columns], down_tile(index))
        return carry

    lax.fori_loop(0, half, forward, 0)

    branch_unit, branch_scale = normed(total[...])
    mixed[...] = ((state[...] + branch_unit * gains[3:4, :]) * live[...]).astype(BF16)
    cotangent = out_grad[...].astype(F32) * live[...]
    d_branch, gain_grads[3:4, :] = normed_back(
        cotangent, branch_unit, branch_scale, gains[3:4, :]
    )
    low_branch[...] = d_branch.astype(BF16)
    back[...] = jnp.zeros_like(back)

    def place(strip, grads):
        turn[0] = grads[:, : tile // 2].astype(BF16)
        turn[1] = grads[:, tile // 2 :].astype(BF16)
        for target, parity in ((keep, core), (send, 1 - core)):
            for part in range(tile // 2 // LANES):
                target[:, strip, part * block_rows : (part + 1) * block_rows, :] = turn[
                    parity, :, part * LANES : (part + 1) * LANES
                ].reshape(blocks, block_rows, LANES)

    down_at = block_rows * (tile // 2 // LANES)
    out_at = down_at + down_rows * (width // LANES)

    def backward(index, carry):
        columns = pl.ds(pl.multiple_of(index * tile, tile), tile)
        d_hidden = dot_nt(low_branch[...], down_tile(index))
        d_gate = (d_hidden * act_slope[:, columns]).astype(BF16)
        d_up = (d_hidden * act[:, columns]).astype(BF16)
        back[...] += dot_nt(d_gate, weights[index]) + dot_nt(d_up, weights[half + index])
        place(index, dot_tn(low[...], d_gate))
        place(half + index, dot_tn(low[...], d_up))
        turn_down[...] = (
            dot_tn(hidden[:, columns], low_branch[...])
            .astype(BF16)
            .reshape(tile_chips // strips, strips, 2, down_rows, width)
        )
        tall = pl.ds(index * (tile_chips // strips), tile_chips // strips)
        for target, parity in ((keep, core), (send, 1 - core)):
            for part in range(width // LANES):
                top = down_at + part * down_rows
                target[tall, :, top : top + down_rows, :] = turn_down[
                    :, :, parity, :, part * LANES : (part + 1) * LANES
                ]
        return carry

    lax.fori_loop(0, half, backward, 0)

    high = back[...].astype(BF16)
    rest = (back[...] - high.astype(F32)).astype(BF16)
    d_low = dot_nt(high, spread_flat) + dot_nt(rest, spread_flat)
    d_norm, gain_grads[2:3, :] = normed_back(d_low, unit, scale, gains[2:3, :])
    d_state[...] = cotangent + d_norm
    proj_unit, proj_scale = normed(proj[...])
    d_proj, gain_grads[1:2, :] = normed_back(d_state[...], proj_unit, proj_scale, gains[1:2, :])
    proj_low = d_proj.astype(BF16)
    offset = own.shape[1] - width
    first = dot_nt(proj_low, own[:, offset:]).astype(BF16)
    second = dot_nt(proj_low, peer[:, offset:]).astype(BF16)
    d_heads[...] = (
        dot_nt(first, pick_rows(q_cols, rows, SLOTS, core))
        + dot_nt(second, pick_rows(q_cols, rows, SLOTS, 1 - core))
    ).astype(BF16)
    out_rows = 2 * SLOTS
    for part in range(width // LANES):
        turn_out[part] = (
            dot_tn(heads_low[...], proj_low[:, part * LANES : (part + 1) * LANES])
            .astype(BF16)
            .reshape(blocks, strips, out_rows, LANES)
        )
    for target, parity in ((keep, core), (send, 1 - core)):
        target[:, :, out_at : out_at + out_rows, :] = turn_out[2 * parity]
        target[:, :, out_at + out_rows : out_at + 2 * out_rows, :] = turn_out[2 * parity + 1]
        target[:, :, out_at + 2 * out_rows : out_at + 3 * out_rows, :] = turn_out[4]


def attention_back(
    query_low, kv_far, kv_near, kv_own, d_heads, log_total, q_seq, k_seq,
    d_query, d_own, d_near, d_far, sum_keys, sum_values,
):
    head = kv_own.shape[1] // 2
    rows = kv_own.shape[0]
    parts = (kv_far, kv_near, kv_own)
    keys = jnp.concatenate([part[:, :head] for part in parts], axis=0)
    values = jnp.concatenate([part[:, head:] for part in parts], axis=0)
    allowed = visible(q_seq, k_seq)
    for index in range(query_low.shape[1] // head):
        span = slice(index * head, (index + 1) * head)
        scores = dot_nt(query_low[:, span], keys) * query_scale
        scores = jnp.where(allowed, scores, MASKED)
        probs = jnp.exp(scores - log_total[:, index : index + 1])
        d_probs = dot_nt(d_heads[:, span], values)
        inner = jnp.sum(probs * d_probs, axis=-1, keepdims=True)
        d_scores = (probs * (d_probs - inner)).astype(BF16)
        d_query[:, span] = dot(d_scores, keys) * query_scale
        key_term = dot_tn(d_scores, query_low[:, span]) * query_scale
        value_term = dot_tn(probs.astype(BF16), d_heads[:, span])
        if index == 0:
            sum_keys[...] = key_term
            sum_values[...] = value_term
        else:
            sum_keys[...] += key_term
            sum_values[...] += value_term
    for target, start in ((d_far, 0), (d_near, rows), (d_own, 2 * rows)):
        target[:, :head] = sum_keys[start : start + rows, :].astype(target.dtype)
        target[:, head:] = sum_values[start : start + rows, :].astype(target.dtype)


def after_attention(
    core_ref, raw, d_query, d_own, near, far, attn_rel, own, peer, tok, gains, head_gains, cos, sin,
    d_state, gain_grads, tokens_grad, keep, send, low,
):
    core = core_ref[0]
    width, rows = tok.shape[1], own.shape[0]
    q_cols, kv_cols = d_query.shape[1], d_own.shape[1]
    head = kv_cols // 2
    per, per_head = width // LANES, head // LANES
    cosine, minus_sine = cos[...], -sin[...]
    query_gain_grad = jnp.zeros((1, head), F32)
    for index in range(q_cols // head):
        span = slice(index * head, (index + 1) * head)
        unit, scale = normed(raw[:, span])
        cot = turned(d_query[:, span], cosine, minus_sine)
        d_raw, part = normed_back(cot, unit, scale, head_gains[0:1, :])
        query_gain_grad += part
        low[:, span] = d_raw.astype(BF16)
    d_kv = d_own[...] + near[...].astype(F32) + far[...].astype(F32)
    unit, scale = normed(raw[:, q_cols : q_cols + head])
    cot = turned(d_kv[:, :head], cosine, minus_sine)
    d_raw, key_gain_grad = normed_back(cot, unit, scale, head_gains[1:2, :])
    low[:, q_cols : q_cols + head] = d_raw.astype(BF16)
    low[:, q_cols + head :] = d_kv[:, head:].astype(BF16)

    columns = q_cols + kv_cols
    d_low = jnp.zeros(tok.shape, F32)
    for weight, parity in ((own, core), (peer, 1 - core)):
        part = dot_nt(low[...], weight[:, :columns])
        high = part.astype(BF16)
        rest = (part - high.astype(F32)).astype(BF16)
        selector = pick_rows(width, rows, per, parity)
        d_low += dot_nt(high, selector) + dot_nt(rest, selector)
    unit, scale = normed(tok[...].astype(F32))
    d_norm, in_gain_grad = normed_back(d_low, unit, scale, gains[0:1, :])
    tokens_grad[...] = (d_state[...] + d_norm).astype(BF16)

    wide = jnp.zeros((LANES, width), F32)
    vectors = [in_gain_grad] + [gain_grads[i : i + 1, :] for i in range(1, 4)]
    for which, vector in enumerate(vectors):
        wide = jnp.where(gain_mask(which * per, per, LANES, width), vector, wide)
    narrow = jnp.zeros((LANES, head), F32)
    for which, vector in enumerate((query_gain_grad, key_gain_grad)):
        mask = gain_mask(4 * per + which * per_head, per_head, LANES, head)
        narrow = jnp.where(mask, vector, narrow)
    wide, narrow = wide.astype(BF16), narrow.astype(BF16)
    for target, start, parity in ((keep, 0, core), (send, rows, 1 - core)):
        extra = dot(wide, pick_slot(width, rows, per, parity)) + dot(
            narrow, pick_slot(head, rows, per_head, parity)
        )
        block = dot_tn(attn_rel[:, start : start + rows], low[:, :LANES])
        target[:, :LANES] = (block + jnp.transpose(extra)).astype(BF16)
        target[:, LANES:] = dot_tn(attn_rel[:, start : start + rows], low[:, LANES:]).astype(BF16)


def on_device(
    tokens,
    out_grad,
    seq_start,
    seq_len,
    w_query,
    w_key_value,
    w_output,
    w_gate_up,
    w_down,
    norm_attn_in,
    norm_attn_out,
    norm_mlp_in,
    norm_mlp_out,
    norm_query,
    norm_key,
):
    size = lax.axis_size("fsdp")
    chips = size // 2
    me = lax.axis_index("fsdp")
    core = me % 2
    core_arg = core.astype(jnp.int32).reshape(1)
    tok_rows, width = tokens.shape
    shard = w_query.shape[0]
    q_cols, kv_cols = w_query.shape[1], w_key_value.shape[1]
    qkv_cols = q_cols + kv_cols
    gu_cols, ff = w_gate_up.shape[1], w_down.shape[0] * size
    down_rows = w_down.shape[0]
    head = kv_cols // 2
    hshard = norm_query.shape[0]
    half_rows = chips * SLOTS

    gateup_flat = lax.all_gather(
        jnp.pad(w_gate_up, ((0, SLOTS - shard), (0, 0))), "fsdp", axis=0, tiled=True
    )

    gain_row = jnp.concatenate(
        [norm_attn_in, norm_attn_out, norm_mlp_in, norm_mlp_out, norm_query, norm_key]
    )
    gain_count = gain_row.shape[0]
    pack = jnp.concatenate(
        [
            jnp.concatenate([w_query, w_key_value], axis=1),
            jnp.pad(gain_row, (0, qkv_cols - gain_count))[None],
            jnp.zeros((SLOTS - shard - 1, qkv_cols), BF16),
        ],
        axis=0,
    )
    own_attn = spread(jnp.concatenate([pack, w_output], axis=1))
    own = own_attn.reshape(half_rows, qkv_cols + width)
    peer = swap_cores(own)

    key_reach = (WINDOW + tok_rows - 2) // tok_rows
    first_token = me * tok_rows
    q_index, q_seq, q_pos, q_live = token_layout(seq_start, seq_len, first_token, tok_rows)
    k_index, k_seq, k_pos, k_live = token_layout(
        seq_start, seq_len, first_token - key_reach * tok_rows, (key_reach + 1) * tok_rows
    )
    live = q_live.astype(F32)[:, None]
    q_seq, k_seq = q_seq[:, None], k_seq[None, :]
    inv_freq = theta_base ** (-2.0 * jnp.arange(head // 2, dtype=F32) / head)
    angles = q_pos.astype(F32)[:, None] * inv_freq[None, :]
    cos_vals, sin_vals = jnp.cos(angles), jnp.sin(angles)

    attn_rel, raw, query_low, own_kv, gains, head_gains = call(
        before_attention,
        (
            shape((tok_rows, 2 * half_rows), BF16),
            shape((tok_rows, qkv_cols), F32),
            shape((tok_rows, q_cols), BF16),
            shape((tok_rows, kv_cols), BF16),
            shape((8, width), F32),
            shape((8, head), F32),
        ),
        (core_arg, tokens, own, peer, cos_vals, sin_vals),
        specs=[SCALAR] + [WHOLE] * 5,
    )
    down_block, own_kv = lax.optimization_barrier((w_down, own_kv))
    own_down = spread(down_block)
    kv_near = shifted(own_kv, "fsdp", 1)
    kv_far = shifted(own_kv, "fsdp", 2)
    heads_low, log_total, proj, state = call(
        attention,
        (
            shape((tok_rows, q_cols), BF16),
            shape((tok_rows, LANES), F32),
            shape((tok_rows, width), F32),
            shape((tok_rows, width), F32),
        ),
        (core_arg, query_low, kv_far, kv_near, own_kv, q_seq, k_seq, own, peer, tokens, gains),
        specs=[SCALAR] + [WHOLE] * 10,
        flops=20e9,
    )

    own_down, state = lax.optimization_barrier((own_down, state))
    peer_down = swap_cores(own_down)

    tile = 512
    blocks, strips = 8, chips // 8
    chunk_rows = (width // blocks) * 2 + down_rows * (width // LANES) + 6 * SLOTS
    mixed, d_state, d_heads, gain_grads, keep, send = call(
        feed_forward,
        (
            shape((tok_rows, width), BF16),
            shape((tok_rows, width), F32),
            shape((tok_rows, q_cols), BF16),
            shape((8, width), F32),
            shape((blocks, strips, chunk_rows, LANES), BF16),
            shape((blocks, strips, chunk_rows, LANES), BF16),
        ),
        (
            core_arg, state, proj, out_grad, live, gains, heads_low, own, peer,
            gateup_flat, own_down, peer_down,
        ),
        scratch=(
            pltpu.VMEM((gu_cols // tile, size * SLOTS, tile), BF16),
            pltpu.VMEM((chips, 2, down_rows, width), BF16),
            pltpu.VMEM((tok_rows, ff), F32),
            pltpu.VMEM((tok_rows, ff), F32),
            pltpu.VMEM((tok_rows, ff), BF16),
            pltpu.VMEM((tok_rows, width), F32),
            pltpu.VMEM((tok_rows, size * SLOTS), F32),
            pltpu.VMEM((tok_rows, size * SLOTS), BF16),
            pltpu.VMEM((tok_rows, width), BF16),
            pltpu.VMEM((tok_rows, width), BF16),
            pltpu.VMEM((2, width, tile // 2), BF16),
            pltpu.VMEM((tile // (2 * down_rows) // strips, strips, 2, down_rows, width), BF16),
            pltpu.VMEM((width // LANES, blocks, strips, 2 * SLOTS, LANES), BF16),
            pltpu.SemaphoreType.DMA((gu_cols // tile,)),
            pltpu.SemaphoreType.DMA((2,)),
        ),
        specs=[SCALAR] + [WHOLE] * 8 + [AWAY] * 3,
        flops=12e9,
    )
    both = keep.astype(F32) + swap_cores(send).astype(F32)
    mlp_parts = exchange(both.astype(BF16).reshape(chips, chunk_rows, LANES))

    d_query, d_own, d_near, d_far = call(
        attention_back,
        (
            shape((tok_rows, q_cols), F32),
            shape((tok_rows, kv_cols), F32),
            shape((tok_rows, kv_cols), BF16),
            shape((tok_rows, kv_cols), BF16),
        ),
        (query_low, kv_far, kv_near, own_kv, d_heads, log_total, q_seq, k_seq),
        scratch=(
            pltpu.VMEM(((key_reach + 1) * tok_rows, head), F32),
            pltpu.VMEM(((key_reach + 1) * tok_rows, head), F32),
        ),
        specs=[WHOLE] * 8,
        flops=20e9,
    )
    near = shifted(d_near, "fsdp", -1)
    far = shifted(d_far, "fsdp", -2)
    tokens_grad, keep, send = call(
        after_attention,
        (
            shape((tok_rows, width), BF16),
            shape((half_rows, qkv_cols), BF16),
            shape((half_rows, qkv_cols), BF16),
        ),
        (
            core_arg, raw, d_query, d_own, near, far, attn_rel, own, peer, tokens, gains,
            head_gains, cos_vals, sin_vals, d_state, gain_grads,
        ),
        scratch=(pltpu.VMEM((tok_rows, qkv_cols), BF16),),
        specs=[SCALAR] + [WHOLE] * 15,
        flops=20e9,
    )
    both = (keep.astype(F32) + swap_cores(send).astype(F32)).astype(BF16)
    both, mlp_parts = lax.optimization_barrier((both, mlp_parts))
    share_attn = jnp.sum(
        exchange(both.reshape(chips, SLOTS, qkv_cols)).astype(F32), axis=0
    )
    share_gains = share_attn[GAIN_SLOT, :gain_count]

    share_mlp = jnp.sum(mlp_parts.astype(F32), axis=0)
    block_rows = width // blocks
    group = size // blocks
    strip = jnp.concatenate([share_mlp[:block_rows], share_mlp[block_rows : 2 * block_rows]], axis=1)
    strip = lax.all_to_all(
        strip.reshape(group, shard, gu_cols // group),
        "fsdp",
        split_axis=0,
        concat_axis=0,
        tiled=True,
        axis_index_groups=[[b * group + i for i in range(group)] for b in range(blocks)],
    )
    share_gate_up = strip.transpose(1, 0, 2).reshape(shard, gu_cols)
    down_at = 2 * block_rows
    out_at = down_at + down_rows * (width // LANES)
    share_down = (
        share_mlp[down_at:out_at]
        .reshape(width // LANES, down_rows, LANES)
        .transpose(1, 0, 2)
        .reshape(down_rows, width)
    )
    out_tiles = share_mlp[out_at:].reshape(3, 2, SLOTS, LANES)
    mine = jnp.where(core == 0, out_tiles[:, 0], out_tiles[:, 1])
    theirs = swap_cores(jnp.where(core == 0, out_tiles[:, 1], out_tiles[:, 0]))
    first = jnp.where(core == 0, mine[:2], theirs[:2])
    second = jnp.where(core == 0, theirs[:2], mine[:2])
    share_output = (
        jnp.concatenate([first, second, mine[2:]], axis=0)
        .transpose(1, 0, 2)
        .reshape(SLOTS, width)
    )
    return (
        mixed,
        tokens_grad,
        share_attn[:shard, :q_cols],
        share_attn[:shard, q_cols:],
        share_output,
        share_gate_up,
        share_down,
        share_gains[:shard],
        share_gains[shard : 2 * shard],
        share_gains[2 * shard : 3 * shard],
        share_gains[3 * shard : 4 * shard],
        share_gains[4 * shard : 4 * shard + hshard],
        share_gains[4 * shard + hshard :],
    )


def solution(mesh):
    placed = (
        P("fsdp", None),
        P("fsdp", None),
        P(),
        P(),
        P("fsdp", None),
        P("fsdp", None),
        P("fsdp", None),
        P("fsdp", None),
        P("fsdp", None),
        P("fsdp"),
        P("fsdp"),
        P("fsdp"),
        P("fsdp"),
        P("fsdp"),
        P("fsdp"),
    )
    return jax.shard_map(
        on_device,
        mesh=mesh,
        in_specs=placed,
        out_specs=(
            P("fsdp", None),
            P("fsdp", None),
            P("fsdp", None),
            P("fsdp", None),
            P("fsdp", None),
            P("fsdp", None),
            P("fsdp", None),
            P("fsdp"),
            P("fsdp"),
            P("fsdp"),
            P("fsdp"),
            P("fsdp"),
            P("fsdp"),
        ),
        check_vma=False,
    )
```

```python
import jax
import jax.numpy as jnp
from jax import lax
from jax.experimental import pallas as pl
from jax.experimental.pallas import tpu as pltpu
from jax.sharding import PartitionSpec as P

WINDOW = 512


epsilon = 1e-06
theta_base = 10000.0
query_scale = 0.0625


def shifted(block, axis, distance):
    devices = range(lax.axis_size(axis))
    route = [(i - distance, i) for i in devices if i - distance in devices]
    return lax.ppermute(block, axis, route)


def token_layout(seq_start, seq_len, first_token, token_count):
    indices = first_token + jnp.arange(token_count, dtype=jnp.int32)
    offsets = indices[:, None] - seq_start[None, :]
    inside = (offsets >= 0) & (offsets < seq_len[None, :])
    live_mask = jnp.any(inside, axis=1)
    seq_numbers = jnp.arange(seq_start.shape[0], dtype=jnp.int32)
    seq_id = jnp.sum(jnp.where(inside, seq_numbers[None, :], 0), axis=1)
    seq_id = jnp.where(live_mask, seq_id, -1)
    positions = jnp.sum(jnp.where(inside, offsets, 0), axis=1)
    return (indices, seq_id, positions, live_mask)


BF16 = jnp.bfloat16
F32 = jnp.float32
SLOTS = 8
GAIN_SLOT = 5
MASKED = -1e30
VMEM_BYTES = 56 * 1024 * 1024
LANES = 128


def same_core_groups(size):
    return [[2 * chip + core for chip in range(size // 2)] for core in range(2)]


def swap_cores(block):
    size = lax.axis_size("fsdp")
    return lax.ppermute(block, "fsdp", [(i, i ^ 1) for i in range(size)])


def exchange(blocks):
    return lax.all_to_all(
        blocks,
        "fsdp",
        split_axis=0,
        concat_axis=0,
        tiled=True,
        axis_index_groups=same_core_groups(lax.axis_size("fsdp")),
    )


def spread(block):
    chips = lax.axis_size("fsdp") // 2
    return exchange(jnp.broadcast_to(block[None], (chips,) + block.shape))


def call(kernel, outs, ins, scratch=(), specs=None, flops=4e9):
    return pl.pallas_call(
        kernel,
        out_shape=outs,
        in_specs=specs,
        scratch_shapes=list(scratch),
        compiler_params=pltpu.CompilerParams(vmem_limit_bytes=VMEM_BYTES),
        cost_estimate=pl.CostEstimate(
            flops=int(flops), bytes_accessed=8_000_000, transcendentals=0
        ),
    )(*ins)


SCALAR = pl.BlockSpec(memory_space=pltpu.SMEM)
WHOLE = pl.BlockSpec(memory_space=pltpu.VMEM)
AWAY = pl.BlockSpec(memory_space=pl.ANY)


def shape(dims, kind):
    return jax.ShapeDtypeStruct(dims, kind)


def dot(left, right):
    return jnp.dot(left, right, preferred_element_type=F32)


def dot_nt(left, right):
    return lax.dot_general(left, right, (((1,), (1,)), ((), ())), preferred_element_type=F32)


def dot_tn(left, right):
    return lax.dot_general(left, right, (((0,), (0,)), ((), ())), preferred_element_type=F32)


def normed(values):
    scale = lax.rsqrt(jnp.mean(values * values, axis=-1, keepdims=True) + epsilon)
    return values * scale, scale


def normed_back(cot, unit, scale, gain):
    weighted = cot * gain
    inner = jnp.mean(weighted * unit, axis=-1, keepdims=True)
    return scale * (weighted - unit * inner), jnp.sum(cot * unit, axis=0, keepdims=True)


def ones_where(mask):
    return jnp.where(mask, 1.0, 0.0).astype(BF16)


def places(count):
    place = lax.broadcasted_iota(jnp.int32, (1, count), 1)
    return lax.shift_right_logical(place, 3), place & (SLOTS - 1)


def pick_rows(rows, count, per, core):
    block, slot = places(count)
    device = block if core is None else 2 * block + core
    source = jnp.where(slot < per, device * per + slot, -1)
    return ones_where(lax.broadcasted_iota(jnp.int32, (rows, count), 0) == source)


def pick_slot(rows, count, per, core):
    block, slot = places(count)
    low = jnp.where(slot == GAIN_SLOT, (2 * block + core) * per, -2 * rows)
    natural = lax.broadcasted_iota(jnp.int32, (rows, count), 0)
    return ones_where((natural >= low) & (natural < low + per))


def gain_mask(first, per, rows, columns):
    row = lax.broadcasted_iota(jnp.int32, (rows, columns), 0)
    column = lax.broadcasted_iota(jnp.int32, (rows, columns), 1)
    return row == first + lax.rem(column, per)


def turned(values, cos, sin):
    half = values.shape[-1] // 2
    first, second = values[:, :half], values[:, half:]
    return jnp.concatenate([first * cos - second * sin, second * cos + first * sin], axis=1)


def before_attention(
    core_ref, tok, own, peer, cos, sin, attn_rel, raw, query_low, own_kv, gains, head_gains
):
    core = core_ref[0]
    width, rows = tok.shape[1], own.shape[0]
    kv_cols = own_kv.shape[1]
    head = kv_cols // 2
    q_cols = query_low.shape[1]
    per, per_head = width // LANES, head // LANES

    def gather(natural, count):
        mine = dot(pick_slot(natural, rows, count, core), own[:, :LANES])
        theirs = dot(pick_slot(natural, rows, count, 1 - core), peer[:, :LANES])
        return jnp.transpose(mine + theirs)[:32]

    wide = gather(width, per)
    for which in range(4):
        mask = gain_mask(which * per, per, 32, width)
        gains[which : which + 1, :] = jnp.sum(jnp.where(mask, wide, 0.0), 0, keepdims=True)
    narrow = gather(head, per_head)
    for which in range(2):
        mask = gain_mask(4 * per + which * per_head, per_head, 32, head)
        head_gains[which : which + 1, :] = jnp.sum(jnp.where(mask, narrow, 0.0), 0, keepdims=True)
    unit, _ = normed(tok[...].astype(F32))
    low = (unit * gains[0:1, :]).astype(BF16)
    attn_rel[:, :rows] = dot(low, pick_rows(width, rows, per, core)).astype(BF16)
    attn_rel[:, rows:] = dot(low, pick_rows(width, rows, per, 1 - core)).astype(BF16)
    columns = q_cols + kv_cols
    raw[...] = dot(attn_rel[:, :rows], own[:, :columns]) + dot(attn_rel[:, rows:], peer[:, :columns])
    for index in range(q_cols // head):
        span = slice(index * head, (index + 1) * head)
        unit, _ = normed(raw[:, span])
        query_low[:, span] = turned(unit * head_gains[0:1, :], cos[...], sin[...]).astype(BF16)
    unit, _ = normed(raw[:, q_cols : q_cols + head])
    own_kv[:, :head] = turned(unit * head_gains[1:2, :], cos[...], sin[...]).astype(BF16)
    own_kv[:, head:] = raw[:, q_cols + head :].astype(BF16)


def visible(q_seq, k_seq):
    queries, keys = q_seq.shape[0], k_seq.shape[1]
    row = lax.broadcasted_iota(jnp.int32, (queries, keys), 0)
    column = lax.broadcasted_iota(jnp.int32, (queries, keys), 1)
    distance = row - column + (keys - queries)
    same = (q_seq[...] == k_seq[...]) & (q_seq[...] >= 0)
    return (same & (distance >= 0) & (distance < WINDOW)) | (distance == 0)


def attention(
    core_ref, query_low, kv_far, kv_near, kv_own, q_seq, k_seq, own, peer, tok, gains,
    heads_low, log_total, proj, state,
):
    core = core_ref[0]
    head = kv_own.shape[1] // 2
    width, rows = tok.shape[1], own.shape[0]
    q_cols = query_low.shape[1]
    parts = (kv_far, kv_near, kv_own)
    keys = jnp.concatenate([part[:, :head] for part in parts], axis=0)
    values = jnp.concatenate([part[:, head:] for part in parts], axis=0)
    allowed = visible(q_seq, k_seq)
    for index in range(q_cols // head):
        span = slice(index * head, (index + 1) * head)
        scores = dot_nt(query_low[:, span], keys) * query_scale
        scores = jnp.where(allowed, scores, MASKED)
        top = jnp.max(scores, axis=-1, keepdims=True)
        terms = jnp.exp(scores - top)
        total = jnp.sum(terms, axis=-1, keepdims=True)
        probs = (terms * (1.0 / total)).astype(BF16)
        heads_low[:, span] = dot(probs, values).astype(BF16)
        log_total[:, index : index + 1] = top + jnp.log(total)
    offset = own.shape[1] - width
    heads = heads_low[...]
    first = dot(heads, pick_rows(q_cols, rows, SLOTS, core)).astype(BF16)
    second = dot(heads, pick_rows(q_cols, rows, SLOTS, 1 - core)).astype(BF16)
    proj[...] = dot(first, own[:, offset:]) + dot(second, peer[:, offset:])
    unit, _ = normed(proj[...])
    state[...] = tok[...].astype(F32) + unit * gains[1:2, :]


def feed_forward(
    core_ref, state, proj, out_grad, live, gains, heads_low, own, peer, gate_up, down_full,
    mixed, d_state, d_heads, gain_grads, keep, send,
    weights, down, act, act_slope, hidden, total, back, low_flat, low, low_branch, turn, turn_down,
    turn_out, weight_sem, down_sem,
):
    core = core_ref[0]
    tiles, tile = weights.shape[0], weights.shape[2]
    half = tiles // 2
    width = state.shape[1]
    rows = own.shape[0]
    q_cols = heads_low.shape[1]
    per = width // LANES
    down_rows = down_full.shape[2]
    blocks, strips = keep.shape[0], keep.shape[1]
    block_rows = width // blocks
    tile_chips = tile // (2 * down_rows)

    def weight_copy(index):
        return pltpu.make_async_copy(
            gate_up.at[:, pl.ds(pl.multiple_of(index * tile, tile), tile)],
            weights.at[index],
            weight_sem.at[index],
        )

    down_copy = pltpu.make_async_copy(down_full, down, down_sem)
    for index in range(half):
        weight_copy(index).start()
        weight_copy(half + index).start()
        if index == 0:
            down_copy.start()

    spread_flat = pick_rows(width, weights.shape[1], per, None)
    unit, scale = normed(state[...])
    low[...] = (unit * gains[2:3, :]).astype(BF16)
    low_flat[...] = dot(low[...], spread_flat).astype(BF16)
    total[...] = jnp.zeros_like(total)
    down_copy.wait()

    def down_tile(index):
        chunk = down[pl.ds(index * tile_chips, tile_chips)]
        return chunk.reshape(tile, width)

    def forward(index, carry):
        columns = pl.ds(pl.multiple_of(index * tile, tile), tile)
        weight_copy(index).wait()
        weight_copy(half + index).wait()
        gate = dot(low_flat[...], weights[index])
        up = dot(low_flat[...], weights[half + index])
        square = gate * gate
        bend = jnp.tanh(gate * (0.7978845608028654 * (1.0 + 0.044715 * square)))
        rise = 0.5 * (1.0 + bend)
        gelu = gate * rise
        slope = rise + 0.5 * gate * (1.0 - bend * bend) * (
            0.7978845608028654 * (1.0 + 0.134145 * square)
        )
        act[:, columns] = gelu
        act_slope[:, columns] = up * slope
        hidden[:, columns] = (gelu * up).astype(BF16)
        total[...] += dot(hidden[:, columns], down_tile(index))
        return carry

    lax.fori_loop(0, half, forward, 0)

    branch_unit, branch_scale = normed(total[...])
    mixed[...] = ((state[...] + branch_unit * gains[3:4, :]) * live[...]).astype(BF16)
    cotangent = out_grad[...].astype(F32) * live[...]
    d_branch, gain_grads[3:4, :] = normed_back(
        cotangent, branch_unit, branch_scale, gains[3:4, :]
    )
    low_branch[...] = d_branch.astype(BF16)
    back[...] = jnp.zeros_like(back)

    def place(strip, grads):
        turn[0] = grads[:, : tile // 2].astype(BF16)
        turn[1] = grads[:, tile // 2 :].astype(BF16)
        for target, parity in ((keep, core), (send, 1 - core)):
            for part in range(tile // 2 // LANES):
                target[:, strip, part * block_rows : (part + 1) * block_rows, :] = turn[
                    parity, :, part * LANES : (part + 1) * LANES
                ].reshape(blocks, block_rows, LANES)

    down_at = block_rows * (tile // 2 // LANES)
    out_at = down_at + down_rows * (width // LANES)

    def backward(index, carry):
        columns = pl.ds(pl.multiple_of(index * tile, tile), tile)
        d_hidden = dot_nt(low_branch[...], down_tile(index))
        d_gate = (d_hidden * act_slope[:, columns]).astype(BF16)
        d_up = (d_hidden * act[:, columns]).astype(BF16)
        back[...] += dot_nt(d_gate, weights[index]) + dot_nt(d_up, weights[half + index])
        place(index, dot_tn(low[...], d_gate))
        place(half + index, dot_tn(low[...], d_up))
        turn_down[...] = (
            dot_tn(hidden[:, columns], low_branch[...])
            .astype(BF16)
            .reshape(tile_chips // strips, strips, 2, down_rows, width)
        )
        tall = pl.ds(index * (tile_chips // strips), tile_chips // strips)
        for target, parity in ((keep, core), (send, 1 - core)):
            for part in range(width // LANES):
                top = down_at + part * down_rows
                target[tall, :, top : top + down_rows, :] = turn_down[
                    :, :, parity, :, part * LANES : (part + 1) * LANES
                ]
        return carry

    lax.fori_loop(0, half, backward, 0)

    high = back[...].astype(BF16)
    rest = (back[...] - high.astype(F32)).astype(BF16)
    d_low = dot_nt(high, spread_flat) + dot_nt(rest, spread_flat)
    d_norm, gain_grads[2:3, :] = normed_back(d_low, unit, scale, gains[2:3, :])
    d_state[...] = cotangent + d_norm
    proj_unit, proj_scale = normed(proj[...])
    d_proj, gain_grads[1:2, :] = normed_back(d_state[...], proj_unit, proj_scale, gains[1:2, :])
    proj_low = d_proj.astype(BF16)
    offset = own.shape[1] - width
    first = dot_nt(proj_low, own[:, offset:]).astype(BF16)
    second = dot_nt(proj_low, peer[:, offset:]).astype(BF16)
    d_heads[...] = (
        dot_nt(first, pick_rows(q_cols, rows, SLOTS, core))
        + dot_nt(second, pick_rows(q_cols, rows, SLOTS, 1 - core))
    ).astype(BF16)
    out_rows = 2 * SLOTS
    for part in range(width // LANES):
        turn_out[part] = (
            dot_tn(heads_low[...], proj_low[:, part * LANES : (part + 1) * LANES])
            .astype(BF16)
            .reshape(blocks, strips, out_rows, LANES)
        )
    for target, parity in ((keep, core), (send, 1 - core)):
        target[:, :, out_at : out_at + out_rows, :] = turn_out[2 * parity]
        target[:, :, out_at + out_rows : out_at + 2 * out_rows, :] = turn_out[2 * parity + 1]
        target[:, :, out_at + 2 * out_rows : out_at + 3 * out_rows, :] = turn_out[4]


def attention_back(
    query_low, kv_far, kv_near, kv_own, d_heads, log_total, q_seq, k_seq,
    d_query, d_own, d_near, d_far, sum_keys, sum_values,
):
    head = kv_own.shape[1] // 2
    rows = kv_own.shape[0]
    parts = (kv_far, kv_near, kv_own)
    keys = jnp.concatenate([part[:, :head] for part in parts], axis=0)
    values = jnp.concatenate([part[:, head:] for part in parts], axis=0)
    allowed = visible(q_seq, k_seq)
    for index in range(query_low.shape[1] // head):
        span = slice(index * head, (index + 1) * head)
        scores = dot_nt(query_low[:, span], keys) * query_scale
        scores = jnp.where(allowed, scores, MASKED)
        probs = jnp.exp(scores - log_total[:, index : index + 1])
        d_probs = dot_nt(d_heads[:, span], values)
        inner = jnp.sum(probs * d_probs, axis=-1, keepdims=True)
        d_scores = (probs * (d_probs - inner)).astype(BF16)
        d_query[:, span] = dot(d_scores, keys) * query_scale
        key_term = dot_tn(d_scores, query_low[:, span]) * query_scale
        value_term = dot_tn(probs.astype(BF16), d_heads[:, span])
        if index == 0:
            sum_keys[...] = key_term
            sum_values[...] = value_term
        else:
            sum_keys[...] += key_term
            sum_values[...] += value_term
    for target, start in ((d_far, 0), (d_near, rows), (d_own, 2 * rows)):
        target[:, :head] = sum_keys[start : start + rows, :].astype(target.dtype)
        target[:, head:] = sum_values[start : start + rows, :].astype(target.dtype)


def after_attention(
    core_ref, raw, d_query, d_own, near, far, attn_rel, own, peer, tok, gains, head_gains, cos, sin,
    d_state, gain_grads, tokens_grad, keep, send, low,
):
    core = core_ref[0]
    width, rows = tok.shape[1], own.shape[0]
    q_cols, kv_cols = d_query.shape[1], d_own.shape[1]
    head = kv_cols // 2
    per, per_head = width // LANES, head // LANES
    cosine, minus_sine = cos[...], -sin[...]
    query_gain_grad = jnp.zeros((1, head), F32)
    for index in range(q_cols // head):
        span = slice(index * head, (index + 1) * head)
        unit, scale = normed(raw[:, span])
        cot = turned(d_query[:, span], cosine, minus_sine)
        d_raw, part = normed_back(cot, unit, scale, head_gains[0:1, :])
        query_gain_grad += part
        low[:, span] = d_raw.astype(BF16)
    d_kv = d_own[...] + near[...].astype(F32) + far[...].astype(F32)
    unit, scale = normed(raw[:, q_cols : q_cols + head])
    cot = turned(d_kv[:, :head], cosine, minus_sine)
    d_raw, key_gain_grad = normed_back(cot, unit, scale, head_gains[1:2, :])
    low[:, q_cols : q_cols + head] = d_raw.astype(BF16)
    low[:, q_cols + head :] = d_kv[:, head:].astype(BF16)

    columns = q_cols + kv_cols
    d_low = jnp.zeros(tok.shape, F32)
    for weight, parity in ((own, core), (peer, 1 - core)):
        part = dot_nt(low[...], weight[:, :columns])
        high = part.astype(BF16)
        rest = (part - high.astype(F32)).astype(BF16)
        selector = pick_rows(width, rows, per, parity)
        d_low += dot_nt(high, selector) + dot_nt(rest, selector)
    unit, scale = normed(tok[...].astype(F32))
    d_norm, in_gain_grad = normed_back(d_low, unit, scale, gains[0:1, :])
    tokens_grad[...] = (d_state[...] + d_norm).astype(BF16)

    wide = jnp.zeros((LANES, width), F32)
    vectors = [in_gain_grad] + [gain_grads[i : i + 1, :] for i in range(1, 4)]
    for which, vector in enumerate(vectors):
        wide = jnp.where(gain_mask(which * per, per, LANES, width), vector, wide)
    narrow = jnp.zeros((LANES, head), F32)
    for which, vector in enumerate((query_gain_grad, key_gain_grad)):
        mask = gain_mask(4 * per + which * per_head, per_head, LANES, head)
        narrow = jnp.where(mask, vector, narrow)
    wide, narrow = wide.astype(BF16), narrow.astype(BF16)
    for target, start, parity in ((keep, 0, core), (send, rows, 1 - core)):
        extra = dot(wide, pick_slot(width, rows, per, parity)) + dot(
            narrow, pick_slot(head, rows, per_head, parity)
        )
        block = dot_tn(attn_rel[:, start : start + rows], low[:, :LANES])
        target[:, :LANES] = (block + jnp.transpose(extra)).astype(BF16)
        target[:, LANES:] = dot_tn(attn_rel[:, start : start + rows], low[:, LANES:]).astype(BF16)


def on_device(
    tokens,
    out_grad,
    seq_start,
    seq_len,
    w_query,
    w_key_value,
    w_output,
    w_gate_up,
    w_down,
    norm_attn_in,
    norm_attn_out,
    norm_mlp_in,
    norm_mlp_out,
    norm_query,
    norm_key,
):
    size = lax.axis_size("fsdp")
    chips = size // 2
    me = lax.axis_index("fsdp")
    core = me % 2
    core_arg = core.astype(jnp.int32).reshape(1)
    tok_rows, width = tokens.shape
    shard = w_query.shape[0]
    q_cols, kv_cols = w_query.shape[1], w_key_value.shape[1]
    qkv_cols = q_cols + kv_cols
    gu_cols, ff = w_gate_up.shape[1], w_down.shape[0] * size
    down_rows = w_down.shape[0]
    head = kv_cols // 2
    hshard = norm_query.shape[0]
    half_rows = chips * SLOTS

    mlp_full = lax.all_gather(
        jnp.concatenate(
            [
                jnp.pad(w_gate_up, ((0, SLOTS - shard), (0, 0))),
                w_down[:SLOTS],
                w_down[SLOTS:],
            ],
            axis=1,
        ),
        "fsdp",
        axis=0,
        tiled=True,
    )
    down_full = jnp.concatenate(
        [
            mlp_full[:, gu_cols : gu_cols + width].reshape(chips, 2, SLOTS, width),
            mlp_full[:, gu_cols + width :].reshape(chips, 2, SLOTS, width),
        ],
        axis=2,
    )

    pack = jnp.zeros((SLOTS, qkv_cols + width), BF16)
    gain_count = 0
    for row, column, part in (
        (0, 0, w_query),
        (0, q_cols, w_key_value),
        (0, qkv_cols, w_output),
        (GAIN_SLOT, None, norm_attn_in[None]),
        (GAIN_SLOT, None, norm_attn_out[None]),
        (GAIN_SLOT, None, norm_mlp_in[None]),
        (GAIN_SLOT, None, norm_mlp_out[None]),
        (GAIN_SLOT, None, norm_query[None]),
        (GAIN_SLOT, None, norm_key[None]),
    ):
        high, wide = part.shape
        if column is None:
            column = gain_count
            gain_count += wide
        pack = pack + jnp.pad(
            part, ((row, SLOTS - row - high), (column, qkv_cols + width - column - wide))
        )
    own_attn = spread(pack)
    own = own_attn.reshape(half_rows, qkv_cols + width)
    peer = swap_cores(own)

    key_reach = (WINDOW + tok_rows - 2) // tok_rows
    first_token = me * tok_rows
    q_index, q_seq, q_pos, q_live = token_layout(seq_start, seq_len, first_token, tok_rows)
    k_index, k_seq, k_pos, k_live = token_layout(
        seq_start, seq_len, first_token - key_reach * tok_rows, (key_reach + 1) * tok_rows
    )
    live = q_live.astype(F32)[:, None]
    q_seq, k_seq = q_seq[:, None], k_seq[None, :]
    inv_freq = theta_base ** (-2.0 * jnp.arange(head // 2, dtype=F32) / head)
    angles = q_pos.astype(F32)[:, None] * inv_freq[None, :]
    cos_vals, sin_vals = jnp.cos(angles), jnp.sin(angles)

    attn_rel, raw, query_low, own_kv, gains, head_gains = call(
        before_attention,
        (
            shape((tok_rows, 2 * half_rows), BF16),
            shape((tok_rows, qkv_cols), F32),
            shape((tok_rows, q_cols), BF16),
            shape((tok_rows, kv_cols), BF16),
            shape((8, width), F32),
            shape((8, head), F32),
        ),
        (core_arg, tokens, own, peer, cos_vals, sin_vals),
        specs=[SCALAR] + [WHOLE] * 5,
    )
    kv_near = shifted(own_kv, "fsdp", 1)
    kv_far = shifted(own_kv, "fsdp", 2)
    heads_low, log_total, proj, state = call(
        attention,
        (
            shape((tok_rows, q_cols), BF16),
            shape((tok_rows, LANES), F32),
            shape((tok_rows, width), F32),
            shape((tok_rows, width), F32),
        ),
        (core_arg, query_low, kv_far, kv_near, own_kv, q_seq, k_seq, own, peer, tokens, gains),
        specs=[SCALAR] + [WHOLE] * 10,
        flops=20e9,
    )

    tile = 512
    blocks, strips = 8, chips // 8
    chunk_rows = (width // blocks) * 2 + down_rows * (width // LANES) + 6 * SLOTS
    mixed, d_state, d_heads, gain_grads, keep, send = call(
        feed_forward,
        (
            shape((tok_rows, width), BF16),
            shape((tok_rows, width), F32),
            shape((tok_rows, q_cols), BF16),
            shape((8, width), F32),
            shape((blocks, strips, chunk_rows, LANES), BF16),
            shape((blocks, strips, chunk_rows, LANES), BF16),
        ),
        (
            core_arg, state, proj, out_grad, live, gains, heads_low, own, peer,
            mlp_full, down_full,
        ),
        scratch=(
            pltpu.VMEM((gu_cols // tile, size * SLOTS, tile), BF16),
            pltpu.VMEM((chips, 2, down_rows, width), BF16),
            pltpu.VMEM((tok_rows, ff), F32),
            pltpu.VMEM((tok_rows, ff), F32),
            pltpu.VMEM((tok_rows, ff), BF16),
            pltpu.VMEM((tok_rows, width), F32),
            pltpu.VMEM((tok_rows, size * SLOTS), F32),
            pltpu.VMEM((tok_rows, size * SLOTS), BF16),
            pltpu.VMEM((tok_rows, width), BF16),
            pltpu.VMEM((tok_rows, width), BF16),
            pltpu.VMEM((2, width, tile // 2), BF16),
            pltpu.VMEM((tile // (2 * down_rows) // strips, strips, 2, down_rows, width), BF16),
            pltpu.VMEM((width // LANES, blocks, strips, 2 * SLOTS, LANES), BF16),
            pltpu.SemaphoreType.DMA((gu_cols // tile,)),
            pltpu.SemaphoreType.DMA,
        ),
        specs=[SCALAR] + [WHOLE] * 8 + [AWAY] * 2,
        flops=12e9,
    )
    both_mlp = (keep.astype(F32) + swap_cores(send).astype(F32)).astype(BF16)

    d_query, d_own, d_near, d_far = call(
        attention_back,
        (
            shape((tok_rows, q_cols), F32),
            shape((tok_rows, kv_cols), F32),
            shape((tok_rows, kv_cols), BF16),
            shape((tok_rows, kv_cols), BF16),
        ),
        (query_low, kv_far, kv_near, own_kv, d_heads, log_total, q_seq, k_seq),
        scratch=(
            pltpu.VMEM(((key_reach + 1) * tok_rows, head), F32),
            pltpu.VMEM(((key_reach + 1) * tok_rows, head), F32),
        ),
        specs=[WHOLE] * 8,
        flops=20e9,
    )
    near = shifted(d_near, "fsdp", -1)
    far = shifted(d_far, "fsdp", -2)
    both_mlp, near, far = lax.optimization_barrier((both_mlp, near, far))
    mlp_parts = exchange(both_mlp.reshape(chips, chunk_rows, LANES))
    tokens_grad, keep, send = call(
        after_attention,
        (
            shape((tok_rows, width), BF16),
            shape((half_rows, qkv_cols), BF16),
            shape((half_rows, qkv_cols), BF16),
        ),
        (
            core_arg, raw, d_query, d_own, near, far, attn_rel, own, peer, tokens, gains,
            head_gains, cos_vals, sin_vals, d_state, gain_grads,
        ),
        scratch=(pltpu.VMEM((tok_rows, qkv_cols), BF16),),
        specs=[SCALAR] + [WHOLE] * 15,
        flops=20e9,
    )
    both = (keep.astype(F32) + swap_cores(send).astype(F32)).astype(BF16)
    both, mlp_parts = lax.optimization_barrier((both, mlp_parts))
    share_attn = jnp.sum(
        exchange(both.reshape(chips, SLOTS, qkv_cols)).astype(F32), axis=0
    )
    share_gains = share_attn[GAIN_SLOT, :gain_count]

    share_mlp = jnp.sum(mlp_parts.astype(F32), axis=0)
    block_rows = width // blocks
    group = size // blocks
    strip = jnp.concatenate([share_mlp[:block_rows], share_mlp[block_rows : 2 * block_rows]], axis=1)
    strip = lax.all_to_all(
        strip.reshape(group, shard, gu_cols // group),
        "fsdp",
        split_axis=0,
        concat_axis=0,
        tiled=True,
        axis_index_groups=[[b * group + i for i in range(group)] for b in range(blocks)],
    )
    share_gate_up = strip.transpose(1, 0, 2).reshape(shard, gu_cols)
    down_at = 2 * block_rows
    out_at = down_at + down_rows * (width // LANES)
    share_down = (
        share_mlp[down_at:out_at]
        .reshape(width // LANES, down_rows, LANES)
        .transpose(1, 0, 2)
        .reshape(down_rows, width)
    )
    out_tiles = share_mlp[out_at:].reshape(3, 2, SLOTS, LANES)
    mine = jnp.where(core == 0, out_tiles[:, 0], out_tiles[:, 1])
    theirs = swap_cores(jnp.where(core == 0, out_tiles[:, 1], out_tiles[:, 0]))
    first = jnp.where(core == 0, mine[:2], theirs[:2])
    second = jnp.where(core == 0, theirs[:2], mine[:2])
    share_output = (
        jnp.concatenate([first, second, mine[2:]], axis=0)
        .transpose(1, 0, 2)
        .reshape(SLOTS, width)
    )
    return (
        mixed,
        tokens_grad,
        share_attn[:shard, :q_cols],
        share_attn[:shard, q_cols:],
        share_output,
        share_gate_up,
        share_down,
        share_gains[:shard],
        share_gains[shard : 2 * shard],
        share_gains[2 * shard : 3 * shard],
        share_gains[3 * shard : 4 * shard],
        share_gains[4 * shard : 4 * shard + hshard],
        share_gains[4 * shard + hshard :],
    )


def solution(mesh):
    placed = (
        P("fsdp", None),
        P("fsdp", None),
        P(),
        P(),
        P("fsdp", None),
        P("fsdp", None),
        P("fsdp", None),
        P("fsdp", None),
        P("fsdp", None),
        P("fsdp"),
        P("fsdp"),
        P("fsdp"),
        P("fsdp"),
        P("fsdp"),
        P("fsdp"),
    )
    return jax.shard_map(
        on_device,
        mesh=mesh,
        in_specs=placed,
        out_specs=(
            P("fsdp", None),
            P("fsdp", None),
            P("fsdp", None),
            P("fsdp", None),
            P("fsdp", None),
            P("fsdp", None),
            P("fsdp", None),
            P("fsdp"),
            P("fsdp"),
            P("fsdp"),
            P("fsdp"),
            P("fsdp"),
            P("fsdp"),
        ),
        check_vma=False,
    )
```

```python
import jax
import jax.numpy as jnp
from jax import lax
from jax.experimental import pallas as pl
from jax.experimental.pallas import tpu as pltpu
from jax.sharding import PartitionSpec as P

WINDOW = 512


epsilon = 1e-06
theta_base = 10000.0
query_scale = 0.0625


def shifted(block, axis, distance):
    devices = range(lax.axis_size(axis))
    route = [(i - distance, i) for i in devices if i - distance in devices]
    return lax.ppermute(block, axis, route)


def token_layout(seq_start, seq_len, first_token, token_count):
    indices = first_token + jnp.arange(token_count, dtype=jnp.int32)
    offsets = indices[:, None] - seq_start[None, :]
    inside = (offsets >= 0) & (offsets < seq_len[None, :])
    live_mask = jnp.any(inside, axis=1)
    seq_numbers = jnp.arange(seq_start.shape[0], dtype=jnp.int32)
    seq_id = jnp.sum(jnp.where(inside, seq_numbers[None, :], 0), axis=1)
    seq_id = jnp.where(live_mask, seq_id, -1)
    positions = jnp.sum(jnp.where(inside, offsets, 0), axis=1)
    return (indices, seq_id, positions, live_mask)


BF16 = jnp.bfloat16
F32 = jnp.float32
SLOTS = 8
MASKED = -1e30
VMEM_BYTES = 56 * 1024 * 1024
LANES = 128


def same_core_groups(size):
    return [[2 * chip + core for chip in range(size // 2)] for core in range(2)]


def swap_cores(block):
    size = lax.axis_size("fsdp")
    return lax.ppermute(block, "fsdp", [(i, i ^ 1) for i in range(size)])


def exchange(blocks):
    return lax.all_to_all(
        blocks,
        "fsdp",
        split_axis=0,
        concat_axis=0,
        tiled=True,
        axis_index_groups=same_core_groups(lax.axis_size("fsdp")),
    )


def spread(block):
    chips = lax.axis_size("fsdp") // 2
    return exchange(jnp.broadcast_to(block[None], (chips,) + block.shape))


def call(kernel, outs, ins, scratch=(), specs=None, flops=4e9):
    return pl.pallas_call(
        kernel,
        out_shape=outs,
        in_specs=specs,
        scratch_shapes=list(scratch),
        compiler_params=pltpu.CompilerParams(vmem_limit_bytes=VMEM_BYTES),
        cost_estimate=pl.CostEstimate(
            flops=int(flops), bytes_accessed=8_000_000, transcendentals=0
        ),
    )(*ins)


SCALAR = pl.BlockSpec(memory_space=pltpu.SMEM)
WHOLE = pl.BlockSpec(memory_space=pltpu.VMEM)
AWAY = pl.BlockSpec(memory_space=pl.ANY)


def shape(dims, kind):
    return jax.ShapeDtypeStruct(dims, kind)


def dot(left, right):
    return jnp.dot(left, right, preferred_element_type=F32)


def dot_nt(left, right):
    return lax.dot_general(left, right, (((1,), (1,)), ((), ())), preferred_element_type=F32)


def dot_tn(left, right):
    return lax.dot_general(left, right, (((0,), (0,)), ((), ())), preferred_element_type=F32)


def normed(values):
    scale = lax.rsqrt(jnp.mean(values * values, axis=-1, keepdims=True) + epsilon)
    return values * scale, scale


def normed_back(cot, unit, scale, gain):
    weighted = cot * gain
    inner = jnp.mean(weighted * unit, axis=-1, keepdims=True)
    return scale * (weighted - unit * inner), jnp.sum(cot * unit, axis=0, keepdims=True)


def ones_where(mask):
    return jnp.where(mask, 1.0, 0.0).astype(BF16)


def pick_flat(rows, count, per):
    place = lax.broadcasted_iota(jnp.int32, (1, count), 1)
    device, slot = lax.shift_right_logical(place, 3), place & (SLOTS - 1)
    source = jnp.where(slot < per, device * per + slot, -1)
    return ones_where(lax.broadcasted_iota(jnp.int32, (rows, count), 0) == source)


def pick_core(rows, chips, per, core):
    place = lax.broadcasted_iota(jnp.int32, (1, chips * per), 1)
    row, chip = lax.div(place, chips), lax.rem(place, chips)
    source = (2 * chip + core) * per + row
    return ones_where(lax.broadcasted_iota(jnp.int32, (rows, chips * per), 0) == source)


def pick_out(rows, count, core):
    place = lax.broadcasted_iota(jnp.int32, (1, count), 1)
    chip, row = lax.shift_right_logical(place, 3), place & (SLOTS - 1)
    source = (2 * chip + core) * SLOTS + row
    return ones_where(lax.broadcasted_iota(jnp.int32, (rows, count), 0) == source)


def pick_chip(rows, chips, per, core):
    low = (2 * lax.broadcasted_iota(jnp.int32, (1, chips), 1) + core) * per
    natural = lax.broadcasted_iota(jnp.int32, (rows, chips), 0)
    return ones_where((natural >= low) & (natural < low + per))


def gain_mask(first, per, rows, columns):
    row = lax.broadcasted_iota(jnp.int32, (rows, columns), 0)
    column = lax.broadcasted_iota(jnp.int32, (rows, columns), 1)
    return row == first + lax.rem(column, per)


def turned(values, cos, sin):
    half = values.shape[-1] // 2
    first, second = values[:, :half], values[:, half:]
    return jnp.concatenate([first * cos - second * sin, second * cos + first * sin], axis=1)


def before_attention(
    core_ref, tok, own, peer, cos, sin, raw, query_low, own_kv, gains, head_gains, weights, loose
):
    core = core_ref[0]
    width = tok.shape[1]
    kv_cols = own_kv.shape[1]
    head = kv_cols // 2
    q_cols = query_low.shape[1]
    columns = q_cols + kv_cols
    tiles = columns // LANES
    per, per_head = width // LANES, head // LANES
    chips = weights.shape[1] // per
    chunk = own.shape[0] // chips
    wide = jnp.zeros((width, LANES), F32)
    narrow = jnp.zeros((head, LANES), F32)
    for which, (block, parity) in enumerate(((own, core), (peer, 1 - core))):
        loose[...] = block[...].astype(F32)
        for row in range(per):
            for tile in range(tiles):
                weights[
                    which, row * chips : (row + 1) * chips, tile * LANES : (tile + 1) * LANES
                ] = loose[pl.ds(row * tiles + tile, chips, stride=chunk), :].astype(BF16)
        found = loose[pl.ds(per * tiles, chips, stride=chunk), :].astype(BF16)
        wide += dot(pick_chip(width, chips, per, parity), found)
        narrow += dot(pick_chip(head, chips, per_head, parity), found)
    wide, narrow = jnp.transpose(wide)[:32], jnp.transpose(narrow)[:32]
    for which in range(4):
        mask = gain_mask(which * per, per, 32, width)
        gains[which : which + 1, :] = jnp.sum(jnp.where(mask, wide, 0.0), 0, keepdims=True)
    for which in range(2):
        mask = gain_mask(4 * per + which * per_head, per_head, 32, head)
        head_gains[which : which + 1, :] = jnp.sum(jnp.where(mask, narrow, 0.0), 0, keepdims=True)
    unit, _ = normed(tok[...].astype(F32))
    low = (unit * gains[0:1, :]).astype(BF16)
    raw[...] = dot(dot(low, pick_core(width, chips, per, core)).astype(BF16), weights[0]) + dot(
        dot(low, pick_core(width, chips, per, 1 - core)).astype(BF16), weights[1]
    )
    for index in range(q_cols // head):
        span = slice(index * head, (index + 1) * head)
        unit, _ = normed(raw[:, span])
        query_low[:, span] = turned(unit * head_gains[0:1, :], cos[...], sin[...]).astype(BF16)
    unit, _ = normed(raw[:, q_cols : q_cols + head])
    own_kv[:, :head] = turned(unit * head_gains[1:2, :], cos[...], sin[...]).astype(BF16)
    own_kv[:, head:] = raw[:, q_cols + head :].astype(BF16)


def visible(q_seq, k_seq):
    queries, keys = q_seq.shape[0], k_seq.shape[1]
    row = lax.broadcasted_iota(jnp.int32, (queries, keys), 0)
    column = lax.broadcasted_iota(jnp.int32, (queries, keys), 1)
    distance = row - column + (keys - queries)
    same = (q_seq[...] == k_seq[...]) & (q_seq[...] >= 0)
    return (same & (distance >= 0) & (distance < WINDOW)) | (distance == 0)


def attention(query_low, kv_far, kv_near, kv_own, q_seq, k_seq, heads_low, log_total):
    head = kv_own.shape[1] // 2
    parts = (kv_far, kv_near, kv_own)
    keys = jnp.concatenate([part[:, :head] for part in parts], axis=0)
    values = jnp.concatenate([part[:, head:] for part in parts], axis=0)
    allowed = visible(q_seq, k_seq)
    for index in range(query_low.shape[1] // head):
        span = slice(index * head, (index + 1) * head)
        scores = dot_nt(query_low[:, span], keys) * query_scale
        scores = jnp.where(allowed, scores, MASKED)
        top = jnp.max(scores, axis=-1, keepdims=True)
        terms = jnp.exp(scores - top)
        total = jnp.sum(terms, axis=-1, keepdims=True)
        probs = (terms * (1.0 / total)).astype(BF16)
        heads_low[:, span] = dot(probs, values).astype(BF16)
        log_total[:, index : index + 1] = top + jnp.log(total)


def feed_forward(
    core_ref, tok, out_grad, live, gains, heads_low, full,
    mixed, d_state, d_heads, gain_grads, keep, send,
    weights, rest, down, act, act_slope, hidden, proj, state, total, back, low_flat, low, low_core,
    low_branch, loose, loose_out, turn_down, weight_sem, rest_sem,
):
    core = core_ref[0]
    tiles, tile = weights.shape[0], weights.shape[2]
    half = tiles // 2
    width = state.shape[1]
    q_cols = heads_low.shape[1]
    per = width // LANES
    blocks, strips, down_rows = keep.shape[0], keep.shape[1], turn_down.shape[3]
    chips = blocks * strips
    tile_chips = tile // (2 * down_rows)
    tile_rows = tile // down_rows * SLOTS
    columns_at = tiles * tile

    def weight_copy(index):
        return pltpu.make_async_copy(
            full.at[:, pl.ds(pl.multiple_of(index * tile, tile), tile)],
            weights.at[index],
            weight_sem.at[index],
        )

    rest_copy = pltpu.make_async_copy(
        full.at[:, columns_at : columns_at + rest.shape[1]], rest, rest_sem
    )
    rest_copy.start()
    for index in range(half):
        weight_copy(index).start()
        weight_copy(half + index).start()

    spread_flat = pick_flat(width, weights.shape[1], per)
    rest_copy.wait()
    w_out = rest[:, 2 * width :]
    proj[...] = dot(heads_low[...], w_out)
    unit, _ = normed(proj[...])
    state[...] = tok[...].astype(F32) + unit * gains[1:2, :]
    unit, scale = normed(state[...])
    low[...] = (unit * gains[2:3, :]).astype(BF16)
    low_flat[...] = dot(low[...], spread_flat).astype(BF16)
    low_core[0] = dot(low[...], pick_core(width, chips, per, core)).astype(BF16)
    low_core[1] = dot(low[...], pick_core(width, chips, per, 1 - core)).astype(BF16)
    total[...] = jnp.zeros_like(total)

    def down_tile(index):
        return down[pl.ds(pl.multiple_of(index * tile, tile), tile)]

    def forward(index, carry):
        columns = pl.ds(pl.multiple_of(index * tile, tile), tile)
        stored = rest[pl.ds(pl.multiple_of(index * tile_rows, tile_rows), tile_rows), : 2 * width]
        stored = stored.astype(F32).reshape(tile_rows // SLOTS, SLOTS, 2 * width)
        down[pl.ds(pl.multiple_of(index * tile, tile), tile)] = (
            jnp.concatenate([stored[:, :, :width], stored[:, :, width:]], axis=1)
            .reshape(tile, width)
            .astype(BF16)
        )
        weight_copy(index).wait()
        weight_copy(half + index).wait()
        gate = dot(low_flat[...], weights[index])
        up = dot(low_flat[...], weights[half + index])
        square = gate * gate
        bend = jnp.tanh(gate * (0.7978845608028654 * (1.0 + 0.044715 * square)))
        rise = 0.5 * (1.0 + bend)
        gelu = gate * rise
        slope = rise + 0.5 * gate * (1.0 - bend * bend) * (
            0.7978845608028654 * (1.0 + 0.134145 * square)
        )
        act[:, columns] = gelu
        act_slope[:, columns] = up * slope
        hidden[:, columns] = (gelu * up).astype(BF16)
        total[...] += dot(hidden[:, columns], down_tile(index))
        return carry

    lax.fori_loop(0, half, forward, 0)

    branch_unit, branch_scale = normed(total[...])
    mixed[...] = ((state[...] + branch_unit * gains[3:4, :]) * live[...]).astype(BF16)
    cotangent = out_grad[...].astype(F32) * live[...]
    d_branch, gain_grads[3:4, :] = normed_back(
        cotangent, branch_unit, branch_scale, gains[3:4, :]
    )
    low_branch[...] = d_branch.astype(BF16)
    back[...] = jnp.zeros_like(back)

    row_tiles = tiles * tile // LANES
    chunk = per * row_tiles

    def place(start, grad):
        for which in range(2):
            block = dot_tn(low_core[which], grad)
            for row in range(per):
                for part in range(tile // LANES):
                    loose[which, pl.ds(row * row_tiles + start + part, chips, stride=chunk), :] = (
                        block[row * chips : (row + 1) * chips, part * LANES : (part + 1) * LANES]
                    )

    down_at = chunk
    out_at = down_at + down_rows * (width // LANES)

    def backward(index, carry):
        columns = pl.ds(pl.multiple_of(index * tile, tile), tile)
        d_hidden = dot_nt(low_branch[...], down_tile(index))
        d_gate = (d_hidden * act_slope[:, columns]).astype(BF16)
        d_up = (d_hidden * act[:, columns]).astype(BF16)
        back[...] += dot_nt(d_gate, weights[index]) + dot_nt(d_up, weights[half + index])
        place(index * (tile // LANES), d_gate)
        place((half + index) * (tile // LANES), d_up)
        turn_down[...] = (
            dot_tn(hidden[:, columns], low_branch[...])
            .astype(BF16)
            .reshape(tile_chips // strips, strips, 2, down_rows, width)
        )
        tall = pl.ds(index * (tile_chips // strips), tile_chips // strips)
        for target, parity in ((keep, core), (send, 1 - core)):
            for part in range(width // LANES):
                top = down_at + part * down_rows
                target[tall, :, top : top + down_rows, :] = turn_down[
                    :, :, parity, :, part * LANES : (part + 1) * LANES
                ]
        return carry

    lax.fori_loop(0, half, backward, 0)

    def pack(block, carry):
        rows = pl.ds(pl.multiple_of(block * strips * chunk, strips * chunk), strips * chunk)
        for which, target in enumerate((keep, send)):
            target[block, :, :chunk, :] = (
                loose[which, rows, :].reshape(strips, chunk, LANES).astype(BF16)
            )
        return carry

    lax.fori_loop(0, blocks, pack, 0)

    high = back[...].astype(BF16)
    rounding = (back[...] - high.astype(F32)).astype(BF16)
    d_low = dot_nt(high, spread_flat) + dot_nt(rounding, spread_flat)
    d_norm, gain_grads[2:3, :] = normed_back(d_low, unit, scale, gains[2:3, :])
    d_state[...] = cotangent + d_norm
    proj_unit, proj_scale = normed(proj[...])
    d_proj, gain_grads[1:2, :] = normed_back(d_state[...], proj_unit, proj_scale, gains[1:2, :])
    proj_low = d_proj.astype(BF16)
    d_heads[...] = dot_nt(proj_low, w_out).astype(BF16)
    out_tiles = width // LANES
    loose_out[:, :, out_tiles * SLOTS :, :] = jnp.zeros(
        (blocks, strips, loose_out.shape[2] - out_tiles * SLOTS, LANES), F32
    )
    for target, parity in ((keep, core), (send, 1 - core)):
        heads = dot(heads_low[...], pick_out(q_cols, chips * SLOTS, parity)).astype(BF16)
        block = dot_tn(heads, proj_low)
        for part in range(out_tiles):
            loose_out[:, :, part * SLOTS : (part + 1) * SLOTS, :] = block[
                :, part * LANES : (part + 1) * LANES
            ].reshape(blocks, strips, SLOTS, LANES)
        target[:, :, out_at:, :] = loose_out[...].astype(BF16)


def attention_back(
    query_low, kv_far, kv_near, kv_own, d_heads, log_total, q_seq, k_seq,
    d_query, d_own, d_near, d_far, sum_keys, sum_values,
):
    head = kv_own.shape[1] // 2
    rows = kv_own.shape[0]
    parts = (kv_far, kv_near, kv_own)
    keys = jnp.concatenate([part[:, :head] for part in parts], axis=0)
    values = jnp.concatenate([part[:, head:] for part in parts], axis=0)
    allowed = visible(q_seq, k_seq)
    for index in range(query_low.shape[1] // head):
        span = slice(index * head, (index + 1) * head)
        scores = dot_nt(query_low[:, span], keys) * query_scale
        scores = jnp.where(allowed, scores, MASKED)
        probs = jnp.exp(scores - log_total[:, index : index + 1])
        d_probs = dot_nt(d_heads[:, span], values)
        inner = jnp.sum(probs * d_probs, axis=-1, keepdims=True)
        d_scores = (probs * (d_probs - inner)).astype(BF16)
        d_query[:, span] = dot(d_scores, keys) * query_scale
        key_term = dot_tn(d_scores, query_low[:, span]) * query_scale
        value_term = dot_tn(probs.astype(BF16), d_heads[:, span])
        if index == 0:
            sum_keys[...] = key_term
            sum_values[...] = value_term
        else:
            sum_keys[...] += key_term
            sum_values[...] += value_term
    for target, start in ((d_far, 0), (d_near, rows), (d_own, 2 * rows)):
        target[:, :head] = sum_keys[start : start + rows, :].astype(target.dtype)
        target[:, head:] = sum_values[start : start + rows, :].astype(target.dtype)


def after_attention(
    core_ref, raw, d_query, d_own, near, far, weights, tok, gains, head_gains, cos, sin,
    d_state, gain_grads, tokens_grad, keep, send, low, loose,
):
    core = core_ref[0]
    width = tok.shape[1]
    q_cols, kv_cols = d_query.shape[1], d_own.shape[1]
    head = kv_cols // 2
    tiles = (q_cols + kv_cols) // LANES
    per, per_head = width // LANES, head // LANES
    chips = weights.shape[1] // per
    chunk = keep.shape[0] // chips
    cosine, minus_sine = cos[...], -sin[...]
    query_gain_grad = jnp.zeros((1, head), F32)
    for index in range(q_cols // head):
        span = slice(index * head, (index + 1) * head)
        unit, scale = normed(raw[:, span])
        cot = turned(d_query[:, span], cosine, minus_sine)
        d_raw, part = normed_back(cot, unit, scale, head_gains[0:1, :])
        query_gain_grad += part
        low[:, span] = d_raw.astype(BF16)
    d_kv = d_own[...] + near[...].astype(F32) + far[...].astype(F32)
    unit, scale = normed(raw[:, q_cols : q_cols + head])
    cot = turned(d_kv[:, :head], cosine, minus_sine)
    d_raw, key_gain_grad = normed_back(cot, unit, scale, head_gains[1:2, :])
    low[:, q_cols : q_cols + head] = d_raw.astype(BF16)
    low[:, q_cols + head :] = d_kv[:, head:].astype(BF16)

    selectors = [pick_core(width, chips, per, parity) for parity in (core, 1 - core)]
    d_low = jnp.zeros(tok.shape, F32)
    for which, selector in enumerate(selectors):
        part = dot_nt(low[...], weights[which])
        high = part.astype(BF16)
        rounding = (part - high.astype(F32)).astype(BF16)
        d_low += dot_nt(high, selector) + dot_nt(rounding, selector)
    unit, scale = normed(tok[...].astype(F32))
    d_norm, in_gain_grad = normed_back(d_low, unit, scale, gains[0:1, :])
    tokens_grad[...] = (d_state[...] + d_norm).astype(BF16)

    wide = jnp.zeros((LANES, width), F32)
    vectors = [in_gain_grad] + [gain_grads[i : i + 1, :] for i in range(1, 4)]
    for which, vector in enumerate(vectors):
        wide = jnp.where(gain_mask(which * per, per, LANES, width), vector, wide)
    narrow = jnp.zeros((LANES, head), F32)
    for which, vector in enumerate((query_gain_grad, key_gain_grad)):
        mask = gain_mask(4 * per + which * per_head, per_head, LANES, head)
        narrow = jnp.where(mask, vector, narrow)
    wide, narrow = wide.astype(BF16), narrow.astype(BF16)
    attn_low = (unit * gains[0:1, :]).astype(BF16)
    for row in range(per * tiles + 1, chunk):
        loose[pl.ds(row, chips, stride=chunk), :] = jnp.zeros((chips, LANES), F32)
    for target, selector, parity in ((keep, selectors[0], core), (send, selectors[1], 1 - core)):
        extra = dot(wide, pick_chip(width, chips, per, parity)) + dot(
            narrow, pick_chip(head, chips, per_head, parity)
        )
        loose[pl.ds(per * tiles, chips, stride=chunk), :] = jnp.transpose(extra)
        block = dot_tn(dot(attn_low, selector).astype(BF16), low[...])
        for row in range(per):
            for tile in range(tiles):
                loose[pl.ds(row * tiles + tile, chips, stride=chunk), :] = block[
                    row * chips : (row + 1) * chips, tile * LANES : (tile + 1) * LANES
                ]
        target[...] = loose[...].astype(BF16)


def on_device(
    tokens,
    out_grad,
    seq_start,
    seq_len,
    w_query,
    w_key_value,
    w_output,
    w_gate_up,
    w_down,
    norm_attn_in,
    norm_attn_out,
    norm_mlp_in,
    norm_mlp_out,
    norm_query,
    norm_key,
):
    size = lax.axis_size("fsdp")
    chips = size // 2
    me = lax.axis_index("fsdp")
    core = me % 2
    core_arg = core.astype(jnp.int32).reshape(1)
    tok_rows, width = tokens.shape
    shard = w_query.shape[0]
    q_cols, kv_cols = w_query.shape[1], w_key_value.shape[1]
    qkv_cols = q_cols + kv_cols
    gu_cols, ff = w_gate_up.shape[1], w_down.shape[0] * size
    down_rows = w_down.shape[0]
    head = kv_cols // 2
    hshard = norm_query.shape[0]

    mlp_full = lax.all_gather(
        jnp.concatenate(
            [
                jnp.pad(w_gate_up, ((0, SLOTS - shard), (0, 0))),
                w_down[:SLOTS],
                w_down[SLOTS:],
                w_output,
            ],
            axis=1,
        ),
        "fsdp",
        axis=0,
        tiled=True,
    )

    tiles = qkv_cols // LANES
    chunk = 64
    gain_row = jnp.zeros((1, LANES), BF16)
    gain_count = 0
    for part in (norm_attn_in, norm_attn_out, norm_mlp_in, norm_mlp_out, norm_query, norm_key):
        wide = part.shape[0]
        gain_row = gain_row + jnp.pad(part[None], ((0, 0), (gain_count, LANES - gain_count - wide)))
        gain_count += wide
    pack = jnp.concatenate(
        [
            jnp.concatenate([w_query, w_key_value], axis=1).reshape(shard * tiles, LANES),
            jnp.pad(gain_row, ((0, chunk - shard * tiles - 1), (0, 0))),
        ],
        axis=0,
    )
    own = spread(pack).reshape(chips * chunk, LANES)
    peer = swap_cores(own)

    key_reach = (WINDOW + tok_rows - 2) // tok_rows
    first_token = me * tok_rows
    q_index, q_seq, q_pos, q_live = token_layout(seq_start, seq_len, first_token, tok_rows)
    k_index, k_seq, k_pos, k_live = token_layout(
        seq_start, seq_len, first_token - key_reach * tok_rows, (key_reach + 1) * tok_rows
    )
    live = q_live.astype(F32)[:, None]
    q_seq, k_seq = q_seq[:, None], k_seq[None, :]
    inv_freq = theta_base ** (-2.0 * jnp.arange(head // 2, dtype=F32) / head)
    angles = q_pos.astype(F32)[:, None] * inv_freq[None, :]
    cos_vals, sin_vals = jnp.cos(angles), jnp.sin(angles)

    raw, query_low, own_kv, gains, head_gains, attn_weights = call(
        before_attention,
        (
            shape((tok_rows, qkv_cols), F32),
            shape((tok_rows, q_cols), BF16),
            shape((tok_rows, kv_cols), BF16),
            shape((8, width), F32),
            shape((8, head), F32),
            shape((2, chips * shard, qkv_cols), BF16),
        ),
        (core_arg, tokens, own, peer, cos_vals, sin_vals),
        scratch=(pltpu.VMEM((chips * chunk, LANES), F32),),
        specs=[SCALAR] + [WHOLE] * 5,
    )
    kv_near = shifted(own_kv, "fsdp", 1)
    kv_far = shifted(own_kv, "fsdp", 2)
    heads_low, log_total = call(
        attention,
        (shape((tok_rows, q_cols), BF16), shape((tok_rows, LANES), F32)),
        (query_low, kv_far, kv_near, own_kv, q_seq, k_seq),
        specs=[WHOLE] * 6,
        flops=20e9,
    )

    tile = 512
    blocks, strips = 8, chips // 8
    down_at = shard * gu_cols // LANES
    out_at = down_at + down_rows * (width // LANES)
    chunk_rows = out_at + 6 * SLOTS
    mixed, d_state, d_heads, gain_grads, keep, send = call(
        feed_forward,
        (
            shape((tok_rows, width), BF16),
            shape((tok_rows, width), F32),
            shape((tok_rows, q_cols), BF16),
            shape((8, width), F32),
            shape((blocks, strips, chunk_rows, LANES), BF16),
            shape((blocks, strips, chunk_rows, LANES), BF16),
        ),
        (
            core_arg, tokens, out_grad, live, gains, heads_low, mlp_full,
        ),
        scratch=(
            pltpu.VMEM((gu_cols // tile, size * SLOTS, tile), BF16),
            pltpu.VMEM((size * SLOTS, 3 * width), BF16),
            pltpu.VMEM((ff, width), BF16),
            pltpu.VMEM((tok_rows, ff), F32),
            pltpu.VMEM((tok_rows, ff), F32),
            pltpu.VMEM((tok_rows, ff), BF16),
            pltpu.VMEM((tok_rows, width), F32),
            pltpu.VMEM((tok_rows, width), F32),
            pltpu.VMEM((tok_rows, width), F32),
            pltpu.VMEM((tok_rows, size * SLOTS), F32),
            pltpu.VMEM((tok_rows, size * SLOTS), BF16),
            pltpu.VMEM((tok_rows, width), BF16),
            pltpu.VMEM((2, tok_rows, width // 2), BF16),
            pltpu.VMEM((tok_rows, width), BF16),
            pltpu.VMEM((2, chips * down_at, LANES), F32),
            pltpu.VMEM((blocks, strips, 6 * SLOTS, LANES), F32),
            pltpu.VMEM((tile // (2 * down_rows) // strips, strips, 2, down_rows, width), BF16),
            pltpu.SemaphoreType.DMA((gu_cols // tile,)),
            pltpu.SemaphoreType.DMA,
        ),
        specs=[SCALAR] + [WHOLE] * 5 + [AWAY],
        flops=12e9,
    )
    both_mlp = (keep.astype(F32) + swap_cores(send).astype(F32)).astype(BF16)

    d_query, d_own, d_near, d_far = call(
        attention_back,
        (
            shape((tok_rows, q_cols), F32),
            shape((tok_rows, kv_cols), F32),
            shape((tok_rows, kv_cols), BF16),
            shape((tok_rows, kv_cols), BF16),
        ),
        (query_low, kv_far, kv_near, own_kv, d_heads, log_total, q_seq, k_seq),
        scratch=(
            pltpu.VMEM(((key_reach + 1) * tok_rows, head), F32),
            pltpu.VMEM(((key_reach + 1) * tok_rows, head), F32),
        ),
        specs=[WHOLE] * 8,
        flops=20e9,
    )
    near = shifted(d_near, "fsdp", -1)
    far = shifted(d_far, "fsdp", -2)
    both_mlp, near, far = lax.optimization_barrier((both_mlp, near, far))
    mlp_parts = exchange(both_mlp.reshape(chips, chunk_rows, LANES))
    tokens_grad, keep, send = call(
        after_attention,
        (
            shape((tok_rows, width), BF16),
            shape((chips * chunk, LANES), BF16),
            shape((chips * chunk, LANES), BF16),
        ),
        (
            core_arg, raw, d_query, d_own, near, far, attn_weights, tokens, gains,
            head_gains, cos_vals, sin_vals, d_state, gain_grads,
        ),
        scratch=(
            pltpu.VMEM((tok_rows, qkv_cols), BF16),
            pltpu.VMEM((chips * chunk, LANES), F32),
        ),
        specs=[SCALAR] + [WHOLE] * 13,
        flops=20e9,
    )
    both = (keep.astype(F32) + swap_cores(send).astype(F32)).astype(BF16)
    both, mlp_parts = lax.optimization_barrier((both, mlp_parts))
    share_attn = jnp.sum(exchange(both.reshape(chips, chunk, LANES)).astype(F32), axis=0)
    share_qkv = share_attn[: shard * tiles].reshape(shard, tiles * LANES)
    share_gains = share_attn[shard * tiles, :gain_count]

    share_mlp = jnp.sum(mlp_parts.astype(F32), axis=0)
    share_gate_up = share_mlp[:down_at].reshape(shard, gu_cols)
    share_down = (
        share_mlp[down_at:out_at]
        .reshape(width // LANES, down_rows, LANES)
        .transpose(1, 0, 2)
        .reshape(down_rows, width)
    )
    share_output = (
        share_mlp[out_at : out_at + SLOTS * (width // LANES)]
        .reshape(width // LANES, SLOTS, LANES)
        .transpose(1, 0, 2)
        .reshape(SLOTS, width)
    )
    return (
        mixed,
        tokens_grad,
        share_qkv[:, :q_cols],
        share_qkv[:, q_cols:],
        share_output,
        share_gate_up,
        share_down,
        share_gains[:shard],
        share_gains[shard : 2 * shard],
        share_gains[2 * shard : 3 * shard],
        share_gains[3 * shard : 4 * shard],
        share_gains[4 * shard : 4 * shard + hshard],
        share_gains[4 * shard + hshard :],
    )


def solution(mesh):
    placed = (
        P("fsdp", None),
        P("fsdp", None),
        P(),
        P(),
        P("fsdp", None),
        P("fsdp", None),
        P("fsdp", None),
        P("fsdp", None),
        P("fsdp", None),
        P("fsdp"),
        P("fsdp"),
        P("fsdp"),
        P("fsdp"),
        P("fsdp"),
        P("fsdp"),
    )
    return jax.shard_map(
        on_device,
        mesh=mesh,
        in_specs=placed,
        out_specs=(
            P("fsdp", None),
            P("fsdp", None),
            P("fsdp", None),
            P("fsdp", None),
            P("fsdp", None),
            P("fsdp", None),
            P("fsdp", None),
            P("fsdp"),
            P("fsdp"),
            P("fsdp"),
            P("fsdp"),
            P("fsdp"),
            P("fsdp"),
        ),
        check_vma=False,
    )
```

```python
import jax
import jax.numpy as jnp
from jax import lax
from jax.experimental import pallas as pl
from jax.experimental.pallas import tpu as pltpu
from jax.sharding import PartitionSpec as P

WINDOW = 512


epsilon = 1e-06
theta_base = 10000.0
query_scale = 0.0625


def shifted(block, axis, distance):
    devices = range(lax.axis_size(axis))
    route = [(i - distance, i) for i in devices if i - distance in devices]
    return lax.ppermute(block, axis, route)


def token_layout(seq_start, seq_len, first_token, token_count):
    indices = first_token + jnp.arange(token_count, dtype=jnp.int32)
    offsets = indices[:, None] - seq_start[None, :]
    inside = (offsets >= 0) & (offsets < seq_len[None, :])
    live_mask = jnp.any(inside, axis=1)
    seq_numbers = jnp.arange(seq_start.shape[0], dtype=jnp.int32)
    seq_id = jnp.sum(jnp.where(inside, seq_numbers[None, :], 0), axis=1)
    seq_id = jnp.where(live_mask, seq_id, -1)
    positions = jnp.sum(jnp.where(inside, offsets, 0), axis=1)
    return (indices, seq_id, positions, live_mask)


BF16 = jnp.bfloat16
F32 = jnp.float32
SLOTS = 8
MASKED = -1e30
ODD = 1
VMEM_BYTES = 56 * 1024 * 1024
LANES = 128


def same_core_groups(size):
    return [[2 * chip + core for chip in range(size // 2)] for core in range(2)]


def swap_cores(block):
    size = lax.axis_size("fsdp")
    return lax.ppermute(block, "fsdp", [(i, i ^ 1) for i in range(size)])


def exchange(blocks):
    return lax.all_to_all(
        blocks,
        "fsdp",
        split_axis=0,
        concat_axis=0,
        tiled=True,
        axis_index_groups=same_core_groups(lax.axis_size("fsdp")),
    )


def spread(block):
    chips = lax.axis_size("fsdp") // 2
    return exchange(jnp.broadcast_to(block[None], (chips,) + block.shape))


def call(kernel, outs, ins, scratch=(), specs=None, flops=4e9, out_specs=None):
    return pl.pallas_call(
        kernel,
        out_shape=outs,
        in_specs=specs,
        **({} if out_specs is None else {"out_specs": out_specs}),
        scratch_shapes=list(scratch),
        compiler_params=pltpu.CompilerParams(vmem_limit_bytes=VMEM_BYTES),
        cost_estimate=pl.CostEstimate(
            flops=int(flops), bytes_accessed=8_000_000, transcendentals=0
        ),
    )(*ins)


SCALAR = pl.BlockSpec(memory_space=pltpu.SMEM)
WHOLE = pl.BlockSpec(memory_space=pltpu.VMEM)
AWAY = pl.BlockSpec(memory_space=pl.ANY)


def shape(dims, kind):
    return jax.ShapeDtypeStruct(dims, kind)


def dot(left, right):
    return jnp.dot(left, right, preferred_element_type=F32)


def dot_nt(left, right):
    return lax.dot_general(left, right, (((1,), (1,)), ((), ())), preferred_element_type=F32)


def dot_tn(left, right):
    return lax.dot_general(left, right, (((0,), (0,)), ((), ())), preferred_element_type=F32)


def normed(values):
    scale = lax.rsqrt(jnp.mean(values * values, axis=-1, keepdims=True) + epsilon)
    return values * scale, scale


def normed_back(cot, unit, scale, gain):
    weighted = cot * gain
    inner = jnp.mean(weighted * unit, axis=-1, keepdims=True)
    return scale * (weighted - unit * inner), jnp.sum(cot * unit, axis=0, keepdims=True)


def ones_where(mask):
    return jnp.where(mask, 1.0, 0.0).astype(BF16)


def pick_flat(rows, count, per):
    place = lax.broadcasted_iota(jnp.int32, (1, count), 1)
    device, slot = lax.shift_right_logical(place, 3), place & (SLOTS - 1)
    source = jnp.where(slot < per, device * per + slot, -1)
    return ones_where(lax.broadcasted_iota(jnp.int32, (rows, count), 0) == source)


def pick_core(rows, chips, per, core):
    place = lax.broadcasted_iota(jnp.int32, (1, chips * per), 1)
    row, chip = lax.div(place, chips), lax.rem(place, chips)
    source = (2 * chip + core) * per + row
    return ones_where(lax.broadcasted_iota(jnp.int32, (rows, chips * per), 0) == source)


def pick_chip(rows, chips, per, core):
    low = (2 * lax.broadcasted_iota(jnp.int32, (1, chips), 1) + core) * per
    natural = lax.broadcasted_iota(jnp.int32, (rows, chips), 0)
    return ones_where((natural >= low) & (natural < low + per))


def gain_mask(first, per, rows, columns):
    row = lax.broadcasted_iota(jnp.int32, (rows, columns), 0)
    column = lax.broadcasted_iota(jnp.int32, (rows, columns), 1)
    return row == first + lax.rem(column, per)


def turned(values, cos, sin):
    half = values.shape[-1] // 2
    first, second = values[:, :half], values[:, half:]
    return jnp.concatenate([first * cos - second * sin, second * cos + first * sin], axis=1)


def before_attention(
    core_ref, tok, own, peer, cos, sin, raw, query_low, own_kv, gains, head_gains, weights, loose
):
    core = core_ref[0]
    width = tok.shape[1]
    kv_cols = own_kv.shape[1]
    head = kv_cols // 2
    q_cols = query_low.shape[1]
    columns = q_cols + kv_cols
    tiles = columns // LANES
    per, per_head = width // LANES, head // LANES
    chips = weights.shape[1] // per
    chunk = own.shape[0] // chips
    wide = jnp.zeros((width, LANES), F32)
    narrow = jnp.zeros((head, LANES), F32)
    stride = chunk + ODD
    for which, (block, parity) in enumerate(((own, core), (peer, 1 - core))):
        for chip in range(chips):
            loose[chip * stride : chip * stride + chunk, :] = block[
                chip * chunk : (chip + 1) * chunk, :
            ].astype(F32)
        for row in range(per):
            for tile in range(tiles):
                weights[
                    which, row * chips : (row + 1) * chips, tile * LANES : (tile + 1) * LANES
                ] = loose[pl.ds(row * tiles + tile, chips, stride=stride), :].astype(BF16)
        found = loose[pl.ds(per * tiles, chips, stride=stride), :].astype(BF16)
        wide += dot(pick_chip(width, chips, per, parity), found)
        narrow += dot(pick_chip(head, chips, per_head, parity), found)
    wide, narrow = jnp.transpose(wide)[:32], jnp.transpose(narrow)[:32]
    for which in range(4):
        mask = gain_mask(which * per, per, 32, width)
        gains[which : which + 1, :] = jnp.sum(jnp.where(mask, wide, 0.0), 0, keepdims=True)
    for which in range(2):
        mask = gain_mask(4 * per + which * per_head, per_head, 32, head)
        head_gains[which : which + 1, :] = jnp.sum(jnp.where(mask, narrow, 0.0), 0, keepdims=True)
    unit, _ = normed(tok[...].astype(F32))
    low = (unit * gains[0:1, :]).astype(BF16)
    raw[...] = dot(dot(low, pick_core(width, chips, per, core)).astype(BF16), weights[0]) + dot(
        dot(low, pick_core(width, chips, per, 1 - core)).astype(BF16), weights[1]
    )
    for index in range(q_cols // head):
        span = slice(index * head, (index + 1) * head)
        unit, _ = normed(raw[:, span])
        query_low[:, span] = turned(unit * head_gains[0:1, :], cos[...], sin[...]).astype(BF16)
    unit, _ = normed(raw[:, q_cols : q_cols + head])
    own_kv[:, :head] = turned(unit * head_gains[1:2, :], cos[...], sin[...]).astype(BF16)
    own_kv[:, head:] = raw[:, q_cols + head :].astype(BF16)


def visible(q_seq, k_seq):
    queries, keys = q_seq.shape[0], k_seq.shape[1]
    row = lax.broadcasted_iota(jnp.int32, (queries, keys), 0)
    column = lax.broadcasted_iota(jnp.int32, (queries, keys), 1)
    distance = row - column + (keys - queries)
    same = (q_seq[...] == k_seq[...]) & (q_seq[...] >= 0)
    return (same & (distance >= 0) & (distance < WINDOW)) | (distance == 0)


def attention(query_low, kv_far, kv_near, kv_own, q_seq, k_seq, heads_low, log_total):
    head = kv_own.shape[1] // 2
    parts = (kv_far, kv_near, kv_own)
    keys = jnp.concatenate([part[:, :head] for part in parts], axis=0)
    values = jnp.concatenate([part[:, head:] for part in parts], axis=0)
    allowed = visible(q_seq, k_seq)
    for index in range(query_low.shape[1] // head):
        span = slice(index * head, (index + 1) * head)
        scores = dot_nt(query_low[:, span], keys) * query_scale
        scores = jnp.where(allowed, scores, MASKED)
        top = jnp.max(scores, axis=-1, keepdims=True)
        terms = jnp.exp(scores - top)
        total = jnp.sum(terms, axis=-1, keepdims=True)
        probs = (terms * (1.0 / total)).astype(BF16)
        heads_low[:, span] = dot(probs, values).astype(BF16)
        log_total[:, index : index + 1] = top + jnp.log(total)


def feed_forward(
    core_ref, tok, out_grad, live, gains, heads_low, full,
    mixed, d_state, d_heads, gain_grads, low_own, d_gate_up_out, own_down_out, own_out_out, send_out,
    weights, rest, down, act, act_slope, hidden, proj, state, total, back, low_flat, low, turned_low,
    low_branch, loose, loose_out, turn_down, d_gate_up, own_down, own_out, send,
    weight_sem, rest_sem, out_sem,
):
    core = core_ref[0]
    tiles, tile = weights.shape[0], weights.shape[2]
    half = tiles // 2
    width = state.shape[1]
    q_cols = heads_low.shape[1]
    per = width // LANES
    blocks, strips, down_rows = send.shape[0], send.shape[1], turn_down.shape[3]
    chips = blocks * strips
    tile_chips = tile // (2 * down_rows)
    tile_rows = tile // down_rows * SLOTS
    columns_at = tiles * tile

    def weight_copy(index):
        return pltpu.make_async_copy(
            full.at[:, pl.ds(pl.multiple_of(index * tile, tile), tile)],
            weights.at[index],
            weight_sem.at[index],
        )

    def rest_copy(which, first, last):
        return pltpu.make_async_copy(
            full.at[:, columns_at + first : columns_at + last],
            rest.at[:, first:last],
            rest_sem.at[which],
        )

    out_copy = rest_copy(0, 2 * width, 3 * width)
    down_copy = rest_copy(1, 0, 2 * width)
    out_copy.start()
    down_copy.start()
    for index in range(half):
        weight_copy(index).start()
        weight_copy(half + index).start()

    spread_flat = pick_flat(width, weights.shape[1], per)
    out_copy.wait()
    w_out = rest[:, 2 * width :]
    proj[...] = dot(heads_low[...], w_out)
    unit, _ = normed(proj[...])
    state[...] = tok[...].astype(F32) + unit * gains[1:2, :]
    unit, scale = normed(state[...])
    low[...] = (unit * gains[2:3, :]).astype(BF16)
    low_flat[...] = dot(low[...], spread_flat).astype(BF16)
    low_own[...] = dot(low[...], pick_core(width, chips, per, core)).astype(BF16)
    turned_low[...] = jnp.transpose(
        dot(low[...], pick_core(width, chips, per, 1 - core))
    ).astype(BF16)
    total[...] = jnp.zeros_like(total)
    down_copy.wait()

    def down_tile(index):
        return down[pl.ds(pl.multiple_of(index * tile, tile), tile)]

    def forward(index, carry):
        columns = pl.ds(pl.multiple_of(index * tile, tile), tile)
        stored = rest[pl.ds(pl.multiple_of(index * tile_rows, tile_rows), tile_rows), : 2 * width]
        stored = stored.astype(F32).reshape(tile_rows // SLOTS, SLOTS, 2 * width)
        down[pl.ds(pl.multiple_of(index * tile, tile), tile)] = (
            jnp.concatenate([stored[:, :, :width], stored[:, :, width:]], axis=1)
            .reshape(tile, width)
            .astype(BF16)
        )
        weight_copy(index).wait()
        weight_copy(half + index).wait()
        gate = dot(low_flat[...], weights[index])
        up = dot(low_flat[...], weights[half + index])
        square = gate * gate
        bend = jnp.tanh(gate * (0.7978845608028654 * (1.0 + 0.044715 * square)))
        rise = 0.5 * (1.0 + bend)
        gelu = gate * rise
        slope = rise + 0.5 * gate * (1.0 - bend * bend) * (
            0.7978845608028654 * (1.0 + 0.134145 * square)
        )
        act[:, columns] = gelu
        act_slope[:, columns] = up * slope
        hidden[:, columns] = (gelu * up).astype(BF16)
        total[...] += dot(hidden[:, columns], down_tile(index))
        return carry

    lax.fori_loop(0, half, forward, 0)

    branch_unit, branch_scale = normed(total[...])
    mixed[...] = ((state[...] + branch_unit * gains[3:4, :]) * live[...]).astype(BF16)
    cotangent = out_grad[...].astype(F32) * live[...]
    d_branch, gain_grads[3:4, :] = normed_back(
        cotangent, branch_unit, branch_scale, gains[3:4, :]
    )
    low_branch[...] = d_branch.astype(BF16)
    back[...] = jnp.zeros_like(back)

    row_tiles = tiles * tile // LANES
    chunk = per * row_tiles

    def place(start, grad):
        place_rows(loose, dot(turned_low[...], grad), start, per, chips, row_tiles)

    down_at = chunk
    out_at = down_at + down_rows * (width // LANES)

    def backward(index, carry):
        columns = pl.ds(pl.multiple_of(index * tile, tile), tile)
        d_hidden = dot_nt(low_branch[...], down_tile(index))
        d_gate = (d_hidden * act_slope[:, columns]).astype(BF16)
        d_up = (d_hidden * act[:, columns]).astype(BF16)
        d_gate_up[:, columns] = d_gate
        d_gate_up[:, pl.ds(pl.multiple_of((half + index) * tile, tile), tile)] = d_up
        back[...] += dot_nt(d_gate, weights[index]) + dot_nt(d_up, weights[half + index])
        place(index * (tile // LANES), d_gate)
        place((half + index) * (tile // LANES), d_up)
        turn_down[...] = (
            dot_tn(hidden[:, columns], low_branch[...])
            .astype(BF16)
            .reshape(tile_chips // strips, strips, 2, down_rows, width)
        )
        tall = pl.ds(index * (tile_chips // strips), tile_chips // strips)
        for part in range(width // LANES):
            top = part * down_rows
            lanes = slice(part * LANES, (part + 1) * LANES)
            own_down[tall, :, top : top + down_rows, :] = turn_down[:, :, core, :, lanes]
            send[tall, :, down_at + top : down_at + top + down_rows, :] = turn_down[
                :, :, 1 - core, :, lanes
            ]
        return carry

    lax.fori_loop(0, half, backward, 0)
    copies = [
        pltpu.make_async_copy(d_gate_up, d_gate_up_out, out_sem.at[0]),
        pltpu.make_async_copy(own_down, own_down_out, out_sem.at[1]),
    ]
    for copy in copies:
        copy.start()

    def pack(block, carry):
        for strip in range(strips):
            send[block, strip, :chunk, :] = loose_chunk(loose, block * strips + strip, chunk).astype(
                BF16
            )
        return carry

    lax.fori_loop(0, blocks, pack, 0)
    copies.append(
        pltpu.make_async_copy(
            send.at[:, :, :out_at, :], send_out.at[:, :, :out_at, :], out_sem.at[2]
        )
    )
    copies[-1].start()

    high = back[...].astype(BF16)
    rounding = (back[...] - high.astype(F32)).astype(BF16)
    d_low = dot_nt(high, spread_flat) + dot_nt(rounding, spread_flat)
    d_norm, gain_grads[2:3, :] = normed_back(d_low, unit, scale, gains[2:3, :])
    d_state[...] = cotangent + d_norm
    proj_unit, proj_scale = normed(proj[...])
    d_proj, gain_grads[1:2, :] = normed_back(d_state[...], proj_unit, proj_scale, gains[1:2, :])
    proj_low = d_proj.astype(BF16)
    d_heads[...] = dot_nt(proj_low, w_out).astype(BF16)
    loose_out[...] = dot_tn(heads_low[...], proj_low).reshape(blocks, strips, 2, SLOTS, width)
    out_tiles = width // LANES
    for target, parity, start in ((own_out, core, 0), (send, 1 - core, out_at)):
        for part in range(out_tiles // 2 + 1):
            lanes = [slice(i * LANES, (i + 1) * LANES) for i in (2 * part, 2 * part + 1)]
            pair = [
                loose_out[:, :, parity, :, lane]
                if lane.stop <= width
                else jnp.zeros((blocks, strips, SLOTS, LANES), F32)
                for lane in lanes
            ]
            top = start + 2 * part * SLOTS
            target[:, :, top : top + 2 * SLOTS, :] = jnp.concatenate(pair, axis=2).astype(BF16)
    copies += [
        pltpu.make_async_copy(own_out, own_out_out, out_sem.at[3]),
        pltpu.make_async_copy(
            send.at[:, :, out_at:, :], send_out.at[:, :, out_at:, :], out_sem.at[4]
        ),
    ]
    for copy in copies[-2:]:
        copy.start()
    for copy in copies:
        copy.wait()


def place_rows(loose, block, start, per, chips, row_tiles):
    stride = per * row_tiles + ODD
    for row in range(per):
        for part in range(block.shape[1] // LANES):
            loose[pl.ds(row * row_tiles + start + part, chips, stride=stride), :] = block[
                row * chips : (row + 1) * chips, part * LANES : (part + 1) * LANES
            ]


def loose_chunk(loose, chip, chunk):
    return loose[pl.ds(chip * (chunk + ODD), chunk), :]


def own_gradients(
    d_gate_up, low_own, own_down, own_out, arrived, both_out,
    both, other, turned_low, loose, arrived_sem, both_sem,
):
    copy = pltpu.make_async_copy(arrived, other, arrived_sem)
    copy.start()
    blocks, strips, down_size = own_down.shape[:3]
    chips = blocks * strips
    per = low_own.shape[1] // chips
    tile = 512
    steps = d_gate_up.shape[1] // tile
    row_tiles = d_gate_up.shape[1] // LANES
    chunk = per * row_tiles
    turned_low[...] = jnp.transpose(low_own[...].astype(F32)).astype(BF16)

    def place(index, carry):
        grad = d_gate_up[:, pl.ds(pl.multiple_of(index * tile, tile), tile)]
        block = dot(turned_low[...], grad)
        place_rows(loose, block, index * (tile // LANES), per, chips, row_tiles)
        return carry

    lax.fori_loop(0, steps, place, 0)
    copy.wait()

    def leave(block):
        return pltpu.make_async_copy(both.at[block], both_out.at[block], both_sem.at[block])

    def pack(block, carry):
        for strip in range(strips):
            both[block, strip, :chunk, :] = (
                loose_chunk(loose, block * strips + strip, chunk)
                + other[block, strip, :chunk, :].astype(F32)
            ).astype(BF16)
        low, high = chunk, chunk + down_size
        both[block, :, low:high, :] = (
            own_down[block].astype(F32) + other[block, :, low:high, :].astype(F32)
        ).astype(BF16)
        both[block, :, high:, :] = (
            own_out[block].astype(F32) + other[block, :, high:, :].astype(F32)
        ).astype(BF16)
        leave(block).start()
        return carry

    lax.fori_loop(0, blocks, pack, 0)
    for block in range(blocks):
        leave(block).wait()


def attention_back(
    query_low, kv_far, kv_near, kv_own, d_heads, log_total, q_seq, k_seq,
    d_query, d_own, d_near, d_far, sum_keys, sum_values,
):
    head = kv_own.shape[1] // 2
    rows = kv_own.shape[0]
    parts = (kv_far, kv_near, kv_own)
    keys = jnp.concatenate([part[:, :head] for part in parts], axis=0)
    values = jnp.concatenate([part[:, head:] for part in parts], axis=0)
    allowed = visible(q_seq, k_seq)
    for index in range(query_low.shape[1] // head):
        span = slice(index * head, (index + 1) * head)
        scores = dot_nt(query_low[:, span], keys) * query_scale
        scores = jnp.where(allowed, scores, MASKED)
        probs = jnp.exp(scores - log_total[:, index : index + 1])
        d_probs = dot_nt(d_heads[:, span], values)
        inner = jnp.sum(probs * d_probs, axis=-1, keepdims=True)
        d_scores = (probs * (d_probs - inner)).astype(BF16)
        d_query[:, span] = dot(d_scores, keys) * query_scale
        key_term = dot_tn(d_scores, query_low[:, span]) * query_scale
        value_term = dot_tn(probs.astype(BF16), d_heads[:, span])
        if index == 0:
            sum_keys[...] = key_term
            sum_values[...] = value_term
        else:
            sum_keys[...] += key_term
            sum_values[...] += value_term
    for target, start in ((d_far, 0), (d_near, rows), (d_own, 2 * rows)):
        target[:, :head] = sum_keys[start : start + rows, :].astype(target.dtype)
        target[:, head:] = sum_values[start : start + rows, :].astype(target.dtype)


def after_attention(
    core_ref, raw, d_query, d_own, near, far, weights, tok, gains, head_gains, cos, sin,
    d_state, gain_grads, tokens_grad, keep, send, low, loose,
):
    core = core_ref[0]
    width = tok.shape[1]
    q_cols, kv_cols = d_query.shape[1], d_own.shape[1]
    head = kv_cols // 2
    tiles = (q_cols + kv_cols) // LANES
    per, per_head = width // LANES, head // LANES
    chips = weights.shape[1] // per
    chunk = keep.shape[0] // chips
    cosine, minus_sine = cos[...], -sin[...]
    query_gain_grad = jnp.zeros((1, head), F32)
    for index in range(q_cols // head):
        span = slice(index * head, (index + 1) * head)
        unit, scale = normed(raw[:, span])
        cot = turned(d_query[:, span], cosine, minus_sine)
        d_raw, part = normed_back(cot, unit, scale, head_gains[0:1, :])
        query_gain_grad += part
        low[:, span] = d_raw.astype(BF16)
    d_kv = d_own[...] + near[...].astype(F32) + far[...].astype(F32)
    unit, scale = normed(raw[:, q_cols : q_cols + head])
    cot = turned(d_kv[:, :head], cosine, minus_sine)
    d_raw, key_gain_grad = normed_back(cot, unit, scale, head_gains[1:2, :])
    low[:, q_cols : q_cols + head] = d_raw.astype(BF16)
    low[:, q_cols + head :] = d_kv[:, head:].astype(BF16)

    selectors = [pick_core(width, chips, per, parity) for parity in (core, 1 - core)]
    d_low = jnp.zeros(tok.shape, F32)
    for which, selector in enumerate(selectors):
        part = dot_nt(low[...], weights[which])
        high = part.astype(BF16)
        rounding = (part - high.astype(F32)).astype(BF16)
        d_low += dot_nt(high, selector) + dot_nt(rounding, selector)
    unit, scale = normed(tok[...].astype(F32))
    d_norm, in_gain_grad = normed_back(d_low, unit, scale, gains[0:1, :])
    tokens_grad[...] = (d_state[...] + d_norm).astype(BF16)

    wide = jnp.zeros((LANES, width), F32)
    vectors = [in_gain_grad] + [gain_grads[i : i + 1, :] for i in range(1, 4)]
    for which, vector in enumerate(vectors):
        wide = jnp.where(gain_mask(which * per, per, LANES, width), vector, wide)
    narrow = jnp.zeros((LANES, head), F32)
    for which, vector in enumerate((query_gain_grad, key_gain_grad)):
        mask = gain_mask(4 * per + which * per_head, per_head, LANES, head)
        narrow = jnp.where(mask, vector, narrow)
    wide, narrow = wide.astype(BF16), narrow.astype(BF16)
    attn_low = (unit * gains[0:1, :]).astype(BF16)
    stride = chunk + ODD
    for row in range(per * tiles + 1, chunk):
        loose[pl.ds(row, chips, stride=stride), :] = jnp.zeros((chips, LANES), F32)
    for target, selector, parity in ((keep, selectors[0], core), (send, selectors[1], 1 - core)):
        extra = dot(wide, pick_chip(width, chips, per, parity)) + dot(
            narrow, pick_chip(head, chips, per_head, parity)
        )
        loose[pl.ds(per * tiles, chips, stride=stride), :] = jnp.transpose(extra)
        block = dot_tn(dot(attn_low, selector).astype(BF16), low[...])
        for row in range(per):
            for tile in range(tiles):
                loose[pl.ds(row * tiles + tile, chips, stride=stride), :] = block[
                    row * chips : (row + 1) * chips, tile * LANES : (tile + 1) * LANES
                ]
        for chip in range(chips):
            target[chip * chunk : (chip + 1) * chunk, :] = loose_chunk(loose, chip, chunk).astype(BF16)


def on_device(
    tokens,
    out_grad,
    seq_start,
    seq_len,
    w_query,
    w_key_value,
    w_output,
    w_gate_up,
    w_down,
    norm_attn_in,
    norm_attn_out,
    norm_mlp_in,
    norm_mlp_out,
    norm_query,
    norm_key,
):
    size = lax.axis_size("fsdp")
    chips = size // 2
    me = lax.axis_index("fsdp")
    core = me % 2
    core_arg = core.astype(jnp.int32).reshape(1)
    tok_rows, width = tokens.shape
    shard = w_query.shape[0]
    q_cols, kv_cols = w_query.shape[1], w_key_value.shape[1]
    qkv_cols = q_cols + kv_cols
    gu_cols, ff = w_gate_up.shape[1], w_down.shape[0] * size
    down_rows = w_down.shape[0]
    head = kv_cols // 2
    hshard = norm_query.shape[0]

    mlp_full = lax.all_gather(
        jnp.concatenate(
            [
                jnp.pad(w_gate_up, ((0, SLOTS - shard), (0, 0))),
                w_down[:SLOTS],
                w_down[SLOTS:],
                w_output,
            ],
            axis=1,
        ),
        "fsdp",
        axis=0,
        tiled=True,
    )

    tiles = qkv_cols // LANES
    chunk = 64
    gain_row = jnp.zeros((1, LANES), BF16)
    gain_count = 0
    for part in (norm_attn_in, norm_attn_out, norm_mlp_in, norm_mlp_out, norm_query, norm_key):
        wide = part.shape[0]
        gain_row = gain_row + jnp.pad(part[None], ((0, 0), (gain_count, LANES - gain_count - wide)))
        gain_count += wide
    pack = jnp.concatenate(
        [
            jnp.concatenate([w_query, w_key_value], axis=1).reshape(shard * tiles, LANES),
            jnp.pad(gain_row, ((0, chunk - shard * tiles - 1), (0, 0))),
        ],
        axis=0,
    )
    own = spread(pack).reshape(chips * chunk, LANES)
    peer = swap_cores(own)

    key_reach = (WINDOW + tok_rows - 2) // tok_rows
    first_token = me * tok_rows
    q_index, q_seq, q_pos, q_live = token_layout(seq_start, seq_len, first_token, tok_rows)
    k_index, k_seq, k_pos, k_live = token_layout(
        seq_start, seq_len, first_token - key_reach * tok_rows, (key_reach + 1) * tok_rows
    )
    live = q_live.astype(F32)[:, None]
    q_seq, k_seq = q_seq[:, None], k_seq[None, :]
    inv_freq = theta_base ** (-2.0 * jnp.arange(head // 2, dtype=F32) / head)
    angles = q_pos.astype(F32)[:, None] * inv_freq[None, :]
    cos_vals, sin_vals = jnp.cos(angles), jnp.sin(angles)

    raw, query_low, own_kv, gains, head_gains, attn_weights = call(
        before_attention,
        (
            shape((tok_rows, qkv_cols), F32),
            shape((tok_rows, q_cols), BF16),
            shape((tok_rows, kv_cols), BF16),
            shape((8, width), F32),
            shape((8, head), F32),
            shape((2, chips * shard, qkv_cols), BF16),
        ),
        (core_arg, tokens, own, peer, cos_vals, sin_vals),
        scratch=(pltpu.VMEM((chips * (chunk + ODD), LANES), F32),),
        specs=[SCALAR] + [WHOLE] * 5,
    )
    kv_near = shifted(own_kv, "fsdp", 1)
    kv_far = shifted(own_kv, "fsdp", 2)
    heads_low, log_total = call(
        attention,
        (shape((tok_rows, q_cols), BF16), shape((tok_rows, LANES), F32)),
        (query_low, kv_far, kv_near, own_kv, q_seq, k_seq),
        specs=[WHOLE] * 6,
        flops=20e9,
    )

    tile = 512
    blocks, strips = 8, chips // 8
    down_at = shard * gu_cols // LANES
    out_at = down_at + down_rows * (width // LANES)
    chunk_rows = out_at + 6 * SLOTS
    chunk_shape = (blocks, strips, chunk_rows, LANES)
    mixed, d_state, d_heads, gain_grads, low_own, d_gate_up, own_down, own_out, send = call(
        feed_forward,
        (
            shape((tok_rows, width), BF16),
            shape((tok_rows, width), F32),
            shape((tok_rows, q_cols), BF16),
            shape((8, width), F32),
            shape((tok_rows, width // 2), BF16),
            shape((tok_rows, gu_cols), BF16),
            shape((blocks, strips, out_at - down_at, LANES), BF16),
            shape((blocks, strips, 6 * SLOTS, LANES), BF16),
            shape(chunk_shape, BF16),
        ),
        (core_arg, tokens, out_grad, live, gains, heads_low, mlp_full),
        scratch=(
            pltpu.VMEM((gu_cols // tile, size * SLOTS, tile), BF16),
            pltpu.VMEM((size * SLOTS, 3 * width), BF16),
            pltpu.VMEM((ff, width), BF16),
            pltpu.VMEM((tok_rows, ff), F32),
            pltpu.VMEM((tok_rows, ff), F32),
            pltpu.VMEM((tok_rows, ff), BF16),
            pltpu.VMEM((tok_rows, width), F32),
            pltpu.VMEM((tok_rows, width), F32),
            pltpu.VMEM((tok_rows, width), F32),
            pltpu.VMEM((tok_rows, size * SLOTS), F32),
            pltpu.VMEM((tok_rows, size * SLOTS), BF16),
            pltpu.VMEM((tok_rows, width), BF16),
            pltpu.VMEM((width // 2, tok_rows), BF16),
            pltpu.VMEM((tok_rows, width), BF16),
            pltpu.VMEM((chips * (down_at + ODD), LANES), F32),
            pltpu.VMEM((blocks, strips, 2, SLOTS, width), F32),
            pltpu.VMEM((tile // (2 * down_rows) // strips, strips, 2, down_rows, width), BF16),
            pltpu.VMEM((tok_rows, gu_cols), BF16),
            pltpu.VMEM((blocks, strips, out_at - down_at, LANES), BF16),
            pltpu.VMEM((blocks, strips, 6 * SLOTS, LANES), BF16),
            pltpu.VMEM(chunk_shape, BF16),
            pltpu.SemaphoreType.DMA((gu_cols // tile,)),
            pltpu.SemaphoreType.DMA((2,)),
            pltpu.SemaphoreType.DMA((5,)),
        ),
        specs=[SCALAR] + [WHOLE] * 5 + [AWAY],
        out_specs=(WHOLE,) * 5 + (AWAY,) * 4,
        flops=12e9,
    )
    arrived = swap_cores(send)

    d_query, d_own, d_near, d_far = call(
        attention_back,
        (
            shape((tok_rows, q_cols), F32),
            shape((tok_rows, kv_cols), F32),
            shape((tok_rows, kv_cols), BF16),
            shape((tok_rows, kv_cols), BF16),
        ),
        (query_low, kv_far, kv_near, own_kv, d_heads, log_total, q_seq, k_seq),
        scratch=(
            pltpu.VMEM(((key_reach + 1) * tok_rows, head), F32),
            pltpu.VMEM(((key_reach + 1) * tok_rows, head), F32),
        ),
        specs=[WHOLE] * 8,
        flops=20e9,
    )
    near = shifted(d_near, "fsdp", -1)
    far = shifted(d_far, "fsdp", -2)
    arrived, far_started = lax.optimization_barrier((arrived, d_far))
    both_mlp = call(
        own_gradients,
        shape(chunk_shape, BF16),
        (d_gate_up, low_own, own_down, own_out, arrived),
        scratch=(
            pltpu.VMEM(chunk_shape, BF16),
            pltpu.VMEM(chunk_shape, BF16),
            pltpu.VMEM((width // 2, tok_rows), BF16),
            pltpu.VMEM((chips * (down_at + ODD), LANES), F32),
            pltpu.SemaphoreType.DMA,
            pltpu.SemaphoreType.DMA((blocks,)),
        ),
        specs=[WHOLE] * 4 + [AWAY],
        out_specs=AWAY,
        flops=12e9,
    )
    both_mlp, near, far = lax.optimization_barrier((both_mlp, near, far))
    mlp_parts = exchange(both_mlp.reshape(chips, chunk_rows, LANES))
    tokens_grad, keep, send = call(
        after_attention,
        (
            shape((tok_rows, width), BF16),
            shape((chips * chunk, LANES), BF16),
            shape((chips * chunk, LANES), BF16),
        ),
        (
            core_arg, raw, d_query, d_own, near, far, attn_weights, tokens, gains,
            head_gains, cos_vals, sin_vals, d_state, gain_grads,
        ),
        scratch=(
            pltpu.VMEM((tok_rows, qkv_cols), BF16),
            pltpu.VMEM((chips * (chunk + ODD), LANES), F32),
        ),
        specs=[SCALAR] + [WHOLE] * 13,
        flops=20e9,
    )
    both = (keep.astype(F32) + swap_cores(send).astype(F32)).astype(BF16)
    both, mlp_parts = lax.optimization_barrier((both, mlp_parts))
    share_attn = jnp.sum(exchange(both.reshape(chips, chunk, LANES)).astype(F32), axis=0)
    share_qkv = share_attn[: shard * tiles].reshape(shard, tiles * LANES)
    share_gains = share_attn[shard * tiles, :gain_count]

    share_mlp = jnp.sum(mlp_parts.astype(F32), axis=0)
    share_gate_up = share_mlp[:down_at].reshape(shard, gu_cols)
    share_down = (
        share_mlp[down_at:out_at]
        .reshape(width // LANES, down_rows, LANES)
        .transpose(1, 0, 2)
        .reshape(down_rows, width)
    )
    share_output = (
        share_mlp[out_at : out_at + SLOTS * (width // LANES)]
        .reshape(width // LANES, SLOTS, LANES)
        .transpose(1, 0, 2)
        .reshape(SLOTS, width)
    )
    return (
        mixed,
        tokens_grad,
        share_qkv[:, :q_cols],
        share_qkv[:, q_cols:],
        share_output,
        share_gate_up,
        share_down,
        share_gains[:shard],
        share_gains[shard : 2 * shard],
        share_gains[2 * shard : 3 * shard],
        share_gains[3 * shard : 4 * shard],
        share_gains[4 * shard : 4 * shard + hshard],
        share_gains[4 * shard + hshard :],
    )


def solution(mesh):
    placed = (
        P("fsdp", None),
        P("fsdp", None),
        P(),
        P(),
        P("fsdp", None),
        P("fsdp", None),
        P("fsdp", None),
        P("fsdp", None),
        P("fsdp", None),
        P("fsdp"),
        P("fsdp"),
        P("fsdp"),
        P("fsdp"),
        P("fsdp"),
        P("fsdp"),
    )
    return jax.shard_map(
        on_device,
        mesh=mesh,
        in_specs=placed,
        out_specs=(
            P("fsdp", None),
            P("fsdp", None),
            P("fsdp", None),
            P("fsdp", None),
            P("fsdp", None),
            P("fsdp", None),
            P("fsdp", None),
            P("fsdp"),
            P("fsdp"),
            P("fsdp"),
            P("fsdp"),
            P("fsdp"),
            P("fsdp"),
        ),
        check_vma=False,
    )
```

```python
import jax
import jax.numpy as jnp
from jax import lax
from jax.experimental import pallas as pl
from jax.experimental.pallas import tpu as pltpu
from jax.sharding import PartitionSpec as P

WINDOW = 512


epsilon = 1e-06
theta_base = 10000.0
query_scale = 0.0625


def shifted(block, axis, distance):
    devices = range(lax.axis_size(axis))
    route = [(i - distance, i) for i in devices if i - distance in devices]
    return lax.ppermute(block, axis, route)


def token_layout(seq_start, seq_len, first_token, token_count):
    indices = first_token + jnp.arange(token_count, dtype=jnp.int32)
    offsets = indices[:, None] - seq_start[None, :]
    inside = (offsets >= 0) & (offsets < seq_len[None, :])
    live_mask = jnp.any(inside, axis=1)
    seq_numbers = jnp.arange(seq_start.shape[0], dtype=jnp.int32)
    seq_id = jnp.sum(jnp.where(inside, seq_numbers[None, :], 0), axis=1)
    seq_id = jnp.where(live_mask, seq_id, -1)
    positions = jnp.sum(jnp.where(inside, offsets, 0), axis=1)
    return (indices, seq_id, positions, live_mask)


BF16 = jnp.bfloat16
F32 = jnp.float32
SLOTS = 8
MASKED = -1e30
ODD = 1
VMEM_BYTES = 56 * 1024 * 1024
LANES = 128


def same_core_groups(size):
    return [[2 * chip + core for chip in range(size // 2)] for core in range(2)]


def swap_cores(block):
    size = lax.axis_size("fsdp")
    return lax.ppermute(block, "fsdp", [(i, i ^ 1) for i in range(size)])


def exchange(blocks):
    return lax.all_to_all(
        blocks,
        "fsdp",
        split_axis=0,
        concat_axis=0,
        tiled=True,
        axis_index_groups=same_core_groups(lax.axis_size("fsdp")),
    )


def spread(block):
    chips = lax.axis_size("fsdp") // 2
    return exchange(jnp.broadcast_to(block[None], (chips,) + block.shape))


def call(kernel, outs, ins, scratch=(), specs=None, flops=4e9, out_specs=None, vmem=VMEM_BYTES):
    return pl.pallas_call(
        kernel,
        out_shape=outs,
        in_specs=specs,
        **({} if out_specs is None else {"out_specs": out_specs}),
        scratch_shapes=list(scratch),
        compiler_params=pltpu.CompilerParams(vmem_limit_bytes=vmem),
        cost_estimate=pl.CostEstimate(
            flops=int(flops), bytes_accessed=8_000_000, transcendentals=0
        ),
    )(*ins)


SCALAR = pl.BlockSpec(memory_space=pltpu.SMEM)
WHOLE = pl.BlockSpec(memory_space=pltpu.VMEM)
AWAY = pl.BlockSpec(memory_space=pl.ANY)


def shape(dims, kind):
    return jax.ShapeDtypeStruct(dims, kind)


def dot(left, right):
    return jnp.dot(left, right, preferred_element_type=F32)


def dot_nt(left, right):
    return lax.dot_general(left, right, (((1,), (1,)), ((), ())), preferred_element_type=F32)


def dot_tn(left, right):
    return lax.dot_general(left, right, (((0,), (0,)), ((), ())), preferred_element_type=F32)


def normed(values):
    scale = lax.rsqrt(jnp.mean(values * values, axis=-1, keepdims=True) + epsilon)
    return values * scale, scale


def normed_back(cot, unit, scale, gain):
    weighted = cot * gain
    inner = jnp.mean(weighted * unit, axis=-1, keepdims=True)
    return scale * (weighted - unit * inner), jnp.sum(cot * unit, axis=0, keepdims=True)


def ones_where(mask):
    return jnp.where(mask, 1.0, 0.0).astype(BF16)


def pick_flat(rows, count, per):
    place = lax.broadcasted_iota(jnp.int32, (1, count), 1)
    device, slot = lax.shift_right_logical(place, 3), place & (SLOTS - 1)
    source = jnp.where(slot < per, device * per + slot, -1)
    return ones_where(lax.broadcasted_iota(jnp.int32, (rows, count), 0) == source)


def pick_core(rows, chips, per, core):
    place = lax.broadcasted_iota(jnp.int32, (1, chips * per), 1)
    row, chip = lax.div(place, chips), lax.rem(place, chips)
    source = (2 * chip + core) * per + row
    return ones_where(lax.broadcasted_iota(jnp.int32, (rows, chips * per), 0) == source)


def pick_chip(rows, chips, per, core):
    low = (2 * lax.broadcasted_iota(jnp.int32, (1, chips), 1) + core) * per
    natural = lax.broadcasted_iota(jnp.int32, (rows, chips), 0)
    return ones_where((natural >= low) & (natural < low + per))


def gain_mask(first, per, rows, columns):
    row = lax.broadcasted_iota(jnp.int32, (rows, columns), 0)
    column = lax.broadcasted_iota(jnp.int32, (rows, columns), 1)
    return row == first + lax.rem(column, per)


def turned(values, cos, sin):
    half = values.shape[-1] // 2
    first, second = values[:, :half], values[:, half:]
    return jnp.concatenate([first * cos - second * sin, second * cos + first * sin], axis=1)


def before_attention(
    core_ref, tok, own, peer, cos, sin, raw, query_low, own_kv, gains, head_gains, weights, loose
):
    core = core_ref[0]
    width = tok.shape[1]
    kv_cols = own_kv.shape[1]
    head = kv_cols // 2
    q_cols = query_low.shape[1]
    columns = q_cols + kv_cols
    tiles = columns // LANES
    per, per_head = width // LANES, head // LANES
    chips = weights.shape[1] // per
    chunk = own.shape[0] // chips
    wide = jnp.zeros((width, LANES), F32)
    narrow = jnp.zeros((head, LANES), F32)
    stride = chunk + ODD
    for which, (block, parity) in enumerate(((own, core), (peer, 1 - core))):
        for chip in range(chips):
            loose[chip * stride : chip * stride + chunk, :] = block[
                chip * chunk : (chip + 1) * chunk, :
            ].astype(F32)
        for row in range(per):
            for tile in range(tiles):
                weights[
                    which, row * chips : (row + 1) * chips, tile * LANES : (tile + 1) * LANES
                ] = loose[pl.ds(row * tiles + tile, chips, stride=stride), :].astype(BF16)
        found = loose[pl.ds(per * tiles, chips, stride=stride), :].astype(BF16)
        wide += dot(pick_chip(width, chips, per, parity), found)
        narrow += dot(pick_chip(head, chips, per_head, parity), found)
    wide, narrow = jnp.transpose(wide)[:32], jnp.transpose(narrow)[:32]
    for which in range(4):
        mask = gain_mask(which * per, per, 32, width)
        gains[which : which + 1, :] = jnp.sum(jnp.where(mask, wide, 0.0), 0, keepdims=True)
    for which in range(2):
        mask = gain_mask(4 * per + which * per_head, per_head, 32, head)
        head_gains[which : which + 1, :] = jnp.sum(jnp.where(mask, narrow, 0.0), 0, keepdims=True)
    unit, _ = normed(tok[...].astype(F32))
    low = (unit * gains[0:1, :]).astype(BF16)
    raw[...] = dot(dot(low, pick_core(width, chips, per, core)).astype(BF16), weights[0]) + dot(
        dot(low, pick_core(width, chips, per, 1 - core)).astype(BF16), weights[1]
    )
    for index in range(q_cols // head):
        span = slice(index * head, (index + 1) * head)
        unit, _ = normed(raw[:, span])
        query_low[:, span] = turned(unit * head_gains[0:1, :], cos[...], sin[...]).astype(BF16)
    unit, _ = normed(raw[:, q_cols : q_cols + head])
    own_kv[:, :head] = turned(unit * head_gains[1:2, :], cos[...], sin[...]).astype(BF16)
    own_kv[:, head:] = raw[:, q_cols + head :].astype(BF16)


def visible(q_seq, k_seq):
    queries, keys = q_seq.shape[0], k_seq.shape[1]
    row = lax.broadcasted_iota(jnp.int32, (queries, keys), 0)
    column = lax.broadcasted_iota(jnp.int32, (queries, keys), 1)
    distance = row - column + (keys - queries)
    same = (q_seq[...] == k_seq[...]) & (q_seq[...] >= 0)
    return (same & (distance >= 0) & (distance < WINDOW)) | (distance == 0)


def attention(
    core_ref, query_low, kv_far, kv_near, kv_own, q_seq, k_seq,
    heads_low, log_total, spread_flat, spread_core,
):
    core = core_ref[0]
    width, per_core = spread_core.shape[1:]
    per = width // LANES
    spread_flat[...] = pick_flat(width, spread_flat.shape[1], per)
    for which, parity in enumerate((core, 1 - core)):
        spread_core[which] = pick_core(width, per_core // per, per, parity)
    head = kv_own.shape[1] // 2
    parts = (kv_far, kv_near, kv_own)
    keys = jnp.concatenate([part[:, :head] for part in parts], axis=0)
    values = jnp.concatenate([part[:, head:] for part in parts], axis=0)
    allowed = visible(q_seq, k_seq)
    for index in range(query_low.shape[1] // head):
        span = slice(index * head, (index + 1) * head)
        scores = dot_nt(query_low[:, span], keys) * query_scale
        scores = jnp.where(allowed, scores, MASKED)
        top = jnp.max(scores, axis=-1, keepdims=True)
        terms = jnp.exp(scores - top)
        total = jnp.sum(terms, axis=-1, keepdims=True)
        probs = (terms * (1.0 / total)).astype(BF16)
        heads_low[:, span] = dot(probs, values).astype(BF16)
        log_total[:, index : index + 1] = top + jnp.log(total)


def feed_forward(
    core_ref, tok, out_grad, live, gains, heads_low, spread_flat_in, spread_core_in, full,
    gain_grads, mixed_out, d_state_out, d_heads_out, low_own_out, d_gate_up_out, own_down_out,
    own_out_out, send_out,
    weights, rest, down, act, act_slope, hidden, proj, state, total, back, low_flat, low, turned_low,
    low_branch, loose, loose_out, turn_down, spread_flat, spread_core, mixed, d_state, d_heads,
    low_own, d_gate_up, own_down, own_out, send, weight_sem, rest_sem, out_sem,
):
    core = core_ref[0]
    tiles, tile = weights.shape[0], weights.shape[2]
    half = tiles // 2
    width = state.shape[1]
    q_cols = heads_low.shape[1]
    per = width // LANES
    blocks, strips, down_rows = send.shape[0], send.shape[1], turn_down.shape[3]
    chips = blocks * strips
    tile_chips = tile // (2 * down_rows)
    tile_rows = tile // down_rows * SLOTS
    columns_at = tiles * tile

    def weight_copy(index):
        return pltpu.make_async_copy(
            full.at[:, pl.ds(pl.multiple_of(index * tile, tile), tile)],
            weights.at[index],
            weight_sem.at[index],
        )

    def rest_copy(which, first, last):
        return pltpu.make_async_copy(
            full.at[:, columns_at + first : columns_at + last],
            rest.at[:, first:last],
            rest_sem.at[which],
        )

    out_copy = rest_copy(0, 2 * width, 3 * width)
    down_copy = rest_copy(1, 0, 2 * width)
    flat_copy = pltpu.make_async_copy(spread_flat_in, spread_flat, rest_sem.at[2])
    core_copy = pltpu.make_async_copy(spread_core_in, spread_core, rest_sem.at[3])
    out_copy.start()
    flat_copy.start()
    down_copy.start()
    for index in range(half):
        weight_copy(index).start()
        weight_copy(half + index).start()
    core_copy.start()
    leaving = []

    def leave(source, target):
        leaving.append(pltpu.make_async_copy(source, target, out_sem.at[len(leaving)]))
        leaving[-1].start()

    out_copy.wait()
    w_out = rest[:, 2 * width :]
    proj[...] = dot(heads_low[...], w_out)
    unit, _ = normed(proj[...])
    state[...] = tok[...].astype(F32) + unit * gains[1:2, :]
    unit, scale = normed(state[...])
    low[...] = (unit * gains[2:3, :]).astype(BF16)
    flat_copy.wait()
    low_flat[...] = dot(low[...], spread_flat[...]).astype(BF16)
    total[...] = jnp.zeros_like(total)
    down_copy.wait()

    def down_tile(index):
        return down[pl.ds(pl.multiple_of(index * tile, tile), tile)]

    def forward(index, carry):
        columns = pl.ds(pl.multiple_of(index * tile, tile), tile)
        stored = rest[pl.ds(pl.multiple_of(index * tile_rows, tile_rows), tile_rows), : 2 * width]
        stored = stored.astype(F32).reshape(tile_rows // SLOTS, SLOTS, 2 * width)
        down[pl.ds(pl.multiple_of(index * tile, tile), tile)] = (
            jnp.concatenate([stored[:, :, :width], stored[:, :, width:]], axis=1)
            .reshape(tile, width)
            .astype(BF16)
        )
        weight_copy(index).wait()
        weight_copy(half + index).wait()
        gate = dot(low_flat[...], weights[index])
        up = dot(low_flat[...], weights[half + index])
        square = gate * gate
        bend = jnp.tanh(gate * (0.7978845608028654 * (1.0 + 0.044715 * square)))
        rise = 0.5 * (1.0 + bend)
        gelu = gate * rise
        slope = rise + 0.5 * gate * (1.0 - bend * bend) * (
            0.7978845608028654 * (1.0 + 0.134145 * square)
        )
        act[:, columns] = gelu
        act_slope[:, columns] = up * slope
        hidden[:, columns] = (gelu * up).astype(BF16)
        total[...] += dot(hidden[:, columns], down_tile(index))
        return carry

    lax.fori_loop(0, half, forward, 0)
    core_copy.wait()
    low_own[...] = dot(low[...], spread_core[0]).astype(BF16)
    turned_low[...] = jnp.transpose(dot(low[...], spread_core[1])).astype(BF16)
    leave(low_own, low_own_out)

    branch_unit, branch_scale = normed(total[...])
    mixed[...] = ((state[...] + branch_unit * gains[3:4, :]) * live[...]).astype(BF16)
    leave(mixed, mixed_out)
    cotangent = out_grad[...].astype(F32) * live[...]
    d_branch, gain_grads[3:4, :] = normed_back(
        cotangent, branch_unit, branch_scale, gains[3:4, :]
    )
    low_branch[...] = d_branch.astype(BF16)
    back[...] = jnp.zeros_like(back)

    row_tiles = tiles * tile // LANES
    chunk = per * row_tiles

    def place(start, grad):
        place_rows(loose, dot(turned_low[...], grad), start, per, chips, row_tiles)

    down_at = chunk
    out_at = down_at + down_rows * (width // LANES)

    def backward(index, carry):
        columns = pl.ds(pl.multiple_of(index * tile, tile), tile)
        d_hidden = dot_nt(low_branch[...], down_tile(index))
        d_gate = (d_hidden * act_slope[:, columns]).astype(BF16)
        d_up = (d_hidden * act[:, columns]).astype(BF16)
        d_gate_up[:, columns] = d_gate
        d_gate_up[:, pl.ds(pl.multiple_of((half + index) * tile, tile), tile)] = d_up
        back[...] += dot_nt(d_gate, weights[index]) + dot_nt(d_up, weights[half + index])
        place(index * (tile // LANES), d_gate)
        place((half + index) * (tile // LANES), d_up)
        turn_down[...] = (
            dot_tn(hidden[:, columns], low_branch[...])
            .astype(BF16)
            .reshape(tile_chips // strips, strips, 2, down_rows, width)
        )
        tall = pl.ds(index * (tile_chips // strips), tile_chips // strips)
        for part in range(width // LANES):
            top = part * down_rows
            lanes = slice(part * LANES, (part + 1) * LANES)
            own_down[tall, :, top : top + down_rows, :] = turn_down[:, :, core, :, lanes]
            send[tall, :, down_at + top : down_at + top + down_rows, :] = turn_down[
                :, :, 1 - core, :, lanes
            ]
        return carry

    lax.fori_loop(0, half, backward, 0)
    leave(d_gate_up, d_gate_up_out)
    leave(own_down, own_down_out)

    def pack(block, carry):
        for strip in range(strips):
            send[block, strip, :chunk, :] = loose_chunk(loose, block * strips + strip, chunk).astype(
                BF16
            )
        return carry

    lax.fori_loop(0, blocks, pack, 0)
    leave(send.at[:, :, :out_at, :], send_out.at[:, :, :out_at, :])

    d_low = dot_nt(back[...].astype(BF16), spread_flat[...])
    d_norm, gain_grads[2:3, :] = normed_back(d_low, unit, scale, gains[2:3, :])
    d_state[...] = cotangent + d_norm
    leave(d_state, d_state_out)
    proj_unit, proj_scale = normed(proj[...])
    d_proj, gain_grads[1:2, :] = normed_back(d_state[...], proj_unit, proj_scale, gains[1:2, :])
    proj_low = d_proj.astype(BF16)
    loose_out[...] = dot_tn(heads_low[...], proj_low).reshape(blocks, strips, 2, SLOTS, width)
    out_tiles = width // LANES
    for target, parity, start in ((own_out, core, 0), (send, 1 - core, out_at)):
        for part in range(out_tiles // 2 + 1):
            lanes = [slice(i * LANES, (i + 1) * LANES) for i in (2 * part, 2 * part + 1)]
            pair = [
                loose_out[:, :, parity, :, lane]
                if lane.stop <= width
                else jnp.zeros((blocks, strips, SLOTS, LANES), F32)
                for lane in lanes
            ]
            top = start + 2 * part * SLOTS
            target[:, :, top : top + 2 * SLOTS, :] = jnp.concatenate(pair, axis=2).astype(BF16)
    leave(own_out, own_out_out)
    leave(send.at[:, :, out_at:, :], send_out.at[:, :, out_at:, :])
    d_heads[...] = dot_nt(proj_low, w_out).astype(BF16)
    leave(d_heads, d_heads_out)
    for copy in leaving:
        copy.wait()


def place_rows(loose, block, start, per, chips, row_tiles):
    stride = per * row_tiles + ODD
    for row in range(per):
        for part in range(block.shape[1] // LANES):
            loose[pl.ds(row * row_tiles + start + part, chips, stride=stride), :] = block[
                row * chips : (row + 1) * chips, part * LANES : (part + 1) * LANES
            ]


def loose_chunk(loose, chip, chunk):
    return loose[pl.ds(chip * (chunk + ODD), chunk), :]


def own_gradients(
    d_gate_up, low_own, own_down, own_out, arrived, both_out,
    both, other, turned_low, loose, arrived_sem, both_sem,
):
    copy = pltpu.make_async_copy(arrived, other, arrived_sem)
    copy.start()
    blocks, strips, down_size = own_down.shape[:3]
    chips = blocks * strips
    per = low_own.shape[1] // chips
    tile = 512
    steps = d_gate_up.shape[1] // tile
    row_tiles = d_gate_up.shape[1] // LANES
    chunk = per * row_tiles
    turned_low[...] = jnp.transpose(low_own[...].astype(F32)).astype(BF16)

    def place(index, carry):
        grad = d_gate_up[:, pl.ds(pl.multiple_of(index * tile, tile), tile)]
        block = dot(turned_low[...], grad)
        place_rows(loose, block, index * (tile // LANES), per, chips, row_tiles)
        return carry

    lax.fori_loop(0, steps, place, 0)
    copy.wait()

    def leave(block):
        return pltpu.make_async_copy(both.at[block], both_out.at[block], both_sem.at[block])

    def pack(block, carry):
        for strip in range(strips):
            both[block, strip, :chunk, :] = (
                loose_chunk(loose, block * strips + strip, chunk)
                + other[block, strip, :chunk, :].astype(F32)
            ).astype(BF16)
        low, high = chunk, chunk + down_size
        both[block, :, low:high, :] = (
            own_down[block].astype(F32) + other[block, :, low:high, :].astype(F32)
        ).astype(BF16)
        both[block, :, high:, :] = (
            own_out[block].astype(F32) + other[block, :, high:, :].astype(F32)
        ).astype(BF16)
        leave(block).start()
        return carry

    lax.fori_loop(0, blocks, pack, 0)
    for block in range(blocks):
        leave(block).wait()


def attention_back(
    query_low, kv_far, kv_near, kv_own, d_heads, log_total, q_seq, k_seq,
    d_query, d_own, d_near, d_far, sum_keys, sum_values,
):
    head = kv_own.shape[1] // 2
    rows = kv_own.shape[0]
    parts = (kv_far, kv_near, kv_own)
    keys = jnp.concatenate([part[:, :head] for part in parts], axis=0)
    values = jnp.concatenate([part[:, head:] for part in parts], axis=0)
    allowed = visible(q_seq, k_seq)
    for index in range(query_low.shape[1] // head):
        span = slice(index * head, (index + 1) * head)
        scores = dot_nt(query_low[:, span], keys) * query_scale
        scores = jnp.where(allowed, scores, MASKED)
        probs = jnp.exp(scores - log_total[:, index : index + 1])
        d_probs = dot_nt(d_heads[:, span], values)
        inner = jnp.sum(probs * d_probs, axis=-1, keepdims=True)
        d_scores = (probs * (d_probs - inner)).astype(BF16)
        d_query[:, span] = dot(d_scores, keys) * query_scale
        key_term = dot_tn(d_scores, query_low[:, span]) * query_scale
        value_term = dot_tn(probs.astype(BF16), d_heads[:, span])
        if index == 0:
            sum_keys[...] = key_term
            sum_values[...] = value_term
        else:
            sum_keys[...] += key_term
            sum_values[...] += value_term
    for target, start in ((d_far, 0), (d_near, rows), (d_own, 2 * rows)):
        target[:, :head] = sum_keys[start : start + rows, :].astype(target.dtype)
        target[:, head:] = sum_values[start : start + rows, :].astype(target.dtype)


def after_attention(
    core_ref, raw, d_query, d_own, near, far, weights, tok, gains, head_gains, cos, sin,
    d_state, gain_grads, tokens_grad, keep, send, low, loose,
):
    core = core_ref[0]
    width = tok.shape[1]
    q_cols, kv_cols = d_query.shape[1], d_own.shape[1]
    head = kv_cols // 2
    tiles = (q_cols + kv_cols) // LANES
    per, per_head = width // LANES, head // LANES
    chips = weights.shape[1] // per
    chunk = keep.shape[0] // chips
    cosine, minus_sine = cos[...], -sin[...]
    query_gain_grad = jnp.zeros((1, head), F32)
    for index in range(q_cols // head):
        span = slice(index * head, (index + 1) * head)
        unit, scale = normed(raw[:, span])
        cot = turned(d_query[:, span], cosine, minus_sine)
        d_raw, part = normed_back(cot, unit, scale, head_gains[0:1, :])
        query_gain_grad += part
        low[:, span] = d_raw.astype(BF16)
    d_kv = d_own[...] + near[...].astype(F32) + far[...].astype(F32)
    unit, scale = normed(raw[:, q_cols : q_cols + head])
    cot = turned(d_kv[:, :head], cosine, minus_sine)
    d_raw, key_gain_grad = normed_back(cot, unit, scale, head_gains[1:2, :])
    low[:, q_cols : q_cols + head] = d_raw.astype(BF16)
    low[:, q_cols + head :] = d_kv[:, head:].astype(BF16)

    selectors = [pick_core(width, chips, per, parity) for parity in (core, 1 - core)]
    d_low = jnp.zeros(tok.shape, F32)
    for which, selector in enumerate(selectors):
        part = dot_nt(low[...], weights[which])
        high = part.astype(BF16)
        rounding = (part - high.astype(F32)).astype(BF16)
        d_low += dot_nt(high, selector) + dot_nt(rounding, selector)
    unit, scale = normed(tok[...].astype(F32))
    d_norm, in_gain_grad = normed_back(d_low, unit, scale, gains[0:1, :])
    tokens_grad[...] = (d_state[...] + d_norm).astype(BF16)

    wide = jnp.zeros((LANES, width), F32)
    vectors = [in_gain_grad] + [gain_grads[i : i + 1, :] for i in range(1, 4)]
    for which, vector in enumerate(vectors):
        wide = jnp.where(gain_mask(which * per, per, LANES, width), vector, wide)
    narrow = jnp.zeros((LANES, head), F32)
    for which, vector in enumerate((query_gain_grad, key_gain_grad)):
        mask = gain_mask(4 * per + which * per_head, per_head, LANES, head)
        narrow = jnp.where(mask, vector, narrow)
    wide, narrow = wide.astype(BF16), narrow.astype(BF16)
    attn_low = (unit * gains[0:1, :]).astype(BF16)
    stride = chunk + ODD
    for row in range(per * tiles + 1, chunk):
        loose[pl.ds(row, chips, stride=stride), :] = jnp.zeros((chips, LANES), F32)
    for target, selector, parity in ((keep, selectors[0], core), (send, selectors[1], 1 - core)):
        extra = dot(wide, pick_chip(width, chips, per, parity)) + dot(
            narrow, pick_chip(head, chips, per_head, parity)
        )
        loose[pl.ds(per * tiles, chips, stride=stride), :] = jnp.transpose(extra)
        block = dot_tn(dot(attn_low, selector).astype(BF16), low[...])
        for row in range(per):
            for tile in range(tiles):
                loose[pl.ds(row * tiles + tile, chips, stride=stride), :] = block[
                    row * chips : (row + 1) * chips, tile * LANES : (tile + 1) * LANES
                ]
        for chip in range(chips):
            target[chip * chunk : (chip + 1) * chunk, :] = loose_chunk(loose, chip, chunk).astype(BF16)


def on_device(
    tokens,
    out_grad,
    seq_start,
    seq_len,
    w_query,
    w_key_value,
    w_output,
    w_gate_up,
    w_down,
    norm_attn_in,
    norm_attn_out,
    norm_mlp_in,
    norm_mlp_out,
    norm_query,
    norm_key,
):
    size = lax.axis_size("fsdp")
    chips = size // 2
    me = lax.axis_index("fsdp")
    core = me % 2
    core_arg = core.astype(jnp.int32).reshape(1)
    tok_rows, width = tokens.shape
    shard = w_query.shape[0]
    q_cols, kv_cols = w_query.shape[1], w_key_value.shape[1]
    qkv_cols = q_cols + kv_cols
    gu_cols, ff = w_gate_up.shape[1], w_down.shape[0] * size
    down_rows = w_down.shape[0]
    head = kv_cols // 2
    hshard = norm_query.shape[0]

    mlp_full = lax.all_gather(
        jnp.concatenate(
            [
                jnp.pad(w_gate_up, ((0, SLOTS - shard), (0, 0))),
                w_down[:SLOTS],
                w_down[SLOTS:],
                w_output,
            ],
            axis=1,
        ),
        "fsdp",
        axis=0,
        tiled=True,
    )

    tiles = qkv_cols // LANES
    chunk = 64
    gain_row = jnp.zeros((1, LANES), BF16)
    gain_count = 0
    for part in (norm_attn_in, norm_attn_out, norm_mlp_in, norm_mlp_out, norm_query, norm_key):
        wide = part.shape[0]
        gain_row = gain_row + jnp.pad(part[None], ((0, 0), (gain_count, LANES - gain_count - wide)))
        gain_count += wide
    pack = jnp.concatenate(
        [
            jnp.concatenate([w_query, w_key_value], axis=1).reshape(shard * tiles, LANES),
            jnp.pad(gain_row, ((0, chunk - shard * tiles - 1), (0, 0))),
        ],
        axis=0,
    )
    own = spread(pack).reshape(chips * chunk, LANES)
    peer = swap_cores(own)

    key_reach = (WINDOW + tok_rows - 2) // tok_rows
    first_token = me * tok_rows
    q_index, q_seq, q_pos, q_live = token_layout(seq_start, seq_len, first_token, tok_rows)
    k_index, k_seq, k_pos, k_live = token_layout(
        seq_start, seq_len, first_token - key_reach * tok_rows, (key_reach + 1) * tok_rows
    )
    live = q_live.astype(F32)[:, None]
    q_seq, k_seq = q_seq[:, None], k_seq[None, :]
    inv_freq = theta_base ** (-2.0 * jnp.arange(head // 2, dtype=F32) / head)
    angles = q_pos.astype(F32)[:, None] * inv_freq[None, :]
    cos_vals, sin_vals = jnp.cos(angles), jnp.sin(angles)

    raw, query_low, own_kv, gains, head_gains, attn_weights = call(
        before_attention,
        (
            shape((tok_rows, qkv_cols), F32),
            shape((tok_rows, q_cols), BF16),
            shape((tok_rows, kv_cols), BF16),
            shape((8, width), F32),
            shape((8, head), F32),
            shape((2, chips * shard, qkv_cols), BF16),
        ),
        (core_arg, tokens, own, peer, cos_vals, sin_vals),
        scratch=(pltpu.VMEM((chips * (chunk + ODD), LANES), F32),),
        specs=[SCALAR] + [WHOLE] * 5,
    )
    kv_near = shifted(own_kv, "fsdp", 1)
    kv_far = shifted(own_kv, "fsdp", 2)
    heads_low, log_total, spread_flat, spread_core = call(
        attention,
        (
            shape((tok_rows, q_cols), BF16),
            shape((tok_rows, LANES), F32),
            shape((width, size * SLOTS), BF16),
            shape((2, width, width // 2), BF16),
        ),
        (core_arg, query_low, kv_far, kv_near, own_kv, q_seq, k_seq),
        specs=[SCALAR] + [WHOLE] * 6,
        flops=20e9,
    )

    tile = 512
    blocks, strips = 8, chips // 8
    down_at = shard * gu_cols // LANES
    out_at = down_at + down_rows * (width // LANES)
    chunk_rows = out_at + 6 * SLOTS
    chunk_shape = (blocks, strips, chunk_rows, LANES)
    gain_grads, mixed, d_state, d_heads, low_own, d_gate_up, own_down, own_out, send = call(
        feed_forward,
        (
            shape((8, width), F32),
            shape((tok_rows, width), BF16),
            shape((tok_rows, width), F32),
            shape((tok_rows, q_cols), BF16),
            shape((tok_rows, width // 2), BF16),
            shape((tok_rows, gu_cols), BF16),
            shape((blocks, strips, out_at - down_at, LANES), BF16),
            shape((blocks, strips, 6 * SLOTS, LANES), BF16),
            shape(chunk_shape, BF16),
        ),
        (
            core_arg, tokens, out_grad, live, gains, heads_low, spread_flat, spread_core, mlp_full,
        ),
        scratch=(
            pltpu.VMEM((gu_cols // tile, size * SLOTS, tile), BF16),
            pltpu.VMEM((size * SLOTS, 3 * width), BF16),
            pltpu.VMEM((ff, width), BF16),
            pltpu.VMEM((tok_rows, ff), F32),
            pltpu.VMEM((tok_rows, ff), F32),
            pltpu.VMEM((tok_rows, ff), BF16),
            pltpu.VMEM((tok_rows, width), F32),
            pltpu.VMEM((tok_rows, width), F32),
            pltpu.VMEM((tok_rows, width), F32),
            pltpu.VMEM((tok_rows, size * SLOTS), F32),
            pltpu.VMEM((tok_rows, size * SLOTS), BF16),
            pltpu.VMEM((tok_rows, width), BF16),
            pltpu.VMEM((width // 2, tok_rows), BF16),
            pltpu.VMEM((tok_rows, width), BF16),
            pltpu.VMEM((chips * (down_at + ODD), LANES), F32),
            pltpu.VMEM((blocks, strips, 2, SLOTS, width), F32),
            pltpu.VMEM((tile // (2 * down_rows) // strips, strips, 2, down_rows, width), BF16),
            pltpu.VMEM((width, size * SLOTS), BF16),
            pltpu.VMEM((2, width, width // 2), BF16),
            pltpu.VMEM((tok_rows, width), BF16),
            pltpu.VMEM((tok_rows, width), F32),
            pltpu.VMEM((tok_rows, q_cols), BF16),
            pltpu.VMEM((tok_rows, width // 2), BF16),
            pltpu.VMEM((tok_rows, gu_cols), BF16),
            pltpu.VMEM((blocks, strips, out_at - down_at, LANES), BF16),
            pltpu.VMEM((blocks, strips, 6 * SLOTS, LANES), BF16),
            pltpu.VMEM(chunk_shape, BF16),
            pltpu.SemaphoreType.DMA((gu_cols // tile,)),
            pltpu.SemaphoreType.DMA((4,)),
            pltpu.SemaphoreType.DMA((9,)),
        ),
        specs=[SCALAR] + [WHOLE] * 5 + [AWAY] * 3,
        out_specs=(WHOLE,) + (AWAY,) * 8,
        flops=12e9,
    )
    arrived = swap_cores(send)

    d_query, d_own, d_near, d_far = call(
        attention_back,
        (
            shape((tok_rows, q_cols), F32),
            shape((tok_rows, kv_cols), F32),
            shape((tok_rows, kv_cols), BF16),
            shape((tok_rows, kv_cols), BF16),
        ),
        (query_low, kv_far, kv_near, own_kv, d_heads, log_total, q_seq, k_seq),
        scratch=(
            pltpu.VMEM(((key_reach + 1) * tok_rows, head), F32),
            pltpu.VMEM(((key_reach + 1) * tok_rows, head), F32),
        ),
        specs=[WHOLE] * 8,
        flops=20e9,
    )
    near = shifted(d_near, "fsdp", -1)
    far = shifted(d_far, "fsdp", -2)
    arrived, far_started = lax.optimization_barrier((arrived, d_far))
    both_mlp = call(
        own_gradients,
        shape(chunk_shape, BF16),
        (d_gate_up, low_own, own_down, own_out, arrived),
        scratch=(
            pltpu.VMEM(chunk_shape, BF16),
            pltpu.VMEM(chunk_shape, BF16),
            pltpu.VMEM((width // 2, tok_rows), BF16),
            pltpu.VMEM((chips * (down_at + ODD), LANES), F32),
            pltpu.SemaphoreType.DMA,
            pltpu.SemaphoreType.DMA((blocks,)),
        ),
        specs=[WHOLE] * 4 + [AWAY],
        out_specs=AWAY,
        flops=12e9,
        vmem=62 * 1024 * 1024,
    )
    both_mlp, near, far = lax.optimization_barrier((both_mlp, near, far))
    mlp_parts = exchange(both_mlp.reshape(chips, chunk_rows, LANES))
    tokens_grad, keep, send = call(
        after_attention,
        (
            shape((tok_rows, width), BF16),
            shape((chips * chunk, LANES), BF16),
            shape((chips * chunk, LANES), BF16),
        ),
        (
            core_arg, raw, d_query, d_own, near, far, attn_weights, tokens, gains,
            head_gains, cos_vals, sin_vals, d_state, gain_grads,
        ),
        scratch=(
            pltpu.VMEM((tok_rows, qkv_cols), BF16),
            pltpu.VMEM((chips * (chunk + ODD), LANES), F32),
        ),
        specs=[SCALAR] + [WHOLE] * 13,
        flops=20e9,
    )
    both = (keep.astype(F32) + swap_cores(send).astype(F32)).astype(BF16)
    both, mlp_parts = lax.optimization_barrier((both, mlp_parts))
    share_attn = jnp.sum(exchange(both.reshape(chips, chunk, LANES)).astype(F32), axis=0)
    share_qkv = share_attn[: shard * tiles].reshape(shard, tiles * LANES)
    share_gains = share_attn[shard * tiles, :gain_count]

    share_mlp = jnp.sum(mlp_parts.astype(F32), axis=0)
    share_gate_up = share_mlp[:down_at].reshape(shard, gu_cols)
    share_down = (
        share_mlp[down_at:out_at]
        .reshape(width // LANES, down_rows, LANES)
        .transpose(1, 0, 2)
        .reshape(down_rows, width)
    )
    share_output = (
        share_mlp[out_at : out_at + SLOTS * (width // LANES)]
        .reshape(width // LANES, SLOTS, LANES)
        .transpose(1, 0, 2)
        .reshape(SLOTS, width)
    )
    return (
        mixed,
        tokens_grad,
        share_qkv[:, :q_cols],
        share_qkv[:, q_cols:],
        share_output,
        share_gate_up,
        share_down,
        share_gains[:shard],
        share_gains[shard : 2 * shard],
        share_gains[2 * shard : 3 * shard],
        share_gains[3 * shard : 4 * shard],
        share_gains[4 * shard : 4 * shard + hshard],
        share_gains[4 * shard + hshard :],
    )


def solution(mesh):
    placed = (
        P("fsdp", None),
        P("fsdp", None),
        P(),
        P(),
        P("fsdp", None),
        P("fsdp", None),
        P("fsdp", None),
        P("fsdp", None),
        P("fsdp", None),
        P("fsdp"),
        P("fsdp"),
        P("fsdp"),
        P("fsdp"),
        P("fsdp"),
        P("fsdp"),
    )
    return jax.shard_map(
        on_device,
        mesh=mesh,
        in_specs=placed,
        out_specs=(
            P("fsdp", None),
            P("fsdp", None),
            P("fsdp", None),
            P("fsdp", None),
            P("fsdp", None),
            P("fsdp", None),
            P("fsdp", None),
            P("fsdp"),
            P("fsdp"),
            P("fsdp"),
            P("fsdp"),
            P("fsdp"),
            P("fsdp"),
        ),
        check_vma=False,
    )
```

```python
import jax
import jax.numpy as jnp
from jax import lax
from jax.experimental import pallas as pl
from jax.experimental.pallas import tpu as pltpu
from jax.sharding import PartitionSpec as P

WINDOW = 512


epsilon = 1e-06
theta_base = 10000.0
query_scale = 0.0625


def shifted(block, axis, distance):
    devices = range(lax.axis_size(axis))
    route = [(i - distance, i) for i in devices if i - distance in devices]
    return lax.ppermute(block, axis, route)


def token_layout(seq_start, seq_len, first_token, token_count):
    indices = first_token + jnp.arange(token_count, dtype=jnp.int32)
    offsets = indices[:, None] - seq_start[None, :]
    inside = (offsets >= 0) & (offsets < seq_len[None, :])
    live_mask = jnp.any(inside, axis=1)
    seq_numbers = jnp.arange(seq_start.shape[0], dtype=jnp.int32)
    seq_id = jnp.sum(jnp.where(inside, seq_numbers[None, :], 0), axis=1)
    seq_id = jnp.where(live_mask, seq_id, -1)
    positions = jnp.sum(jnp.where(inside, offsets, 0), axis=1)
    return (indices, seq_id, positions, live_mask)


BF16 = jnp.bfloat16
F32 = jnp.float32
SLOTS = 8
MASKED = -1e30
ODD = 1
VMEM_BYTES = 56 * 1024 * 1024
LANES = 128


def same_core_groups(size):
    return [[2 * chip + core for chip in range(size // 2)] for core in range(2)]


def swap_cores(block):
    size = lax.axis_size("fsdp")
    return lax.ppermute(block, "fsdp", [(i, i ^ 1) for i in range(size)])


def exchange(blocks):
    return lax.all_to_all(
        blocks,
        "fsdp",
        split_axis=0,
        concat_axis=0,
        tiled=True,
        axis_index_groups=same_core_groups(lax.axis_size("fsdp")),
    )


def spread(block):
    chips = lax.axis_size("fsdp") // 2
    return exchange(jnp.broadcast_to(block[None], (chips,) + block.shape))


def call(kernel, outs, ins, scratch=(), specs=None, flops=4e9, out_specs=None, vmem=VMEM_BYTES):
    return pl.pallas_call(
        kernel,
        out_shape=outs,
        in_specs=specs,
        **({} if out_specs is None else {"out_specs": out_specs}),
        scratch_shapes=list(scratch),
        compiler_params=pltpu.CompilerParams(vmem_limit_bytes=vmem),
        cost_estimate=pl.CostEstimate(
            flops=int(flops), bytes_accessed=8_000_000, transcendentals=0
        ),
    )(*ins)


SCALAR = pl.BlockSpec(memory_space=pltpu.SMEM)
WHOLE = pl.BlockSpec(memory_space=pltpu.VMEM)
AWAY = pl.BlockSpec(memory_space=pl.ANY)


def shape(dims, kind):
    return jax.ShapeDtypeStruct(dims, kind)


def dot(left, right):
    return jnp.dot(left, right, preferred_element_type=F32)


def dot_nt(left, right):
    return lax.dot_general(left, right, (((1,), (1,)), ((), ())), preferred_element_type=F32)


def dot_tn(left, right):
    return lax.dot_general(left, right, (((0,), (0,)), ((), ())), preferred_element_type=F32)


def normed(values):
    scale = lax.rsqrt(jnp.mean(values * values, axis=-1, keepdims=True) + epsilon)
    return values * scale, scale


def normed_back(cot, unit, scale, gain):
    weighted = cot * gain
    inner = jnp.mean(weighted * unit, axis=-1, keepdims=True)
    return scale * (weighted - unit * inner), jnp.sum(cot * unit, axis=0, keepdims=True)


def ones_where(mask):
    return jnp.where(mask, 1.0, 0.0).astype(BF16)


def pick_flat(rows, count, per):
    place = lax.broadcasted_iota(jnp.int32, (1, count), 1)
    device, slot = lax.shift_right_logical(place, 3), place & (SLOTS - 1)
    source = jnp.where(slot < per, device * per + slot, -1)
    return ones_where(lax.broadcasted_iota(jnp.int32, (rows, count), 0) == source)


def pick_core(rows, chips, per, core):
    place = lax.broadcasted_iota(jnp.int32, (1, chips * per), 1)
    row, chip = lax.div(place, chips), lax.rem(place, chips)
    source = (2 * chip + core) * per + row
    return ones_where(lax.broadcasted_iota(jnp.int32, (rows, chips * per), 0) == source)


def pick_chip(rows, chips, per, core):
    low = (2 * lax.broadcasted_iota(jnp.int32, (1, chips), 1) + core) * per
    natural = lax.broadcasted_iota(jnp.int32, (rows, chips), 0)
    return ones_where((natural >= low) & (natural < low + per))


def gain_mask(first, per, rows, columns):
    row = lax.broadcasted_iota(jnp.int32, (rows, columns), 0)
    column = lax.broadcasted_iota(jnp.int32, (rows, columns), 1)
    return row == first + lax.rem(column, per)


def turned(values, cos, sin):
    half = values.shape[-1] // 2
    first, second = values[:, :half], values[:, half:]
    return jnp.concatenate([first * cos - second * sin, second * cos + first * sin], axis=1)


def before_attention(
    core_ref, tok, own, peer, cos, sin, raw, query_low, own_kv, gains, head_gains, weights, loose
):
    core = core_ref[0]
    width = tok.shape[1]
    kv_cols = own_kv.shape[1]
    head = kv_cols // 2
    q_cols = query_low.shape[1]
    columns = q_cols + kv_cols
    tiles = columns // LANES
    per, per_head = width // LANES, head // LANES
    chips = weights.shape[1] // per
    chunk = own.shape[0] // chips
    wide = jnp.zeros((width, LANES), F32)
    narrow = jnp.zeros((head, LANES), F32)
    stride = chunk + ODD
    for which, (block, parity) in enumerate(((own, core), (peer, 1 - core))):
        for chip in range(chips):
            loose[chip * stride : chip * stride + chunk, :] = block[
                chip * chunk : (chip + 1) * chunk, :
            ].astype(F32)
        for row in range(per):
            for tile in range(tiles):
                weights[
                    which, row * chips : (row + 1) * chips, tile * LANES : (tile + 1) * LANES
                ] = loose[pl.ds(row * tiles + tile, chips, stride=stride), :].astype(BF16)
        found = loose[pl.ds(per * tiles, chips, stride=stride), :].astype(BF16)
        wide += dot(pick_chip(width, chips, per, parity), found)
        narrow += dot(pick_chip(head, chips, per_head, parity), found)
    wide, narrow = jnp.transpose(wide)[:32], jnp.transpose(narrow)[:32]
    for which in range(4):
        mask = gain_mask(which * per, per, 32, width)
        gains[which : which + 1, :] = jnp.sum(jnp.where(mask, wide, 0.0), 0, keepdims=True)
    for which in range(2):
        mask = gain_mask(4 * per + which * per_head, per_head, 32, head)
        head_gains[which : which + 1, :] = jnp.sum(jnp.where(mask, narrow, 0.0), 0, keepdims=True)
    unit, _ = normed(tok[...].astype(F32))
    low = (unit * gains[0:1, :]).astype(BF16)
    raw[...] = dot(dot(low, pick_core(width, chips, per, core)).astype(BF16), weights[0]) + dot(
        dot(low, pick_core(width, chips, per, 1 - core)).astype(BF16), weights[1]
    )
    for index in range(q_cols // head):
        span = slice(index * head, (index + 1) * head)
        unit, _ = normed(raw[:, span])
        query_low[:, span] = turned(unit * head_gains[0:1, :], cos[...], sin[...]).astype(BF16)
    unit, _ = normed(raw[:, q_cols : q_cols + head])
    own_kv[:, :head] = turned(unit * head_gains[1:2, :], cos[...], sin[...]).astype(BF16)
    own_kv[:, head:] = raw[:, q_cols + head :].astype(BF16)


def visible(q_seq, k_seq):
    queries, keys = q_seq.shape[0], k_seq.shape[1]
    row = lax.broadcasted_iota(jnp.int32, (queries, keys), 0)
    column = lax.broadcasted_iota(jnp.int32, (queries, keys), 1)
    distance = row - column + (keys - queries)
    same = (q_seq[...] == k_seq[...]) & (q_seq[...] >= 0)
    return (same & (distance >= 0) & (distance < WINDOW)) | (distance == 0)


def attention(
    core_ref, query_low, kv_far, kv_near, kv_own, q_seq, k_seq,
    heads_low, log_total, spread_flat, spread_core,
):
    core = core_ref[0]
    width, per_core = spread_core.shape[1:]
    per = width // LANES
    spread_flat[...] = pick_flat(width, spread_flat.shape[1], per)
    for which, parity in enumerate((core, 1 - core)):
        spread_core[which] = pick_core(width, per_core // per, per, parity)
    head = kv_own.shape[1] // 2
    parts = (kv_far, kv_near, kv_own)
    keys = jnp.concatenate([part[:, :head] for part in parts], axis=0)
    values = jnp.concatenate([part[:, head:] for part in parts], axis=0)
    allowed = visible(q_seq, k_seq)
    for index in range(query_low.shape[1] // head):
        span = slice(index * head, (index + 1) * head)
        scores = dot_nt(query_low[:, span], keys) * query_scale
        scores = jnp.where(allowed, scores, MASKED)
        top = jnp.max(scores, axis=-1, keepdims=True)
        terms = jnp.exp(scores - top)
        total = jnp.sum(terms, axis=-1, keepdims=True)
        probs = (terms * (1.0 / total)).astype(BF16)
        heads_low[:, span] = dot(probs, values).astype(BF16)
        log_total[:, index : index + 1] = top + jnp.log(total)


def feed_forward(
    core_ref, live, gains, tok_in, out_grad_in, heads_in, spread_flat_in, spread_core_in, full,
    gain_grads, mixed_out, d_state_out, d_heads_out, low_own_out, d_gate_up_out, own_down_out,
    own_out_out, send_out,
    weights, rest, down, act, act_slope, hidden, proj, state, total, back, low_flat, low, turned_low,
    low_branch, loose, loose_out, turn_down, spread_flat, spread_core, mixed, d_state, d_heads,
    low_own, d_gate_up, own_down, own_out, send, tok, out_grad, heads_low,
    weight_sem, rest_sem, out_sem,
):
    core = core_ref[0]
    tiles, tile = weights.shape[0], weights.shape[2]
    half = tiles // 2
    width = state.shape[1]
    q_cols = heads_low.shape[1]
    per = width // LANES
    blocks, strips, down_rows = send.shape[0], send.shape[1], turn_down.shape[3]
    chips = blocks * strips
    tile_chips = tile // (2 * down_rows)
    tile_rows = tile // down_rows * SLOTS
    columns_at = tiles * tile

    def weight_copy(index):
        return pltpu.make_async_copy(
            full.at[:, pl.ds(pl.multiple_of(index * tile, tile), tile)],
            weights.at[index],
            weight_sem.at[index],
        )

    def rest_copy(which, first, last):
        return pltpu.make_async_copy(
            full.at[:, columns_at + first : columns_at + last],
            rest.at[:, first:last],
            rest_sem.at[which],
        )

    out_copy = rest_copy(0, 2 * width, 3 * width)
    down_copy = rest_copy(1, 0, 2 * width)
    flat_copy = pltpu.make_async_copy(spread_flat_in, spread_flat, rest_sem.at[2])
    core_copy = pltpu.make_async_copy(spread_core_in, spread_core, rest_sem.at[3])
    heads_copy = pltpu.make_async_copy(heads_in, heads_low, rest_sem.at[4])
    tok_copy = pltpu.make_async_copy(tok_in, tok, rest_sem.at[5])
    grad_copy = pltpu.make_async_copy(out_grad_in, out_grad, rest_sem.at[6])
    heads_copy.start()
    out_copy.start()
    tok_copy.start()
    flat_copy.start()
    down_copy.start()
    for index in range(half):
        weight_copy(index).start()
        weight_copy(half + index).start()
    core_copy.start()
    grad_copy.start()
    leaving = []

    def leave(source, target):
        leaving.append(pltpu.make_async_copy(source, target, out_sem.at[len(leaving)]))
        leaving[-1].start()

    heads_copy.wait()
    out_copy.wait()
    w_out = rest[:, 2 * width :]
    proj[...] = dot(heads_low[...], w_out)
    tok_copy.wait()
    unit, _ = normed(proj[...])
    state[...] = tok[...].astype(F32) + unit * gains[1:2, :]
    unit, scale = normed(state[...])
    low[...] = (unit * gains[2:3, :]).astype(BF16)
    flat_copy.wait()
    low_flat[...] = dot(low[...], spread_flat[...]).astype(BF16)
    total[...] = jnp.zeros_like(total)
    down_copy.wait()

    def down_tile(index):
        return down[pl.ds(pl.multiple_of(index * tile, tile), tile)]

    def forward(index, carry):
        columns = pl.ds(pl.multiple_of(index * tile, tile), tile)
        stored = rest[pl.ds(pl.multiple_of(index * tile_rows, tile_rows), tile_rows), : 2 * width]
        stored = stored.astype(F32).reshape(tile_rows // SLOTS, SLOTS, 2 * width)
        down[pl.ds(pl.multiple_of(index * tile, tile), tile)] = (
            jnp.concatenate([stored[:, :, :width], stored[:, :, width:]], axis=1)
            .reshape(tile, width)
            .astype(BF16)
        )
        weight_copy(index).wait()
        weight_copy(half + index).wait()
        gate = dot(low_flat[...], weights[index])
        up = dot(low_flat[...], weights[half + index])
        square = gate * gate
        bend = jnp.tanh(gate * (0.7978845608028654 * (1.0 + 0.044715 * square)))
        rise = 0.5 * (1.0 + bend)
        gelu = gate * rise
        slope = rise + 0.5 * gate * (1.0 - bend * bend) * (
            0.7978845608028654 * (1.0 + 0.134145 * square)
        )
        act[:, columns] = gelu
        act_slope[:, columns] = up * slope
        hidden[:, columns] = (gelu * up).astype(BF16)
        total[...] += dot(hidden[:, columns], down_tile(index))
        return carry

    lax.fori_loop(0, half, forward, 0, unroll=True)
    core_copy.wait()
    low_own[...] = dot(low[...], spread_core[0]).astype(BF16)
    turned_low[...] = jnp.transpose(dot(low[...], spread_core[1])).astype(BF16)
    leave(low_own, low_own_out)

    branch_unit, branch_scale = normed(total[...])
    mixed[...] = ((state[...] + branch_unit * gains[3:4, :]) * live[...]).astype(BF16)
    leave(mixed, mixed_out)
    grad_copy.wait()
    cotangent = out_grad[...].astype(F32) * live[...]
    d_branch, gain_grads[3:4, :] = normed_back(
        cotangent, branch_unit, branch_scale, gains[3:4, :]
    )
    low_branch[...] = d_branch.astype(BF16)
    back[...] = jnp.zeros_like(back)

    row_tiles = tiles * tile // LANES
    chunk = per * row_tiles

    def place(start, grad):
        place_rows(loose, dot(turned_low[...], grad), start, per, chips, row_tiles)

    down_at = chunk
    out_at = down_at + down_rows * (width // LANES)

    def backward(index, carry):
        columns = pl.ds(pl.multiple_of(index * tile, tile), tile)
        d_hidden = dot_nt(low_branch[...], down_tile(index))
        d_gate = (d_hidden * act_slope[:, columns]).astype(BF16)
        d_up = (d_hidden * act[:, columns]).astype(BF16)
        d_gate_up[:, columns] = d_gate
        d_gate_up[:, pl.ds(pl.multiple_of((half + index) * tile, tile), tile)] = d_up
        back[...] += dot_nt(d_gate, weights[index]) + dot_nt(d_up, weights[half + index])
        place(index * (tile // LANES), d_gate)
        place((half + index) * (tile // LANES), d_up)
        turn_down[...] = (
            dot_tn(hidden[:, columns], low_branch[...])
            .astype(BF16)
            .reshape(tile_chips // strips, strips, 2, down_rows, width)
        )
        tall = pl.ds(index * (tile_chips // strips), tile_chips // strips)
        for part in range(width // LANES):
            top = part * down_rows
            lanes = slice(part * LANES, (part + 1) * LANES)
            own_down[tall, :, top : top + down_rows, :] = turn_down[:, :, core, :, lanes]
            send[tall, :, down_at + top : down_at + top + down_rows, :] = turn_down[
                :, :, 1 - core, :, lanes
            ]
        return carry

    lax.fori_loop(0, half, backward, 0, unroll=True)
    leave(d_gate_up, d_gate_up_out)
    leave(own_down, own_down_out)

    def pack(block, carry):
        for strip in range(strips):
            send[block, strip, :chunk, :] = loose_chunk(loose, block * strips + strip, chunk).astype(
                BF16
            )
        return carry

    lax.fori_loop(0, blocks, pack, 0)
    leave(send.at[:, :, :out_at, :], send_out.at[:, :, :out_at, :])

    d_low = dot_nt(back[...].astype(BF16), spread_flat[...])
    d_norm, gain_grads[2:3, :] = normed_back(d_low, unit, scale, gains[2:3, :])
    d_state[...] = cotangent + d_norm
    leave(d_state, d_state_out)
    proj_unit, proj_scale = normed(proj[...])
    d_proj, gain_grads[1:2, :] = normed_back(d_state[...], proj_unit, proj_scale, gains[1:2, :])
    proj_low = d_proj.astype(BF16)
    loose_out[...] = dot_tn(heads_low[...], proj_low).reshape(blocks, strips, 2, SLOTS, width)
    out_tiles = width // LANES
    for target, parity, start in ((own_out, core, 0), (send, 1 - core, out_at)):
        for part in range(out_tiles // 2 + 1):
            lanes = [slice(i * LANES, (i + 1) * LANES) for i in (2 * part, 2 * part + 1)]
            pair = [
                loose_out[:, :, parity, :, lane]
                if lane.stop <= width
                else jnp.zeros((blocks, strips, SLOTS, LANES), F32)
                for lane in lanes
            ]
            top = start + 2 * part * SLOTS
            target[:, :, top : top + 2 * SLOTS, :] = jnp.concatenate(pair, axis=2).astype(BF16)
    leave(own_out, own_out_out)
    leave(send.at[:, :, out_at:, :], send_out.at[:, :, out_at:, :])
    d_heads[...] = dot_nt(proj_low, w_out).astype(BF16)
    leave(d_heads, d_heads_out)
    for copy in leaving:
        copy.wait()


def place_rows(loose, block, start, per, chips, row_tiles):
    stride = per * row_tiles + ODD
    for row in range(per):
        for part in range(block.shape[1] // LANES):
            loose[pl.ds(row * row_tiles + start + part, chips, stride=stride), :] = block[
                row * chips : (row + 1) * chips, part * LANES : (part + 1) * LANES
            ]


def loose_chunk(loose, chip, chunk):
    return loose[pl.ds(chip * (chunk + ODD), chunk), :]


def own_gradients(
    low_own, d_gate_up_in, own_down_in, own_out_in, arrived, both_out,
    both, other, d_gate_up, own_down, own_out, turned_low, loose, tile_sem, in_sem, arrived_sem, both_sem,
):
    tile = 512
    steps = d_gate_up.shape[1] // tile

    def tile_copy(index):
        span = pl.ds(pl.multiple_of(index * tile, tile), tile)
        return pltpu.make_async_copy(
            d_gate_up_in.at[:, span], d_gate_up.at[:, span], tile_sem.at[index]
        )

    for index in range(steps):
        tile_copy(index).start()
    copies = [
        pltpu.make_async_copy(own_down_in, own_down, in_sem.at[0]),
        pltpu.make_async_copy(own_out_in, own_out, in_sem.at[1]),
    ]

    def arrival(block):
        return pltpu.make_async_copy(arrived.at[block], other.at[block], arrived_sem.at[block])

    for copy in copies:
        copy.start()
    blocks, strips, down_size = own_down.shape[:3]
    for block in range(blocks):
        arrival(block).start()
    chips = blocks * strips
    per = low_own.shape[1] // chips
    row_tiles = d_gate_up.shape[1] // LANES
    chunk = per * row_tiles
    turned_low[...] = jnp.transpose(low_own[...].astype(F32)).astype(BF16)

    def place(index, carry):
        tile_copy(index).wait()
        grad = d_gate_up[:, pl.ds(pl.multiple_of(index * tile, tile), tile)]
        block = dot(turned_low[...], grad)
        place_rows(loose, block, index * (tile // LANES), per, chips, row_tiles)
        return carry

    lax.fori_loop(0, steps, place, 0)
    for copy in copies:
        copy.wait()

    def leave(block):
        return pltpu.make_async_copy(both.at[block], both_out.at[block], both_sem.at[block])

    def pack(block, carry):
        arrival(block).wait()
        for strip in range(strips):
            both[block, strip, :chunk, :] = (
                loose_chunk(loose, block * strips + strip, chunk)
                + other[block, strip, :chunk, :].astype(F32)
            ).astype(BF16)
        low, high = chunk, chunk + down_size
        both[block, :, low:high, :] = (
            own_down[block].astype(F32) + other[block, :, low:high, :].astype(F32)
        ).astype(BF16)
        both[block, :, high:, :] = (
            own_out[block].astype(F32) + other[block, :, high:, :].astype(F32)
        ).astype(BF16)
        leave(block).start()
        return carry

    lax.fori_loop(0, blocks, pack, 0)
    for block in range(blocks):
        leave(block).wait()


def attention_back(
    query_low, kv_far, kv_near, kv_own, d_heads, log_total, q_seq, k_seq,
    d_query, d_own, d_near, d_far, sum_keys, sum_values,
):
    head = kv_own.shape[1] // 2
    rows = kv_own.shape[0]
    parts = (kv_far, kv_near, kv_own)
    keys = jnp.concatenate([part[:, :head] for part in parts], axis=0)
    values = jnp.concatenate([part[:, head:] for part in parts], axis=0)
    allowed = visible(q_seq, k_seq)
    for index in range(query_low.shape[1] // head):
        span = slice(index * head, (index + 1) * head)
        scores = dot_nt(query_low[:, span], keys) * query_scale
        scores = jnp.where(allowed, scores, MASKED)
        probs = jnp.exp(scores - log_total[:, index : index + 1])
        d_probs = dot_nt(d_heads[:, span], values)
        inner = jnp.sum(probs * d_probs, axis=-1, keepdims=True)
        d_scores = (probs * (d_probs - inner)).astype(BF16)
        d_query[:, span] = dot(d_scores, keys) * query_scale
        key_term = dot_tn(d_scores, query_low[:, span]) * query_scale
        value_term = dot_tn(probs.astype(BF16), d_heads[:, span])
        if index == 0:
            sum_keys[...] = key_term
            sum_values[...] = value_term
        else:
            sum_keys[...] += key_term
            sum_values[...] += value_term
    for target, start in ((d_far, 0), (d_near, rows), (d_own, 2 * rows)):
        target[:, :head] = sum_keys[start : start + rows, :].astype(target.dtype)
        target[:, head:] = sum_values[start : start + rows, :].astype(target.dtype)


def after_attention(
    core_ref, raw, d_query, d_own, near, far, weights, tok, gains, head_gains, cos, sin,
    d_state, gain_grads, tokens_grad, keep, send, low, loose,
):
    core = core_ref[0]
    width = tok.shape[1]
    q_cols, kv_cols = d_query.shape[1], d_own.shape[1]
    head = kv_cols // 2
    tiles = (q_cols + kv_cols) // LANES
    per, per_head = width // LANES, head // LANES
    chips = weights.shape[1] // per
    chunk = keep.shape[0] // chips
    cosine, minus_sine = cos[...], -sin[...]
    query_gain_grad = jnp.zeros((1, head), F32)
    for index in range(q_cols // head):
        span = slice(index * head, (index + 1) * head)
        unit, scale = normed(raw[:, span])
        cot = turned(d_query[:, span], cosine, minus_sine)
        d_raw, part = normed_back(cot, unit, scale, head_gains[0:1, :])
        query_gain_grad += part
        low[:, span] = d_raw.astype(BF16)
    d_kv = d_own[...] + near[...].astype(F32) + far[...].astype(F32)
    unit, scale = normed(raw[:, q_cols : q_cols + head])
    cot = turned(d_kv[:, :head], cosine, minus_sine)
    d_raw, key_gain_grad = normed_back(cot, unit, scale, head_gains[1:2, :])
    low[:, q_cols : q_cols + head] = d_raw.astype(BF16)
    low[:, q_cols + head :] = d_kv[:, head:].astype(BF16)

    selectors = [pick_core(width, chips, per, parity) for parity in (core, 1 - core)]
    d_low = jnp.zeros(tok.shape, F32)
    for which, selector in enumerate(selectors):
        part = dot_nt(low[...], weights[which])
        high = part.astype(BF16)
        rounding = (part - high.astype(F32)).astype(BF16)
        d_low += dot_nt(high, selector) + dot_nt(rounding, selector)
    unit, scale = normed(tok[...].astype(F32))
    d_norm, in_gain_grad = normed_back(d_low, unit, scale, gains[0:1, :])
    tokens_grad[...] = (d_state[...] + d_norm).astype(BF16)

    wide = jnp.zeros((LANES, width), F32)
    vectors = [in_gain_grad] + [gain_grads[i : i + 1, :] for i in range(1, 4)]
    for which, vector in enumerate(vectors):
        wide = jnp.where(gain_mask(which * per, per, LANES, width), vector, wide)
    narrow = jnp.zeros((LANES, head), F32)
    for which, vector in enumerate((query_gain_grad, key_gain_grad)):
        mask = gain_mask(4 * per + which * per_head, per_head, LANES, head)
        narrow = jnp.where(mask, vector, narrow)
    wide, narrow = wide.astype(BF16), narrow.astype(BF16)
    attn_low = (unit * gains[0:1, :]).astype(BF16)
    stride = chunk + ODD
    for row in range(per * tiles + 1, chunk):
        loose[pl.ds(row, chips, stride=stride), :] = jnp.zeros((chips, LANES), F32)
    for target, selector, parity in ((keep, selectors[0], core), (send, selectors[1], 1 - core)):
        extra = dot(wide, pick_chip(width, chips, per, parity)) + dot(
            narrow, pick_chip(head, chips, per_head, parity)
        )
        loose[pl.ds(per * tiles, chips, stride=stride), :] = jnp.transpose(extra)
        block = dot_tn(dot(attn_low, selector).astype(BF16), low[...])
        for row in range(per):
            for tile in range(tiles):
                loose[pl.ds(row * tiles + tile, chips, stride=stride), :] = block[
                    row * chips : (row + 1) * chips, tile * LANES : (tile + 1) * LANES
                ]
        for chip in range(chips):
            target[chip * chunk : (chip + 1) * chunk, :] = loose_chunk(loose, chip, chunk).astype(BF16)


def on_device(
    tokens,
    out_grad,
    seq_start,
    seq_len,
    w_query,
    w_key_value,
    w_output,
    w_gate_up,
    w_down,
    norm_attn_in,
    norm_attn_out,
    norm_mlp_in,
    norm_mlp_out,
    norm_query,
    norm_key,
):
    size = lax.axis_size("fsdp")
    chips = size // 2
    me = lax.axis_index("fsdp")
    core = me % 2
    core_arg = core.astype(jnp.int32).reshape(1)
    tok_rows, width = tokens.shape
    shard = w_query.shape[0]
    q_cols, kv_cols = w_query.shape[1], w_key_value.shape[1]
    qkv_cols = q_cols + kv_cols
    gu_cols, ff = w_gate_up.shape[1], w_down.shape[0] * size
    down_rows = w_down.shape[0]
    head = kv_cols // 2
    hshard = norm_query.shape[0]

    gathered = jnp.zeros((SLOTS, gu_cols + 3 * width), BF16)
    column = 0
    zero = jnp.zeros((), BF16)
    for part, first in ((w_gate_up, 0), (w_down, 0), (w_down, SLOTS), (w_output, 0)):
        high, wide = part.shape
        after = gathered.shape[1] - column - wide
        rows = (-first, SLOTS - high + first, 0)
        gathered = gathered + lax.pad(part, zero, (rows, (column, after, 0)))
        column += wide
    mlp_full = lax.all_gather(gathered, "fsdp", axis=0, tiled=True)

    tiles = qkv_cols // LANES
    chunk = 64
    gain_row = jnp.zeros((1, LANES), BF16)
    gain_count = 0
    for part in (norm_attn_in, norm_attn_out, norm_mlp_in, norm_mlp_out, norm_query, norm_key):
        wide = part.shape[0]
        gain_row = gain_row + jnp.pad(part[None], ((0, 0), (gain_count, LANES - gain_count - wide)))
        gain_count += wide
    pack = jnp.concatenate(
        [
            jnp.concatenate([w_query, w_key_value], axis=1).reshape(shard * tiles, LANES),
            jnp.pad(gain_row, ((0, chunk - shard * tiles - 1), (0, 0))),
        ],
        axis=0,
    )
    own = spread(pack).reshape(chips * chunk, LANES)
    peer = swap_cores(own)

    key_reach = (WINDOW + tok_rows - 2) // tok_rows
    first_token = me * tok_rows
    q_index, q_seq, q_pos, q_live = token_layout(seq_start, seq_len, first_token, tok_rows)
    k_index, k_seq, k_pos, k_live = token_layout(
        seq_start, seq_len, first_token - key_reach * tok_rows, (key_reach + 1) * tok_rows
    )
    live = q_live.astype(F32)[:, None]
    q_seq, k_seq = q_seq[:, None], k_seq[None, :]
    inv_freq = theta_base ** (-2.0 * jnp.arange(head // 2, dtype=F32) / head)
    angles = q_pos.astype(F32)[:, None] * inv_freq[None, :]
    cos_vals, sin_vals = jnp.cos(angles), jnp.sin(angles)

    raw, query_low, own_kv, gains, head_gains, attn_weights = call(
        before_attention,
        (
            shape((tok_rows, qkv_cols), F32),
            shape((tok_rows, q_cols), BF16),
            shape((tok_rows, kv_cols), BF16),
            shape((8, width), F32),
            shape((8, head), F32),
            shape((2, chips * shard, qkv_cols), BF16),
        ),
        (core_arg, tokens, own, peer, cos_vals, sin_vals),
        scratch=(pltpu.VMEM((chips * (chunk + ODD), LANES), F32),),
        specs=[SCALAR] + [WHOLE] * 5,
    )
    kv_near = shifted(own_kv, "fsdp", 1)
    kv_far = shifted(own_kv, "fsdp", 2)
    heads_low, log_total, spread_flat, spread_core = call(
        attention,
        (
            shape((tok_rows, q_cols), BF16),
            shape((tok_rows, LANES), F32),
            shape((width, size * SLOTS), BF16),
            shape((2, width, width // 2), BF16),
        ),
        (core_arg, query_low, kv_far, kv_near, own_kv, q_seq, k_seq),
        specs=[SCALAR] + [WHOLE] * 6,
        flops=20e9,
    )

    tile = 512
    blocks, strips = 8, chips // 8
    down_at = shard * gu_cols // LANES
    out_at = down_at + down_rows * (width // LANES)
    chunk_rows = out_at + 6 * SLOTS
    chunk_shape = (blocks, strips, chunk_rows, LANES)
    gain_grads, mixed, d_state, d_heads, low_own, d_gate_up, own_down, own_out, send = call(
        feed_forward,
        (
            shape((8, width), F32),
            shape((tok_rows, width), BF16),
            shape((tok_rows, width), F32),
            shape((tok_rows, q_cols), BF16),
            shape((tok_rows, width // 2), BF16),
            shape((tok_rows, gu_cols), BF16),
            shape((blocks, strips, out_at - down_at, LANES), BF16),
            shape((blocks, strips, 6 * SLOTS, LANES), BF16),
            shape(chunk_shape, BF16),
        ),
        (
            core_arg, live, gains, tokens, out_grad, heads_low, spread_flat, spread_core, mlp_full,
        ),
        scratch=(
            pltpu.VMEM((gu_cols // tile, size * SLOTS, tile), BF16),
            pltpu.VMEM((size * SLOTS, 3 * width), BF16),
            pltpu.VMEM((ff, width), BF16),
            pltpu.VMEM((tok_rows, ff), F32),
            pltpu.VMEM((tok_rows, ff), F32),
            pltpu.VMEM((tok_rows, ff), BF16),
            pltpu.VMEM((tok_rows, width), F32),
            pltpu.VMEM((tok_rows, width), F32),
            pltpu.VMEM((tok_rows, width), F32),
            pltpu.VMEM((tok_rows, size * SLOTS), F32),
            pltpu.VMEM((tok_rows, size * SLOTS), BF16),
            pltpu.VMEM((tok_rows, width), BF16),
            pltpu.VMEM((width // 2, tok_rows), BF16),
            pltpu.VMEM((tok_rows, width), BF16),
            pltpu.VMEM((chips * (down_at + ODD), LANES), F32),
            pltpu.VMEM((blocks, strips, 2, SLOTS, width), F32),
            pltpu.VMEM((tile // (2 * down_rows) // strips, strips, 2, down_rows, width), BF16),
            pltpu.VMEM((width, size * SLOTS), BF16),
            pltpu.VMEM((2, width, width // 2), BF16),
            pltpu.VMEM((tok_rows, width), BF16),
            pltpu.VMEM((tok_rows, width), F32),
            pltpu.VMEM((tok_rows, q_cols), BF16),
            pltpu.VMEM((tok_rows, width // 2), BF16),
            pltpu.VMEM((tok_rows, gu_cols), BF16),
            pltpu.VMEM((blocks, strips, out_at - down_at, LANES), BF16),
            pltpu.VMEM((blocks, strips, 6 * SLOTS, LANES), BF16),
            pltpu.VMEM(chunk_shape, BF16),
            pltpu.VMEM((tok_rows, width), BF16),
            pltpu.VMEM((tok_rows, width), BF16),
            pltpu.VMEM((tok_rows, q_cols), BF16),
            pltpu.SemaphoreType.DMA((gu_cols // tile,)),
            pltpu.SemaphoreType.DMA((7,)),
            pltpu.SemaphoreType.DMA((9,)),
        ),
        specs=[SCALAR] + [WHOLE] * 2 + [AWAY] * 6,
        out_specs=(WHOLE,) + (AWAY,) * 8,
        flops=12e9,
    )
    arrived = swap_cores(send)

    d_query, d_own, d_near, d_far = call(
        attention_back,
        (
            shape((tok_rows, q_cols), F32),
            shape((tok_rows, kv_cols), F32),
            shape((tok_rows, kv_cols), BF16),
            shape((tok_rows, kv_cols), BF16),
        ),
        (query_low, kv_far, kv_near, own_kv, d_heads, log_total, q_seq, k_seq),
        scratch=(
            pltpu.VMEM(((key_reach + 1) * tok_rows, head), F32),
            pltpu.VMEM(((key_reach + 1) * tok_rows, head), F32),
        ),
        specs=[WHOLE] * 8,
        flops=20e9,
    )
    near = shifted(d_near, "fsdp", -1)
    far = shifted(d_far, "fsdp", -2)
    arrived, far_started = lax.optimization_barrier((arrived, d_far))
    both_mlp = call(
        own_gradients,
        shape(chunk_shape, BF16),
        (low_own, d_gate_up, own_down, own_out, arrived),
        scratch=(
            pltpu.VMEM(chunk_shape, BF16),
            pltpu.VMEM(chunk_shape, BF16),
            pltpu.VMEM((tok_rows, gu_cols), BF16),
            pltpu.VMEM((blocks, strips, out_at - down_at, LANES), BF16),
            pltpu.VMEM((blocks, strips, 6 * SLOTS, LANES), BF16),
            pltpu.VMEM((width // 2, tok_rows), BF16),
            pltpu.VMEM((chips * (down_at + ODD), LANES), F32),
            pltpu.SemaphoreType.DMA((gu_cols // tile,)),
            pltpu.SemaphoreType.DMA((2,)),
            pltpu.SemaphoreType.DMA((blocks,)),
            pltpu.SemaphoreType.DMA((blocks,)),
        ),
        specs=[WHOLE] + [AWAY] * 4,
        out_specs=AWAY,
        flops=12e9,
        vmem=62 * 1024 * 1024,
    )
    both_mlp, near, far = lax.optimization_barrier((both_mlp, near, far))
    mlp_parts = exchange(both_mlp.reshape(chips, chunk_rows, LANES))
    tokens_grad, keep, send = call(
        after_attention,
        (
            shape((tok_rows, width), BF16),
            shape((chips * chunk, LANES), BF16),
            shape((chips * chunk, LANES), BF16),
        ),
        (
            core_arg, raw, d_query, d_own, near, far, attn_weights, tokens, gains,
            head_gains, cos_vals, sin_vals, d_state, gain_grads,
        ),
        scratch=(
            pltpu.VMEM((tok_rows, qkv_cols), BF16),
            pltpu.VMEM((chips * (chunk + ODD), LANES), F32),
        ),
        specs=[SCALAR] + [WHOLE] * 13,
        flops=20e9,
    )
    both = (keep.astype(F32) + swap_cores(send).astype(F32)).astype(BF16)
    both, mlp_parts = lax.optimization_barrier((both, mlp_parts))
    share_attn = jnp.sum(exchange(both.reshape(chips, chunk, LANES)).astype(F32), axis=0)
    share_qkv = share_attn[: shard * tiles].reshape(shard, tiles * LANES)
    share_gains = share_attn[shard * tiles, :gain_count]

    share_mlp = jnp.sum(mlp_parts.astype(F32), axis=0)
    share_gate_up = share_mlp[:down_at].reshape(shard, gu_cols)
    share_down = (
        share_mlp[down_at:out_at]
        .reshape(width // LANES, down_rows, LANES)
        .transpose(1, 0, 2)
        .reshape(down_rows, width)
    )
    share_output = (
        share_mlp[out_at : out_at + SLOTS * (width // LANES)]
        .reshape(width // LANES, SLOTS, LANES)
        .transpose(1, 0, 2)
        .reshape(SLOTS, width)
    )
    return (
        mixed,
        tokens_grad,
        share_qkv[:, :q_cols],
        share_qkv[:, q_cols:],
        share_output,
        share_gate_up,
        share_down,
        share_gains[:shard],
        share_gains[shard : 2 * shard],
        share_gains[2 * shard : 3 * shard],
        share_gains[3 * shard : 4 * shard],
        share_gains[4 * shard : 4 * shard + hshard],
        share_gains[4 * shard + hshard :],
    )


def solution(mesh):
    placed = (
        P("fsdp", None),
        P("fsdp", None),
        P(),
        P(),
        P("fsdp", None),
        P("fsdp", None),
        P("fsdp", None),
        P("fsdp", None),
        P("fsdp", None),
        P("fsdp"),
        P("fsdp"),
        P("fsdp"),
        P("fsdp"),
        P("fsdp"),
        P("fsdp"),
    )
    return jax.shard_map(
        on_device,
        mesh=mesh,
        in_specs=placed,
        out_specs=(
            P("fsdp", None),
            P("fsdp", None),
            P("fsdp", None),
            P("fsdp", None),
            P("fsdp", None),
            P("fsdp", None),
            P("fsdp", None),
            P("fsdp"),
            P("fsdp"),
            P("fsdp"),
            P("fsdp"),
            P("fsdp"),
            P("fsdp"),
        ),
        check_vma=False,
    )
```

```python
import jax
import jax.numpy as jnp
from jax import lax
from jax.experimental import pallas as pl
from jax.experimental.pallas import tpu as pltpu
from jax.sharding import PartitionSpec as P

WINDOW = 512


epsilon = 1e-06
theta_base = 10000.0
query_scale = 0.0625


def shifted(block, axis, distance):
    devices = range(lax.axis_size(axis))
    route = [(i - distance, i) for i in devices if i - distance in devices]
    return lax.ppermute(block, axis, route)


def token_layout(seq_start, seq_len, first_token, token_count):
    indices = first_token + jnp.arange(token_count, dtype=jnp.int32)
    offsets = indices[:, None] - seq_start[None, :]
    inside = (offsets >= 0) & (offsets < seq_len[None, :])
    live_mask = jnp.any(inside, axis=1)
    seq_numbers = jnp.arange(seq_start.shape[0], dtype=jnp.int32)
    seq_id = jnp.sum(jnp.where(inside, seq_numbers[None, :], 0), axis=1)
    seq_id = jnp.where(live_mask, seq_id, -1)
    positions = jnp.sum(jnp.where(inside, offsets, 0), axis=1)
    return (indices, seq_id, positions, live_mask)


BF16 = jnp.bfloat16
F32 = jnp.float32
SLOTS = 8
MASKED = -1e30
ODD = 1
VMEM_BYTES = 56 * 1024 * 1024
LANES = 128


def same_core_groups(size):
    return [[2 * chip + core for chip in range(size // 2)] for core in range(2)]


LINE = 4


def line_groups(size):
    planes = size // 2 // LINE
    return [
        [2 * (plane * LINE + x) + core for x in range(LINE)]
        for plane in range(planes)
        for core in range(2)
    ]


def plane_groups(size):
    planes = size // 2 // LINE
    return [
        [2 * (plane * LINE + x) + core for plane in range(planes)]
        for x in range(LINE)
        for core in range(2)
    ]


def line_first(place, chips):
    planes = chips // LINE
    return lax.rem(place, planes) * LINE + lax.div(place, planes)


def swap_cores(block):
    size = lax.axis_size("fsdp")
    return lax.ppermute(block, "fsdp", [(i, i ^ 1) for i in range(size)])


def exchange(blocks):
    return lax.all_to_all(
        blocks,
        "fsdp",
        split_axis=0,
        concat_axis=0,
        tiled=True,
        axis_index_groups=same_core_groups(lax.axis_size("fsdp")),
    )


def spread(block):
    chips = lax.axis_size("fsdp") // 2
    return exchange(jnp.broadcast_to(block[None], (chips,) + block.shape))


def call(kernel, outs, ins, scratch=(), specs=None, flops=4e9, out_specs=None, vmem=VMEM_BYTES):
    return pl.pallas_call(
        kernel,
        out_shape=outs,
        in_specs=specs,
        **({} if out_specs is None else {"out_specs": out_specs}),
        scratch_shapes=list(scratch),
        compiler_params=pltpu.CompilerParams(vmem_limit_bytes=vmem),
        cost_estimate=pl.CostEstimate(
            flops=int(flops), bytes_accessed=8_000_000, transcendentals=0
        ),
    )(*ins)


SCALAR = pl.BlockSpec(memory_space=pltpu.SMEM)
WHOLE = pl.BlockSpec(memory_space=pltpu.VMEM)
AWAY = pl.BlockSpec(memory_space=pl.ANY)


def shape(dims, kind):
    return jax.ShapeDtypeStruct(dims, kind)


def dot(left, right):
    return jnp.dot(left, right, preferred_element_type=F32)


def dot_nt(left, right):
    return lax.dot_general(left, right, (((1,), (1,)), ((), ())), preferred_element_type=F32)


def dot_tn(left, right):
    return lax.dot_general(left, right, (((0,), (0,)), ((), ())), preferred_element_type=F32)


def normed(values):
    scale = lax.rsqrt(jnp.mean(values * values, axis=-1, keepdims=True) + epsilon)
    return values * scale, scale


def normed_back(cot, unit, scale, gain):
    weighted = cot * gain
    inner = jnp.mean(weighted * unit, axis=-1, keepdims=True)
    return scale * (weighted - unit * inner), jnp.sum(cot * unit, axis=0, keepdims=True)


def ones_where(mask):
    return jnp.where(mask, 1.0, 0.0).astype(BF16)


def pick_flat(rows, count, per):
    place = lax.broadcasted_iota(jnp.int32, (1, count), 1)
    device, slot = lax.shift_right_logical(place, 3), place & (SLOTS - 1)
    source = jnp.where(slot < per, device * per + slot, -1)
    return ones_where(lax.broadcasted_iota(jnp.int32, (rows, count), 0) == source)


def pick_core(rows, chips, per, core, lines=False):
    place = lax.broadcasted_iota(jnp.int32, (1, chips * per), 1)
    row, chip = lax.div(place, chips), lax.rem(place, chips)
    if lines:
        chip = line_first(chip, chips)
    source = (2 * chip + core) * per + row
    return ones_where(lax.broadcasted_iota(jnp.int32, (rows, chips * per), 0) == source)


def pick_chip(rows, chips, per, core, lines=False):
    chip = lax.broadcasted_iota(jnp.int32, (1, chips), 1)
    if lines:
        chip = line_first(chip, chips)
    low = (2 * chip + core) * per
    natural = lax.broadcasted_iota(jnp.int32, (rows, chips), 0)
    return ones_where((natural >= low) & (natural < low + per))


def gain_mask(first, per, rows, columns):
    row = lax.broadcasted_iota(jnp.int32, (rows, columns), 0)
    column = lax.broadcasted_iota(jnp.int32, (rows, columns), 1)
    return row == first + lax.rem(column, per)


def turned(values, cos, sin):
    half = values.shape[-1] // 2
    first, second = values[:, :half], values[:, half:]
    return jnp.concatenate([first * cos - second * sin, second * cos + first * sin], axis=1)


def before_attention(
    core_ref, tok, own, peer, cos, sin, raw, query_low, own_kv, gains, head_gains, weights, loose
):
    core = core_ref[0]
    width = tok.shape[1]
    kv_cols = own_kv.shape[1]
    head = kv_cols // 2
    q_cols = query_low.shape[1]
    columns = q_cols + kv_cols
    tiles = columns // LANES
    per, per_head = width // LANES, head // LANES
    chips = weights.shape[1] // per
    chunk = own.shape[0] // chips
    wide = jnp.zeros((width, LANES), F32)
    narrow = jnp.zeros((head, LANES), F32)
    stride = chunk + ODD
    for which, (block, parity) in enumerate(((own, core), (peer, 1 - core))):
        for chip in range(chips):
            loose[chip * stride : chip * stride + chunk, :] = block[
                chip * chunk : (chip + 1) * chunk, :
            ].astype(F32)
        for row in range(per):
            for tile in range(tiles):
                weights[
                    which, row * chips : (row + 1) * chips, tile * LANES : (tile + 1) * LANES
                ] = loose[pl.ds(row * tiles + tile, chips, stride=stride), :].astype(BF16)
        found = loose[pl.ds(per * tiles, chips, stride=stride), :].astype(BF16)
        wide += dot(pick_chip(width, chips, per, parity), found)
        narrow += dot(pick_chip(head, chips, per_head, parity), found)
    wide, narrow = jnp.transpose(wide)[:32], jnp.transpose(narrow)[:32]
    for which in range(4):
        mask = gain_mask(which * per, per, 32, width)
        gains[which : which + 1, :] = jnp.sum(jnp.where(mask, wide, 0.0), 0, keepdims=True)
    for which in range(2):
        mask = gain_mask(4 * per + which * per_head, per_head, 32, head)
        head_gains[which : which + 1, :] = jnp.sum(jnp.where(mask, narrow, 0.0), 0, keepdims=True)
    unit, _ = normed(tok[...].astype(F32))
    low = (unit * gains[0:1, :]).astype(BF16)
    raw[...] = dot(dot(low, pick_core(width, chips, per, core)).astype(BF16), weights[0]) + dot(
        dot(low, pick_core(width, chips, per, 1 - core)).astype(BF16), weights[1]
    )
    for index in range(q_cols // head):
        span = slice(index * head, (index + 1) * head)
        unit, _ = normed(raw[:, span])
        query_low[:, span] = turned(unit * head_gains[0:1, :], cos[...], sin[...]).astype(BF16)
    unit, _ = normed(raw[:, q_cols : q_cols + head])
    own_kv[:, :head] = turned(unit * head_gains[1:2, :], cos[...], sin[...]).astype(BF16)
    own_kv[:, head:] = raw[:, q_cols + head :].astype(BF16)


def visible(q_seq, k_seq):
    queries, keys = q_seq.shape[0], k_seq.shape[1]
    row = lax.broadcasted_iota(jnp.int32, (queries, keys), 0)
    column = lax.broadcasted_iota(jnp.int32, (queries, keys), 1)
    distance = row - column + (keys - queries)
    same = (q_seq[...] == k_seq[...]) & (q_seq[...] >= 0)
    return (same & (distance >= 0) & (distance < WINDOW)) | (distance == 0)


def attention(
    core_ref, query_low, kv_far, kv_near, kv_own, q_seq, k_seq,
    heads_low, log_total, spread_flat, spread_core,
):
    core = core_ref[0]
    width, per_core = spread_core.shape[1:]
    per = width // LANES
    spread_flat[...] = pick_flat(width, spread_flat.shape[1], per)
    for which, parity in enumerate((core, 1 - core)):
        spread_core[which] = pick_core(width, per_core // per, per, parity)
    head = kv_own.shape[1] // 2
    parts = (kv_far, kv_near, kv_own)
    keys = jnp.concatenate([part[:, :head] for part in parts], axis=0)
    values = jnp.concatenate([part[:, head:] for part in parts], axis=0)
    allowed = visible(q_seq, k_seq)
    for index in range(query_low.shape[1] // head):
        span = slice(index * head, (index + 1) * head)
        scores = dot_nt(query_low[:, span], keys) * query_scale
        scores = jnp.where(allowed, scores, MASKED)
        top = jnp.max(scores, axis=-1, keepdims=True)
        terms = jnp.exp(scores - top)
        total = jnp.sum(terms, axis=-1, keepdims=True)
        probs = (terms * (1.0 / total)).astype(BF16)
        heads_low[:, span] = dot(probs, values).astype(BF16)
        log_total[:, index : index + 1] = top + jnp.log(total)


def feed_forward(
    core_ref, live, gains, tok_in, out_grad_in, heads_in, spread_flat_in, spread_core_in, full,
    gain_grads, mixed_out, d_state_out, d_heads_out, low_own_out, d_gate_up_out, own_down_out,
    own_out_out, send_out,
    weights, rest, down, act, act_slope, hidden, proj, state, total, back, low_flat, low, turned_low,
    low_branch, loose, loose_out, turn_down, spread_flat, spread_core, mixed, d_state, d_heads,
    low_own, d_gate_up, own_down, own_out, send, tok, out_grad, heads_low,
    weight_sem, rest_sem, out_sem,
):
    core = core_ref[0]
    tiles, tile = weights.shape[0], weights.shape[2]
    half = tiles // 2
    width = state.shape[1]
    q_cols = heads_low.shape[1]
    per = width // LANES
    blocks, strips, down_rows = send.shape[0], send.shape[1], turn_down.shape[3]
    chips = blocks * strips
    tile_chips = tile // (2 * down_rows)
    tile_rows = tile // down_rows * SLOTS
    columns_at = tiles * tile

    def weight_copy(index):
        return pltpu.make_async_copy(
            full.at[:, pl.ds(pl.multiple_of(index * tile, tile), tile)],
            weights.at[index],
            weight_sem.at[index],
        )

    def rest_copy(which, first, last):
        return pltpu.make_async_copy(
            full.at[:, columns_at + first : columns_at + last],
            rest.at[:, first:last],
            rest_sem.at[which],
        )

    out_copy = rest_copy(0, 2 * width, 3 * width)
    down_copy = rest_copy(1, 0, 2 * width)
    flat_copy = pltpu.make_async_copy(spread_flat_in, spread_flat, rest_sem.at[2])
    core_copy = pltpu.make_async_copy(spread_core_in, spread_core, rest_sem.at[3])
    heads_copy = pltpu.make_async_copy(heads_in, heads_low, rest_sem.at[4])
    tok_copy = pltpu.make_async_copy(tok_in, tok, rest_sem.at[5])
    grad_copy = pltpu.make_async_copy(out_grad_in, out_grad, rest_sem.at[6])
    heads_copy.start()
    out_copy.start()
    tok_copy.start()
    flat_copy.start()
    down_copy.start()
    for index in range(half):
        weight_copy(index).start()
        weight_copy(half + index).start()
    core_copy.start()
    grad_copy.start()
    leaving = []

    def leave(source, target):
        leaving.append(pltpu.make_async_copy(source, target, out_sem.at[len(leaving)]))
        leaving[-1].start()

    heads_copy.wait()
    out_copy.wait()
    w_out = rest[:, 2 * width :]
    proj[...] = dot(heads_low[...], w_out)
    tok_copy.wait()
    unit, _ = normed(proj[...])
    state[...] = tok[...].astype(F32) + unit * gains[1:2, :]
    unit, scale = normed(state[...])
    low[...] = (unit * gains[2:3, :]).astype(BF16)
    flat_copy.wait()
    low_flat[...] = dot(low[...], spread_flat[...]).astype(BF16)
    total[...] = jnp.zeros_like(total)
    down_copy.wait()

    def down_tile(index):
        return down[pl.ds(pl.multiple_of(index * tile, tile), tile)]

    def forward(index, carry):
        columns = pl.ds(pl.multiple_of(index * tile, tile), tile)
        stored = rest[pl.ds(pl.multiple_of(index * tile_rows, tile_rows), tile_rows), : 2 * width]
        stored = stored.astype(F32).reshape(tile_rows // SLOTS, SLOTS, 2 * width)
        down[pl.ds(pl.multiple_of(index * tile, tile), tile)] = (
            jnp.concatenate([stored[:, :, :width], stored[:, :, width:]], axis=1)
            .reshape(tile, width)
            .astype(BF16)
        )
        weight_copy(index).wait()
        weight_copy(half + index).wait()
        gate = dot(low_flat[...], weights[index])
        up = dot(low_flat[...], weights[half + index])
        square = gate * gate
        bend = jnp.tanh(gate * (0.7978845608028654 * (1.0 + 0.044715 * square)))
        rise = 0.5 * (1.0 + bend)
        gelu = gate * rise
        slope = rise + 0.5 * gate * (1.0 - bend * bend) * (
            0.7978845608028654 * (1.0 + 0.134145 * square)
        )
        act[:, columns] = gelu
        act_slope[:, columns] = up * slope
        hidden[:, columns] = (gelu * up).astype(BF16)
        total[...] += dot(hidden[:, columns], down_tile(index))
        return carry

    lax.fori_loop(0, half, forward, 0, unroll=True)
    core_copy.wait()
    low_own[...] = dot(low[...], spread_core[0]).astype(BF16)
    turned_low[...] = jnp.transpose(dot(low[...], spread_core[1])).astype(BF16)
    leave(low_own, low_own_out)

    branch_unit, branch_scale = normed(total[...])
    mixed[...] = ((state[...] + branch_unit * gains[3:4, :]) * live[...]).astype(BF16)
    leave(mixed, mixed_out)
    grad_copy.wait()
    cotangent = out_grad[...].astype(F32) * live[...]
    d_branch, gain_grads[3:4, :] = normed_back(
        cotangent, branch_unit, branch_scale, gains[3:4, :]
    )
    low_branch[...] = d_branch.astype(BF16)
    back[...] = jnp.zeros_like(back)

    row_tiles = tiles * tile // LANES
    chunk = per * row_tiles

    def place(start, grad):
        place_rows(loose, dot(turned_low[...], grad), start, per, chips, row_tiles)

    down_at = chunk
    out_at = down_at + down_rows * (width // LANES)

    def backward(index, carry):
        columns = pl.ds(pl.multiple_of(index * tile, tile), tile)
        d_hidden = dot_nt(low_branch[...], down_tile(index))
        d_gate = (d_hidden * act_slope[:, columns]).astype(BF16)
        d_up = (d_hidden * act[:, columns]).astype(BF16)
        d_gate_up[:, columns] = d_gate
        d_gate_up[:, pl.ds(pl.multiple_of((half + index) * tile, tile), tile)] = d_up
        back[...] += dot_nt(d_gate, weights[index]) + dot_nt(d_up, weights[half + index])
        place(index * (tile // LANES), d_gate)
        place((half + index) * (tile // LANES), d_up)
        turn_down[...] = (
            dot_tn(hidden[:, columns], low_branch[...])
            .astype(BF16)
            .reshape(tile_chips // strips, strips, 2, down_rows, width)
        )
        tall = pl.ds(index * (tile_chips // strips), tile_chips // strips)
        for part in range(width // LANES):
            top = part * down_rows
            lanes = slice(part * LANES, (part + 1) * LANES)
            own_down[tall, :, top : top + down_rows, :] = turn_down[:, :, core, :, lanes]
            send[tall, :, down_at + top : down_at + top + down_rows, :] = turn_down[
                :, :, 1 - core, :, lanes
            ]
        return carry

    lax.fori_loop(0, half, backward, 0, unroll=True)
    leave(d_gate_up, d_gate_up_out)
    leave(own_down, own_down_out)

    def pack(block, carry):
        for strip in range(strips):
            send[block, strip, :chunk, :] = loose_chunk(loose, block * strips + strip, chunk).astype(
                BF16
            )
        return carry

    lax.fori_loop(0, blocks, pack, 0)
    leave(send.at[:, :, :out_at, :], send_out.at[:, :, :out_at, :])

    d_low = dot_nt(back[...].astype(BF16), spread_flat[...])
    d_norm, gain_grads[2:3, :] = normed_back(d_low, unit, scale, gains[2:3, :])
    d_state[...] = cotangent + d_norm
    leave(d_state, d_state_out)
    proj_unit, proj_scale = normed(proj[...])
    d_proj, gain_grads[1:2, :] = normed_back(d_state[...], proj_unit, proj_scale, gains[1:2, :])
    proj_low = d_proj.astype(BF16)
    loose_out[...] = dot_tn(heads_low[...], proj_low).reshape(blocks, strips, 2, SLOTS, width)
    out_tiles = width // LANES
    for target, parity, start in ((own_out, core, 0), (send, 1 - core, out_at)):
        for part in range(out_tiles // 2 + 1):
            lanes = [slice(i * LANES, (i + 1) * LANES) for i in (2 * part, 2 * part + 1)]
            pair = [
                loose_out[:, :, parity, :, lane]
                if lane.stop <= width
                else jnp.zeros((blocks, strips, SLOTS, LANES), F32)
                for lane in lanes
            ]
            top = start + 2 * part * SLOTS
            target[:, :, top : top + 2 * SLOTS, :] = jnp.concatenate(pair, axis=2).astype(BF16)
    leave(own_out, own_out_out)
    leave(send.at[:, :, out_at:, :], send_out.at[:, :, out_at:, :])
    d_heads[...] = dot_nt(proj_low, w_out).astype(BF16)
    leave(d_heads, d_heads_out)
    for copy in leaving:
        copy.wait()


def place_rows(loose, block, start, per, chips, row_tiles):
    stride = per * row_tiles + ODD
    for row in range(per):
        for part in range(block.shape[1] // LANES):
            loose[pl.ds(row * row_tiles + start + part, chips, stride=stride), :] = block[
                row * chips : (row + 1) * chips, part * LANES : (part + 1) * LANES
            ]


def loose_chunk(loose, chip, chunk):
    return loose[pl.ds(chip * (chunk + ODD), chunk), :]


def own_gradients(
    low_own, d_gate_up_in, own_down_in, own_out_in, arrived, both_out,
    both, other, d_gate_up, own_down, own_out, turned_low, loose, tile_sem, in_sem, arrived_sem, both_sem,
):
    tile = 512
    steps = d_gate_up.shape[1] // tile

    def tile_copy(index):
        span = pl.ds(pl.multiple_of(index * tile, tile), tile)
        return pltpu.make_async_copy(
            d_gate_up_in.at[:, span], d_gate_up.at[:, span], tile_sem.at[index]
        )

    for index in range(steps):
        tile_copy(index).start()
    copies = [
        pltpu.make_async_copy(own_down_in, own_down, in_sem.at[0]),
        pltpu.make_async_copy(own_out_in, own_out, in_sem.at[1]),
    ]

    def arrival(block):
        return pltpu.make_async_copy(arrived.at[block], other.at[block], arrived_sem.at[block])

    for copy in copies:
        copy.start()
    blocks, strips, down_size = own_down.shape[:3]
    for block in range(blocks):
        arrival(block).start()
    chips = blocks * strips
    per = low_own.shape[1] // chips
    row_tiles = d_gate_up.shape[1] // LANES
    chunk = per * row_tiles
    turned_low[...] = jnp.transpose(low_own[...].astype(F32)).astype(BF16)

    def place(index, carry):
        tile_copy(index).wait()
        grad = d_gate_up[:, pl.ds(pl.multiple_of(index * tile, tile), tile)]
        block = dot(turned_low[...], grad)
        place_rows(loose, block, index * (tile // LANES), per, chips, row_tiles)
        return carry

    lax.fori_loop(0, steps, place, 0)
    for copy in copies:
        copy.wait()

    def leave(block):
        return pltpu.make_async_copy(both.at[block], both_out.at[block], both_sem.at[block])

    def pack(block, carry):
        arrival(block).wait()
        for strip in range(strips):
            both[block, strip, :chunk, :] = (
                loose_chunk(loose, block * strips + strip, chunk)
                + other[block, strip, :chunk, :].astype(F32)
            ).astype(BF16)
        low, high = chunk, chunk + down_size
        both[block, :, low:high, :] = (
            own_down[block].astype(F32) + other[block, :, low:high, :].astype(F32)
        ).astype(BF16)
        both[block, :, high:, :] = (
            own_out[block].astype(F32) + other[block, :, high:, :].astype(F32)
        ).astype(BF16)
        leave(block).start()
        return carry

    lax.fori_loop(0, blocks, pack, 0)
    for block in range(blocks):
        leave(block).wait()


def attention_back(
    query_low, kv_far, kv_near, kv_own, d_heads, log_total, q_seq, k_seq,
    d_query, d_own, d_near, d_far, sum_keys, sum_values,
):
    head = kv_own.shape[1] // 2
    rows = kv_own.shape[0]
    parts = (kv_far, kv_near, kv_own)
    keys = jnp.concatenate([part[:, :head] for part in parts], axis=0)
    values = jnp.concatenate([part[:, head:] for part in parts], axis=0)
    allowed = visible(q_seq, k_seq)
    for index in range(query_low.shape[1] // head):
        span = slice(index * head, (index + 1) * head)
        scores = dot_nt(query_low[:, span], keys) * query_scale
        scores = jnp.where(allowed, scores, MASKED)
        probs = jnp.exp(scores - log_total[:, index : index + 1])
        d_probs = dot_nt(d_heads[:, span], values)
        inner = jnp.sum(probs * d_probs, axis=-1, keepdims=True)
        d_scores = (probs * (d_probs - inner)).astype(BF16)
        d_query[:, span] = dot(d_scores, keys) * query_scale
        key_term = dot_tn(d_scores, query_low[:, span]) * query_scale
        value_term = dot_tn(probs.astype(BF16), d_heads[:, span])
        if index == 0:
            sum_keys[...] = key_term
            sum_values[...] = value_term
        else:
            sum_keys[...] += key_term
            sum_values[...] += value_term
    for target, start in ((d_far, 0), (d_near, rows), (d_own, 2 * rows)):
        target[:, :head] = sum_keys[start : start + rows, :].astype(target.dtype)
        target[:, head:] = sum_values[start : start + rows, :].astype(target.dtype)


def after_attention(
    core_ref, raw, d_query, d_own, near, far, weights, tok, gains, head_gains, cos, sin,
    d_state, gain_grads, tokens_grad, keep, send, low, loose,
):
    core = core_ref[0]
    width = tok.shape[1]
    q_cols, kv_cols = d_query.shape[1], d_own.shape[1]
    head = kv_cols // 2
    tiles = (q_cols + kv_cols) // LANES
    per, per_head = width // LANES, head // LANES
    chips = weights.shape[1] // per
    chunk = keep.shape[0] // chips
    cosine, minus_sine = cos[...], -sin[...]
    query_gain_grad = jnp.zeros((1, head), F32)
    for index in range(q_cols // head):
        span = slice(index * head, (index + 1) * head)
        unit, scale = normed(raw[:, span])
        cot = turned(d_query[:, span], cosine, minus_sine)
        d_raw, part = normed_back(cot, unit, scale, head_gains[0:1, :])
        query_gain_grad += part
        low[:, span] = d_raw.astype(BF16)
    d_kv = d_own[...] + near[...].astype(F32) + far[...].astype(F32)
    unit, scale = normed(raw[:, q_cols : q_cols + head])
    cot = turned(d_kv[:, :head], cosine, minus_sine)
    d_raw, key_gain_grad = normed_back(cot, unit, scale, head_gains[1:2, :])
    low[:, q_cols : q_cols + head] = d_raw.astype(BF16)
    low[:, q_cols + head :] = d_kv[:, head:].astype(BF16)

    selectors = [pick_core(width, chips, per, parity) for parity in (core, 1 - core)]
    d_low = jnp.zeros(tok.shape, F32)
    for which, selector in enumerate(selectors):
        part = dot_nt(low[...], weights[which])
        high = part.astype(BF16)
        rounding = (part - high.astype(F32)).astype(BF16)
        d_low += dot_nt(high, selector) + dot_nt(rounding, selector)
    unit, scale = normed(tok[...].astype(F32))
    d_norm, in_gain_grad = normed_back(d_low, unit, scale, gains[0:1, :])
    tokens_grad[...] = (d_state[...] + d_norm).astype(BF16)

    wide = jnp.zeros((LANES, width), F32)
    vectors = [in_gain_grad] + [gain_grads[i : i + 1, :] for i in range(1, 4)]
    for which, vector in enumerate(vectors):
        wide = jnp.where(gain_mask(which * per, per, LANES, width), vector, wide)
    narrow = jnp.zeros((LANES, head), F32)
    for which, vector in enumerate((query_gain_grad, key_gain_grad)):
        mask = gain_mask(4 * per + which * per_head, per_head, LANES, head)
        narrow = jnp.where(mask, vector, narrow)
    wide, narrow = wide.astype(BF16), narrow.astype(BF16)
    attn_low = (unit * gains[0:1, :]).astype(BF16)
    stride = chunk + ODD
    for row in range(per * tiles + 1, chunk):
        loose[pl.ds(row, chips, stride=stride), :] = jnp.zeros((chips, LANES), F32)
    for target, parity in ((keep, core), (send, 1 - core)):
        extra = dot(wide, pick_chip(width, chips, per, parity, lines=True)) + dot(
            narrow, pick_chip(head, chips, per_head, parity, lines=True)
        )
        selector = pick_core(width, chips, per, parity, lines=True)
        loose[pl.ds(per * tiles, chips, stride=stride), :] = jnp.transpose(extra)
        block = dot_tn(dot(attn_low, selector).astype(BF16), low[...])
        for row in range(per):
            for tile in range(tiles):
                loose[pl.ds(row * tiles + tile, chips, stride=stride), :] = block[
                    row * chips : (row + 1) * chips, tile * LANES : (tile + 1) * LANES
                ]
        for chip in range(chips):
            target[chip * chunk : (chip + 1) * chunk, :] = loose_chunk(loose, chip, chunk).astype(BF16)


def on_device(
    tokens,
    out_grad,
    seq_start,
    seq_len,
    w_query,
    w_key_value,
    w_output,
    w_gate_up,
    w_down,
    norm_attn_in,
    norm_attn_out,
    norm_mlp_in,
    norm_mlp_out,
    norm_query,
    norm_key,
):
    size = lax.axis_size("fsdp")
    chips = size // 2
    me = lax.axis_index("fsdp")
    core = me % 2
    core_arg = core.astype(jnp.int32).reshape(1)
    tok_rows, width = tokens.shape
    shard = w_query.shape[0]
    q_cols, kv_cols = w_query.shape[1], w_key_value.shape[1]
    qkv_cols = q_cols + kv_cols
    gu_cols, ff = w_gate_up.shape[1], w_down.shape[0] * size
    down_rows = w_down.shape[0]
    head = kv_cols // 2
    hshard = norm_query.shape[0]

    gathered = jnp.zeros((SLOTS, gu_cols + 3 * width), BF16)
    column = 0
    zero = jnp.zeros((), BF16)
    for part, first in ((w_gate_up, 0), (w_down, 0), (w_down, SLOTS), (w_output, 0)):
        high, wide = part.shape
        after = gathered.shape[1] - column - wide
        rows = (-first, SLOTS - high + first, 0)
        gathered = gathered + lax.pad(part, zero, (rows, (column, after, 0)))
        column += wide
    mlp_full = lax.all_gather(gathered, "fsdp", axis=0, tiled=True)

    tiles = qkv_cols // LANES
    chunk = 64
    gain_row = jnp.zeros((1, LANES), BF16)
    gain_count = 0
    for part in (norm_attn_in, norm_attn_out, norm_mlp_in, norm_mlp_out, norm_query, norm_key):
        wide = part.shape[0]
        gain_row = gain_row + jnp.pad(part[None], ((0, 0), (gain_count, LANES - gain_count - wide)))
        gain_count += wide
    pack = jnp.concatenate(
        [
            jnp.concatenate([w_query, w_key_value], axis=1).reshape(shard * tiles, LANES),
            jnp.pad(gain_row, ((0, chunk - shard * tiles - 1), (0, 0))),
        ],
        axis=0,
    )
    own = spread(pack).reshape(chips * chunk, LANES)
    peer = swap_cores(own)

    key_reach = (WINDOW + tok_rows - 2) // tok_rows
    first_token = me * tok_rows
    q_index, q_seq, q_pos, q_live = token_layout(seq_start, seq_len, first_token, tok_rows)
    k_index, k_seq, k_pos, k_live = token_layout(
        seq_start, seq_len, first_token - key_reach * tok_rows, (key_reach + 1) * tok_rows
    )
    live = q_live.astype(F32)[:, None]
    q_seq, k_seq = q_seq[:, None], k_seq[None, :]
    inv_freq = theta_base ** (-2.0 * jnp.arange(head // 2, dtype=F32) / head)
    angles = q_pos.astype(F32)[:, None] * inv_freq[None, :]
    cos_vals, sin_vals = jnp.cos(angles), jnp.sin(angles)

    raw, query_low, own_kv, gains, head_gains, attn_weights = call(
        before_attention,
        (
            shape((tok_rows, qkv_cols), F32),
            shape((tok_rows, q_cols), BF16),
            shape((tok_rows, kv_cols), BF16),
            shape((8, width), F32),
            shape((8, head), F32),
            shape((2, chips * shard, qkv_cols), BF16),
        ),
        (core_arg, tokens, own, peer, cos_vals, sin_vals),
        scratch=(pltpu.VMEM((chips * (chunk + ODD), LANES), F32),),
        specs=[SCALAR] + [WHOLE] * 5,
    )
    kv_near = shifted(own_kv, "fsdp", 1)
    kv_far = shifted(own_kv, "fsdp", 2)
    heads_low, log_total, spread_flat, spread_core = call(
        attention,
        (
            shape((tok_rows, q_cols), BF16),
            shape((tok_rows, LANES), F32),
            shape((width, size * SLOTS), BF16),
            shape((2, width, width // 2), BF16),
        ),
        (core_arg, query_low, kv_far, kv_near, own_kv, q_seq, k_seq),
        specs=[SCALAR] + [WHOLE] * 6,
        flops=20e9,
    )

    tile = 512
    blocks, strips = 8, chips // 8
    down_at = shard * gu_cols // LANES
    out_at = down_at + down_rows * (width // LANES)
    chunk_rows = out_at + 6 * SLOTS
    chunk_shape = (blocks, strips, chunk_rows, LANES)
    gain_grads, mixed, d_state, d_heads, low_own, d_gate_up, own_down, own_out, send = call(
        feed_forward,
        (
            shape((8, width), F32),
            shape((tok_rows, width), BF16),
            shape((tok_rows, width), F32),
            shape((tok_rows, q_cols), BF16),
            shape((tok_rows, width // 2), BF16),
            shape((tok_rows, gu_cols), BF16),
            shape((blocks, strips, out_at - down_at, LANES), BF16),
            shape((blocks, strips, 6 * SLOTS, LANES), BF16),
            shape(chunk_shape, BF16),
        ),
        (
            core_arg, live, gains, tokens, out_grad, heads_low, spread_flat, spread_core, mlp_full,
        ),
        scratch=(
            pltpu.VMEM((gu_cols // tile, size * SLOTS, tile), BF16),
            pltpu.VMEM((size * SLOTS, 3 * width), BF16),
            pltpu.VMEM((ff, width), BF16),
            pltpu.VMEM((tok_rows, ff), F32),
            pltpu.VMEM((tok_rows, ff), F32),
            pltpu.VMEM((tok_rows, ff), BF16),
            pltpu.VMEM((tok_rows, width), F32),
            pltpu.VMEM((tok_rows, width), F32),
            pltpu.VMEM((tok_rows, width), F32),
            pltpu.VMEM((tok_rows, size * SLOTS), F32),
            pltpu.VMEM((tok_rows, size * SLOTS), BF16),
            pltpu.VMEM((tok_rows, width), BF16),
            pltpu.VMEM((width // 2, tok_rows), BF16),
            pltpu.VMEM((tok_rows, width), BF16),
            pltpu.VMEM((chips * (down_at + ODD), LANES), F32),
            pltpu.VMEM((blocks, strips, 2, SLOTS, width), F32),
            pltpu.VMEM((tile // (2 * down_rows) // strips, strips, 2, down_rows, width), BF16),
            pltpu.VMEM((width, size * SLOTS), BF16),
            pltpu.VMEM((2, width, width // 2), BF16),
            pltpu.VMEM((tok_rows, width), BF16),
            pltpu.VMEM((tok_rows, width), F32),
            pltpu.VMEM((tok_rows, q_cols), BF16),
            pltpu.VMEM((tok_rows, width // 2), BF16),
            pltpu.VMEM((tok_rows, gu_cols), BF16),
            pltpu.VMEM((blocks, strips, out_at - down_at, LANES), BF16),
            pltpu.VMEM((blocks, strips, 6 * SLOTS, LANES), BF16),
            pltpu.VMEM(chunk_shape, BF16),
            pltpu.VMEM((tok_rows, width), BF16),
            pltpu.VMEM((tok_rows, width), BF16),
            pltpu.VMEM((tok_rows, q_cols), BF16),
            pltpu.SemaphoreType.DMA((gu_cols // tile,)),
            pltpu.SemaphoreType.DMA((7,)),
            pltpu.SemaphoreType.DMA((9,)),
        ),
        specs=[SCALAR] + [WHOLE] * 2 + [AWAY] * 6,
        out_specs=(WHOLE,) + (AWAY,) * 8,
        flops=12e9,
    )
    arrived = swap_cores(send)

    d_query, d_own, d_near, d_far = call(
        attention_back,
        (
            shape((tok_rows, q_cols), F32),
            shape((tok_rows, kv_cols), F32),
            shape((tok_rows, kv_cols), BF16),
            shape((tok_rows, kv_cols), BF16),
        ),
        (query_low, kv_far, kv_near, own_kv, d_heads, log_total, q_seq, k_seq),
        scratch=(
            pltpu.VMEM(((key_reach + 1) * tok_rows, head), F32),
            pltpu.VMEM(((key_reach + 1) * tok_rows, head), F32),
        ),
        specs=[WHOLE] * 8,
        flops=20e9,
    )
    near = shifted(d_near, "fsdp", -1)
    far = shifted(d_far, "fsdp", -2)
    arrived, far_started = lax.optimization_barrier((arrived, d_far))
    both_mlp = call(
        own_gradients,
        shape(chunk_shape, BF16),
        (low_own, d_gate_up, own_down, own_out, arrived),
        scratch=(
            pltpu.VMEM(chunk_shape, BF16),
            pltpu.VMEM(chunk_shape, BF16),
            pltpu.VMEM((tok_rows, gu_cols), BF16),
            pltpu.VMEM((blocks, strips, out_at - down_at, LANES), BF16),
            pltpu.VMEM((blocks, strips, 6 * SLOTS, LANES), BF16),
            pltpu.VMEM((width // 2, tok_rows), BF16),
            pltpu.VMEM((chips * (down_at + ODD), LANES), F32),
            pltpu.SemaphoreType.DMA((gu_cols // tile,)),
            pltpu.SemaphoreType.DMA((2,)),
            pltpu.SemaphoreType.DMA((blocks,)),
            pltpu.SemaphoreType.DMA((blocks,)),
        ),
        specs=[WHOLE] + [AWAY] * 4,
        out_specs=AWAY,
        flops=12e9,
        vmem=62 * 1024 * 1024,
    )
    both_mlp, near, far = lax.optimization_barrier((both_mlp, near, far))
    mlp_parts = exchange(both_mlp.reshape(chips, chunk_rows, LANES))
    tokens_grad, keep, send = call(
        after_attention,
        (
            shape((tok_rows, width), BF16),
            shape((chips * chunk, LANES), BF16),
            shape((chips * chunk, LANES), BF16),
        ),
        (
            core_arg, raw, d_query, d_own, near, far, attn_weights, tokens, gains,
            head_gains, cos_vals, sin_vals, d_state, gain_grads,
        ),
        scratch=(
            pltpu.VMEM((tok_rows, qkv_cols), BF16),
            pltpu.VMEM((chips * (chunk + ODD), LANES), F32),
        ),
        specs=[SCALAR] + [WHOLE] * 13,
        flops=20e9,
        vmem=62 * 1024 * 1024,
    )
    both = (keep.astype(F32) + swap_cores(send).astype(F32)).astype(BF16)
    line = lax.psum_scatter(
        both, "fsdp", scatter_dimension=0, axis_index_groups=line_groups(size), tiled=True
    )
    line, mlp_parts = lax.optimization_barrier((line, mlp_parts))
    attn_parts = lax.all_to_all(
        line.reshape(chips // LINE, chunk, LANES),
        "fsdp",
        split_axis=0,
        concat_axis=0,
        tiled=True,
        axis_index_groups=plane_groups(size),
    )
    share_attn = jnp.sum(attn_parts.astype(F32), axis=0)
    share_qkv = share_attn[: shard * tiles].reshape(shard, tiles * LANES)
    share_gains = share_attn[shard * tiles, :gain_count]

    share_mlp = jnp.sum(mlp_parts.astype(F32), axis=0)
    share_gate_up = share_mlp[:down_at].reshape(shard, gu_cols)
    share_down = (
        share_mlp[down_at:out_at]
        .reshape(width // LANES, down_rows, LANES)
        .transpose(1, 0, 2)
        .reshape(down_rows, width)
    )
    share_output = (
        share_mlp[out_at : out_at + SLOTS * (width // LANES)]
        .reshape(width // LANES, SLOTS, LANES)
        .transpose(1, 0, 2)
        .reshape(SLOTS, width)
    )
    return (
        mixed,
        tokens_grad,
        share_qkv[:, :q_cols],
        share_qkv[:, q_cols:],
        share_output,
        share_gate_up,
        share_down,
        share_gains[:shard],
        share_gains[shard : 2 * shard],
        share_gains[2 * shard : 3 * shard],
        share_gains[3 * shard : 4 * shard],
        share_gains[4 * shard : 4 * shard + hshard],
        share_gains[4 * shard + hshard :],
    )


def solution(mesh):
    placed = (
        P("fsdp", None),
        P("fsdp", None),
        P(),
        P(),
        P("fsdp", None),
        P("fsdp", None),
        P("fsdp", None),
        P("fsdp", None),
        P("fsdp", None),
        P("fsdp"),
        P("fsdp"),
        P("fsdp"),
        P("fsdp"),
        P("fsdp"),
        P("fsdp"),
    )
    return jax.shard_map(
        on_device,
        mesh=mesh,
        in_specs=placed,
        out_specs=(
            P("fsdp", None),
            P("fsdp", None),
            P("fsdp", None),
            P("fsdp", None),
            P("fsdp", None),
            P("fsdp", None),
            P("fsdp", None),
            P("fsdp"),
            P("fsdp"),
            P("fsdp"),
            P("fsdp"),
            P("fsdp"),
            P("fsdp"),
        ),
        check_vma=False,
    )
```

```python
import jax
import jax.numpy as jnp
from jax import lax
from jax.experimental import pallas as pl
from jax.experimental.pallas import tpu as pltpu
from jax.sharding import PartitionSpec as P

WINDOW = 512


epsilon = 1e-06
theta_base = 10000.0
query_scale = 0.0625


def shifted(block, axis, distance):
    devices = range(lax.axis_size(axis))
    route = [(i - distance, i) for i in devices if i - distance in devices]
    return lax.ppermute(block, axis, route)


def token_layout(seq_start, seq_len, first_token, token_count):
    indices = first_token + jnp.arange(token_count, dtype=jnp.int32)
    offsets = indices[:, None] - seq_start[None, :]
    inside = (offsets >= 0) & (offsets < seq_len[None, :])
    live_mask = jnp.any(inside, axis=1)
    seq_numbers = jnp.arange(seq_start.shape[0], dtype=jnp.int32)
    seq_id = jnp.sum(jnp.where(inside, seq_numbers[None, :], 0), axis=1)
    seq_id = jnp.where(live_mask, seq_id, -1)
    positions = jnp.sum(jnp.where(inside, offsets, 0), axis=1)
    return (indices, seq_id, positions, live_mask)


BF16 = jnp.bfloat16
F32 = jnp.float32
SLOTS = 8
MASKED = -1e30
ODD = 1
VMEM_BYTES = 56 * 1024 * 1024
LANES = 128


def same_core_groups(size):
    return [[2 * chip + core for chip in range(size // 2)] for core in range(2)]


LINE = 4


def line_groups(size):
    planes = size // 2 // LINE
    return [
        [2 * (plane * LINE + x) + core for x in range(LINE)]
        for plane in range(planes)
        for core in range(2)
    ]


def plane_groups(size):
    planes = size // 2 // LINE
    return [
        [2 * (plane * LINE + x) + core for plane in range(planes)]
        for x in range(LINE)
        for core in range(2)
    ]


def line_first(place, chips):
    planes = chips // LINE
    return lax.rem(place, planes) * LINE + lax.div(place, planes)


def swap_cores(block):
    size = lax.axis_size("fsdp")
    return lax.ppermute(block, "fsdp", [(i, i ^ 1) for i in range(size)])


def exchange(blocks):
    return lax.all_to_all(
        blocks,
        "fsdp",
        split_axis=0,
        concat_axis=0,
        tiled=True,
        axis_index_groups=same_core_groups(lax.axis_size("fsdp")),
    )


def spread(block):
    chips = lax.axis_size("fsdp") // 2
    return exchange(jnp.broadcast_to(block[None], (chips,) + block.shape))


def call(kernel, outs, ins, scratch=(), specs=None, flops=4e9, out_specs=None, vmem=VMEM_BYTES):
    return pl.pallas_call(
        kernel,
        out_shape=outs,
        in_specs=specs,
        **({} if out_specs is None else {"out_specs": out_specs}),
        scratch_shapes=list(scratch),
        compiler_params=pltpu.CompilerParams(vmem_limit_bytes=vmem),
        cost_estimate=pl.CostEstimate(
            flops=int(flops), bytes_accessed=8_000_000, transcendentals=0
        ),
    )(*ins)


SCALAR = pl.BlockSpec(memory_space=pltpu.SMEM)
WHOLE = pl.BlockSpec(memory_space=pltpu.VMEM)
AWAY = pl.BlockSpec(memory_space=pl.ANY)


def shape(dims, kind):
    return jax.ShapeDtypeStruct(dims, kind)


def dot(left, right):
    return jnp.dot(left, right, preferred_element_type=F32)


def dot_nt(left, right):
    return lax.dot_general(left, right, (((1,), (1,)), ((), ())), preferred_element_type=F32)


def dot_tn(left, right):
    return lax.dot_general(left, right, (((0,), (0,)), ((), ())), preferred_element_type=F32)


def normed(values):
    scale = lax.rsqrt(jnp.mean(values * values, axis=-1, keepdims=True) + epsilon)
    return values * scale, scale


def normed_back(cot, unit, scale, gain):
    weighted = cot * gain
    inner = jnp.mean(weighted * unit, axis=-1, keepdims=True)
    return scale * (weighted - unit * inner), jnp.sum(cot * unit, axis=0, keepdims=True)


def ones_where(mask):
    return jnp.where(mask, 1.0, 0.0).astype(BF16)


def pick_flat(rows, count, per):
    place = lax.broadcasted_iota(jnp.int32, (1, count), 1)
    device, slot = lax.shift_right_logical(place, 3), place & (SLOTS - 1)
    source = jnp.where(slot < per, device * per + slot, -1)
    return ones_where(lax.broadcasted_iota(jnp.int32, (rows, count), 0) == source)


def pick_core(rows, chips, per, core, lines=False):
    place = lax.broadcasted_iota(jnp.int32, (1, chips * per), 1)
    row, chip = lax.div(place, chips), lax.rem(place, chips)
    if lines:
        chip = line_first(chip, chips)
    source = (2 * chip + core) * per + row
    return ones_where(lax.broadcasted_iota(jnp.int32, (rows, chips * per), 0) == source)


def pick_chip(rows, chips, per, core, lines=False):
    chip = lax.broadcasted_iota(jnp.int32, (1, chips), 1)
    if lines:
        chip = line_first(chip, chips)
    low = (2 * chip + core) * per
    natural = lax.broadcasted_iota(jnp.int32, (rows, chips), 0)
    return ones_where((natural >= low) & (natural < low + per))


def gain_mask(first, per, rows, columns):
    row = lax.broadcasted_iota(jnp.int32, (rows, columns), 0)
    column = lax.broadcasted_iota(jnp.int32, (rows, columns), 1)
    return row == first + lax.rem(column, per)


def turned(values, cos, sin):
    half = values.shape[-1] // 2
    first, second = values[:, :half], values[:, half:]
    return jnp.concatenate([first * cos - second * sin, second * cos + first * sin], axis=1)


def before_attention(
    core_ref, tok, own, peer, cos, sin, raw, query_low, own_kv, gains, head_gains, weights, loose
):
    core = core_ref[0]
    width = tok.shape[1]
    kv_cols = own_kv.shape[1]
    head = kv_cols // 2
    q_cols = query_low.shape[1]
    columns = q_cols + kv_cols
    tiles = columns // LANES
    per, per_head = width // LANES, head // LANES
    chips = weights.shape[1] // per
    chunk = own.shape[0] // chips
    wide = jnp.zeros((width, LANES), F32)
    narrow = jnp.zeros((head, LANES), F32)
    stride = chunk + ODD
    for which, (block, parity) in enumerate(((own, core), (peer, 1 - core))):
        for chip in range(chips):
            loose[chip * stride : chip * stride + chunk, :] = block[
                chip * chunk : (chip + 1) * chunk, :
            ].astype(F32)
        for row in range(per):
            for tile in range(tiles):
                weights[
                    which, row * chips : (row + 1) * chips, tile * LANES : (tile + 1) * LANES
                ] = loose[pl.ds(row * tiles + tile, chips, stride=stride), :].astype(BF16)
        found = loose[pl.ds(per * tiles, chips, stride=stride), :].astype(BF16)
        wide += dot(pick_chip(width, chips, per, parity), found)
        narrow += dot(pick_chip(head, chips, per_head, parity), found)
    wide, narrow = jnp.transpose(wide)[:32], jnp.transpose(narrow)[:32]
    for which in range(4):
        mask = gain_mask(which * per, per, 32, width)
        gains[which : which + 1, :] = jnp.sum(jnp.where(mask, wide, 0.0), 0, keepdims=True)
    for which in range(2):
        mask = gain_mask(4 * per + which * per_head, per_head, 32, head)
        head_gains[which : which + 1, :] = jnp.sum(jnp.where(mask, narrow, 0.0), 0, keepdims=True)
    unit, _ = normed(tok[...].astype(F32))
    low = (unit * gains[0:1, :]).astype(BF16)
    raw[...] = dot(dot(low, pick_core(width, chips, per, core)).astype(BF16), weights[0]) + dot(
        dot(low, pick_core(width, chips, per, 1 - core)).astype(BF16), weights[1]
    )
    for index in range(q_cols // head):
        span = slice(index * head, (index + 1) * head)
        unit, _ = normed(raw[:, span])
        query_low[:, span] = turned(unit * head_gains[0:1, :], cos[...], sin[...]).astype(BF16)
    unit, _ = normed(raw[:, q_cols : q_cols + head])
    own_kv[:, :head] = turned(unit * head_gains[1:2, :], cos[...], sin[...]).astype(BF16)
    own_kv[:, head:] = raw[:, q_cols + head :].astype(BF16)


def visible(q_seq, k_seq):
    queries, keys = q_seq.shape[0], k_seq.shape[1]
    row = lax.broadcasted_iota(jnp.int32, (queries, keys), 0)
    column = lax.broadcasted_iota(jnp.int32, (queries, keys), 1)
    distance = row - column + (keys - queries)
    same = (q_seq[...] == k_seq[...]) & (q_seq[...] >= 0)
    return (same & (distance >= 0) & (distance < WINDOW)) | (distance == 0)


def attention(
    core_ref, query_low, kv_far, kv_near, kv_own, q_seq, k_seq,
    heads_low, log_total, spread_flat, spread_core,
):
    core = core_ref[0]
    width, per_core = spread_core.shape[1:]
    per = width // LANES
    spread_flat[...] = pick_flat(width, spread_flat.shape[1], per)
    for which, parity in enumerate((core, 1 - core)):
        spread_core[which] = pick_core(width, per_core // per, per, parity)
    head = kv_own.shape[1] // 2
    parts = (kv_far, kv_near, kv_own)
    keys = jnp.concatenate([part[:, :head] for part in parts], axis=0)
    values = jnp.concatenate([part[:, head:] for part in parts], axis=0)
    allowed = visible(q_seq, k_seq)
    for index in range(query_low.shape[1] // head):
        span = slice(index * head, (index + 1) * head)
        scores = dot_nt(query_low[:, span], keys) * query_scale
        scores = jnp.where(allowed, scores, MASKED)
        top = jnp.max(scores, axis=-1, keepdims=True)
        terms = jnp.exp(scores - top)
        total = jnp.sum(terms, axis=-1, keepdims=True)
        probs = (terms * (1.0 / total)).astype(BF16)
        heads_low[:, span] = dot(probs, values).astype(BF16)
        log_total[:, index : index + 1] = top + jnp.log(total)


def feed_forward(
    core_ref, live, gains, tok_in, out_grad_in, heads_in, spread_flat_in, spread_core_in, full,
    gain_grads, mixed_out, d_state_out, d_heads_out, low_own_out, d_gate_up_out, own_down_out,
    own_out_out, send_out,
    weights, rest, down, act, act_slope, hidden, proj, state, total, back, low_flat, low, turned_low,
    low_branch, loose, loose_out, turn_down, spread_flat, spread_core, mixed, d_state, d_heads,
    low_own, d_gate_up, own_down, own_out, send, tok, out_grad, heads_low,
    weight_sem, rest_sem, out_sem,
):
    core = core_ref[0]
    tiles, tile = weights.shape[0], weights.shape[2]
    half = tiles // 2
    width = state.shape[1]
    q_cols = heads_low.shape[1]
    per = width // LANES
    blocks, strips, down_rows = send.shape[0], send.shape[1], turn_down.shape[3]
    chips = blocks * strips
    tile_chips = tile // (2 * down_rows)
    tile_rows = tile // down_rows * SLOTS
    columns_at = tiles * tile

    def weight_copy(index):
        return pltpu.make_async_copy(
            full.at[:, pl.ds(pl.multiple_of(index * tile, tile), tile)],
            weights.at[index],
            weight_sem.at[index],
        )

    def rest_copy(which, first, last):
        return pltpu.make_async_copy(
            full.at[:, columns_at + first : columns_at + last],
            rest.at[:, first:last],
            rest_sem.at[which],
        )

    out_copy = rest_copy(0, 2 * width, 3 * width)
    down_copy = rest_copy(1, 0, 2 * width)
    flat_copy = pltpu.make_async_copy(spread_flat_in, spread_flat, rest_sem.at[2])
    core_copy = pltpu.make_async_copy(spread_core_in, spread_core, rest_sem.at[3])
    heads_copy = pltpu.make_async_copy(heads_in, heads_low, rest_sem.at[4])
    tok_copy = pltpu.make_async_copy(tok_in, tok, rest_sem.at[5])
    grad_copy = pltpu.make_async_copy(out_grad_in, out_grad, rest_sem.at[6])
    heads_copy.start()
    out_copy.start()
    tok_copy.start()
    flat_copy.start()
    down_copy.start()
    for index in range(half):
        weight_copy(index).start()
        weight_copy(half + index).start()
    core_copy.start()
    grad_copy.start()
    leaving = []

    def leave(source, target):
        leaving.append(pltpu.make_async_copy(source, target, out_sem.at[len(leaving)]))
        leaving[-1].start()

    heads_copy.wait()
    out_copy.wait()
    w_out = rest[:, 2 * width :]
    proj[...] = dot(heads_low[...], w_out)
    tok_copy.wait()
    unit, _ = normed(proj[...])
    state[...] = tok[...].astype(F32) + unit * gains[1:2, :]
    unit, scale = normed(state[...])
    low[...] = (unit * gains[2:3, :]).astype(BF16)
    flat_copy.wait()
    low_flat[...] = dot(low[...], spread_flat[...]).astype(BF16)
    total[...] = jnp.zeros_like(total)
    down_copy.wait()

    def down_tile(index):
        return down[pl.ds(pl.multiple_of(index * tile, tile), tile)]

    def forward(index, carry):
        columns = pl.ds(pl.multiple_of(index * tile, tile), tile)
        stored = rest[pl.ds(pl.multiple_of(index * tile_rows, tile_rows), tile_rows), : 2 * width]
        stored = stored.astype(F32).reshape(tile_rows // SLOTS, SLOTS, 2 * width)
        down[pl.ds(pl.multiple_of(index * tile, tile), tile)] = (
            jnp.concatenate([stored[:, :, :width], stored[:, :, width:]], axis=1)
            .reshape(tile, width)
            .astype(BF16)
        )
        weight_copy(index).wait()
        weight_copy(half + index).wait()
        gate = dot(low_flat[...], weights[index])
        up = dot(low_flat[...], weights[half + index])
        square = gate * gate
        bend = jnp.tanh(gate * (0.7978845608028654 * (1.0 + 0.044715 * square)))
        rise = 0.5 * (1.0 + bend)
        gelu = gate * rise
        slope = rise + 0.5 * gate * (1.0 - bend * bend) * (
            0.7978845608028654 * (1.0 + 0.134145 * square)
        )
        act[:, columns] = gelu
        act_slope[:, columns] = up * slope
        hidden[:, columns] = (gelu * up).astype(BF16)
        total[...] += dot(hidden[:, columns], down_tile(index))
        return carry

    lax.fori_loop(0, half, forward, 0, unroll=True)
    core_copy.wait()
    low_own[...] = dot(low[...], spread_core[0]).astype(BF16)
    turned_low[...] = jnp.transpose(dot(low[...], spread_core[1])).astype(BF16)
    leave(low_own, low_own_out)

    branch_unit, branch_scale = normed(total[...])
    mixed[...] = ((state[...] + branch_unit * gains[3:4, :]) * live[...]).astype(BF16)
    leave(mixed, mixed_out)
    grad_copy.wait()
    cotangent = out_grad[...].astype(F32) * live[...]
    d_branch, gain_grads[3:4, :] = normed_back(
        cotangent, branch_unit, branch_scale, gains[3:4, :]
    )
    low_branch[...] = d_branch.astype(BF16)
    back[...] = jnp.zeros_like(back)

    row_tiles = tiles * tile // LANES
    chunk = per * row_tiles

    def place(start, grad):
        place_rows(loose, dot(turned_low[...], grad), start, per, chips, row_tiles)

    down_at = chunk
    out_at = down_at + down_rows * (width // LANES)

    def backward(index, carry):
        columns = pl.ds(pl.multiple_of(index * tile, tile), tile)
        d_hidden = dot_nt(low_branch[...], down_tile(index))
        d_gate = (d_hidden * act_slope[:, columns]).astype(BF16)
        d_up = (d_hidden * act[:, columns]).astype(BF16)
        d_gate_up[:, columns] = d_gate
        d_gate_up[:, pl.ds(pl.multiple_of((half + index) * tile, tile), tile)] = d_up
        back[...] += dot_nt(d_gate, weights[index]) + dot_nt(d_up, weights[half + index])
        place(index * (tile // LANES), d_gate)
        place((half + index) * (tile // LANES), d_up)
        turn_down[...] = (
            dot_tn(hidden[:, columns], low_branch[...])
            .astype(BF16)
            .reshape(tile_chips // strips, strips, 2, down_rows, width)
        )
        tall = pl.ds(index * (tile_chips // strips), tile_chips // strips)
        for part in range(width // LANES):
            top = part * down_rows
            lanes = slice(part * LANES, (part + 1) * LANES)
            own_down[tall, :, top : top + down_rows, :] = turn_down[:, :, core, :, lanes]
            send[tall, :, down_at + top : down_at + top + down_rows, :] = turn_down[
                :, :, 1 - core, :, lanes
            ]
        return carry

    lax.fori_loop(0, half, backward, 0, unroll=True)
    leave(d_gate_up, d_gate_up_out)
    leave(own_down, own_down_out)

    def pack(block, carry):
        for strip in range(strips):
            send[block, strip, :chunk, :] = loose_chunk(loose, block * strips + strip, chunk).astype(
                BF16
            )
        return carry

    lax.fori_loop(0, blocks, pack, 0)
    leave(send.at[:, :, :out_at, :], send_out.at[:, :, :out_at, :])

    d_low = dot_nt(back[...].astype(BF16), spread_flat[...])
    d_norm, gain_grads[2:3, :] = normed_back(d_low, unit, scale, gains[2:3, :])
    d_state[...] = cotangent + d_norm
    leave(d_state, d_state_out)
    proj_unit, proj_scale = normed(proj[...])
    d_proj, gain_grads[1:2, :] = normed_back(d_state[...], proj_unit, proj_scale, gains[1:2, :])
    proj_low = d_proj.astype(BF16)
    loose_out[...] = dot_tn(heads_low[...], proj_low).reshape(blocks, strips, 2, SLOTS, width)
    out_tiles = width // LANES
    for target, parity, start in ((own_out, core, 0), (send, 1 - core, out_at)):
        for part in range(out_tiles // 2 + 1):
            lanes = [slice(i * LANES, (i + 1) * LANES) for i in (2 * part, 2 * part + 1)]
            pair = [
                loose_out[:, :, parity, :, lane]
                if lane.stop <= width
                else jnp.zeros((blocks, strips, SLOTS, LANES), F32)
                for lane in lanes
            ]
            top = start + 2 * part * SLOTS
            target[:, :, top : top + 2 * SLOTS, :] = jnp.concatenate(pair, axis=2).astype(BF16)
    leave(own_out, own_out_out)
    leave(send.at[:, :, out_at:, :], send_out.at[:, :, out_at:, :])
    d_heads[...] = dot_nt(proj_low, w_out).astype(BF16)
    leave(d_heads, d_heads_out)
    for copy in leaving:
        copy.wait()


def place_rows(loose, block, start, per, chips, row_tiles):
    stride = per * row_tiles + ODD
    for row in range(per):
        for part in range(block.shape[1] // LANES):
            loose[pl.ds(row * row_tiles + start + part, chips, stride=stride), :] = block[
                row * chips : (row + 1) * chips, part * LANES : (part + 1) * LANES
            ]


def loose_rows(chips, chunk):
    return -(-(chips + 1) * (chunk + ODD) // SLOTS) * SLOTS


def loose_chunk(loose, chip, chunk):
    return loose[pl.ds(chip * (chunk + ODD), chunk), :]


def own_gradients(
    low_own, d_gate_up_in, own_down_in, own_out_in, arrived, both_out,
    both, other, d_gate_up, own_down, own_out, turned_low, loose, tile_sem, in_sem, arrived_sem, both_sem,
):
    tile = 512
    steps = d_gate_up.shape[1] // tile

    def tile_copy(index):
        span = pl.ds(pl.multiple_of(index * tile, tile), tile)
        return pltpu.make_async_copy(
            d_gate_up_in.at[:, span], d_gate_up.at[:, span], tile_sem.at[index]
        )

    for index in range(steps):
        tile_copy(index).start()
    copies = [
        pltpu.make_async_copy(own_down_in, own_down, in_sem.at[0]),
        pltpu.make_async_copy(own_out_in, own_out, in_sem.at[1]),
    ]

    def arrival(block):
        return pltpu.make_async_copy(arrived.at[block], other.at[block], arrived_sem.at[block])

    for copy in copies:
        copy.start()
    blocks, strips, down_size = own_down.shape[:3]
    for block in range(blocks):
        arrival(block).start()
    chips = blocks * strips
    per = low_own.shape[1] // chips
    row_tiles = d_gate_up.shape[1] // LANES
    chunk = per * row_tiles
    turned_low[...] = jnp.transpose(low_own[...].astype(F32)).astype(BF16)

    def place(index, carry):
        tile_copy(index).wait()
        grad = d_gate_up[:, pl.ds(pl.multiple_of(index * tile, tile), tile)]
        block = dot(turned_low[...], grad)
        place_rows(loose, block, index * (tile // LANES), per, chips, row_tiles)
        return carry

    lax.fori_loop(0, steps, place, 0)
    for copy in copies:
        copy.wait()

    def leave(block):
        return pltpu.make_async_copy(both.at[block], both_out.at[block], both_sem.at[block])

    def pack(block, carry):
        arrival(block).wait()
        for strip in range(strips):
            both[block, strip, :chunk, :] = (
                loose_chunk(loose, block * strips + strip, chunk)
                + other[block, strip, :chunk, :].astype(F32)
            ).astype(BF16)
        low, high = chunk, chunk + down_size
        both[block, :, low:high, :] = (
            own_down[block].astype(F32) + other[block, :, low:high, :].astype(F32)
        ).astype(BF16)
        both[block, :, high:, :] = (
            own_out[block].astype(F32) + other[block, :, high:, :].astype(F32)
        ).astype(BF16)
        leave(block).start()
        return carry

    lax.fori_loop(0, blocks, pack, 0)
    for block in range(blocks):
        leave(block).wait()


def attention_back(
    query_low, kv_far, kv_near, kv_own, d_heads, log_total, q_seq, k_seq,
    d_query, d_own, d_near, d_far, sum_keys, sum_values,
):
    head = kv_own.shape[1] // 2
    rows = kv_own.shape[0]
    parts = (kv_far, kv_near, kv_own)
    keys = jnp.concatenate([part[:, :head] for part in parts], axis=0)
    values = jnp.concatenate([part[:, head:] for part in parts], axis=0)
    allowed = visible(q_seq, k_seq)
    for index in range(query_low.shape[1] // head):
        span = slice(index * head, (index + 1) * head)
        scores = dot_nt(query_low[:, span], keys) * query_scale
        scores = jnp.where(allowed, scores, MASKED)
        probs = jnp.exp(scores - log_total[:, index : index + 1])
        d_probs = dot_nt(d_heads[:, span], values)
        inner = jnp.sum(probs * d_probs, axis=-1, keepdims=True)
        d_scores = (probs * (d_probs - inner)).astype(BF16)
        d_query[:, span] = dot(d_scores, keys) * query_scale
        key_term = dot_tn(d_scores, query_low[:, span]) * query_scale
        value_term = dot_tn(probs.astype(BF16), d_heads[:, span])
        if index == 0:
            sum_keys[...] = key_term
            sum_values[...] = value_term
        else:
            sum_keys[...] += key_term
            sum_values[...] += value_term
    for target, start in ((d_far, 0), (d_near, rows), (d_own, 2 * rows)):
        target[:, :head] = sum_keys[start : start + rows, :].astype(target.dtype)
        target[:, head:] = sum_values[start : start + rows, :].astype(target.dtype)


def after_attention(
    core_ref, raw, d_query, d_own, near, far, weights, tok, gains, head_gains, cos, sin,
    d_state, gain_grads, tokens_grad, keep, send, low, loose,
):
    core = core_ref[0]
    width = tok.shape[1]
    q_cols, kv_cols = d_query.shape[1], d_own.shape[1]
    head = kv_cols // 2
    tiles = (q_cols + kv_cols) // LANES
    per, per_head = width // LANES, head // LANES
    chips = weights.shape[1] // per
    chunk = keep.shape[0] // chips
    cosine, minus_sine = cos[...], -sin[...]
    query_gain_grad = jnp.zeros((1, head), F32)
    for index in range(q_cols // head):
        span = slice(index * head, (index + 1) * head)
        unit, scale = normed(raw[:, span])
        cot = turned(d_query[:, span], cosine, minus_sine)
        d_raw, part = normed_back(cot, unit, scale, head_gains[0:1, :])
        query_gain_grad += part
        low[:, span] = d_raw.astype(BF16)
    d_kv = d_own[...] + near[...].astype(F32) + far[...].astype(F32)
    unit, scale = normed(raw[:, q_cols : q_cols + head])
    cot = turned(d_kv[:, :head], cosine, minus_sine)
    d_raw, key_gain_grad = normed_back(cot, unit, scale, head_gains[1:2, :])
    low[:, q_cols : q_cols + head] = d_raw.astype(BF16)
    low[:, q_cols + head :] = d_kv[:, head:].astype(BF16)

    selectors = [pick_core(width, chips, per, parity) for parity in (core, 1 - core)]
    d_low = jnp.zeros(tok.shape, F32)
    for which, selector in enumerate(selectors):
        part = dot_nt(low[...], weights[which])
        high = part.astype(BF16)
        rounding = (part - high.astype(F32)).astype(BF16)
        d_low += dot_nt(high, selector) + dot_nt(rounding, selector)
    unit, scale = normed(tok[...].astype(F32))
    d_norm, in_gain_grad = normed_back(d_low, unit, scale, gains[0:1, :])
    tokens_grad[...] = (d_state[...] + d_norm).astype(BF16)

    wide = jnp.zeros((LANES, width), F32)
    vectors = [in_gain_grad] + [gain_grads[i : i + 1, :] for i in range(1, 4)]
    for which, vector in enumerate(vectors):
        wide = jnp.where(gain_mask(which * per, per, LANES, width), vector, wide)
    narrow = jnp.zeros((LANES, head), F32)
    for which, vector in enumerate((query_gain_grad, key_gain_grad)):
        mask = gain_mask(4 * per + which * per_head, per_head, LANES, head)
        narrow = jnp.where(mask, vector, narrow)
    wide, narrow = wide.astype(BF16), narrow.astype(BF16)
    attn_low = (unit * gains[0:1, :]).astype(BF16)
    stride = chunk + ODD
    for row in range(per * tiles + 1, chunk):
        loose[pl.ds(row, chips, stride=stride), :] = jnp.zeros((chips, LANES), F32)
    for target, parity in ((keep, core), (send, 1 - core)):
        extra = dot(wide, pick_chip(width, chips, per, parity, lines=True)) + dot(
            narrow, pick_chip(head, chips, per_head, parity, lines=True)
        )
        selector = pick_core(width, chips, per, parity, lines=True)
        loose[pl.ds(per * tiles, chips, stride=stride), :] = jnp.transpose(extra)
        block = dot_tn(dot(attn_low, selector).astype(BF16), low[...])
        for row in range(per):
            for tile in range(tiles):
                loose[pl.ds(row * tiles + tile, chips, stride=stride), :] = block[
                    row * chips : (row + 1) * chips, tile * LANES : (tile + 1) * LANES
                ]
        for chip in range(chips):
            target[chip * chunk : (chip + 1) * chunk, :] = loose_chunk(loose, chip, chunk).astype(BF16)


def on_device(
    tokens,
    out_grad,
    seq_start,
    seq_len,
    w_query,
    w_key_value,
    w_output,
    w_gate_up,
    w_down,
    norm_attn_in,
    norm_attn_out,
    norm_mlp_in,
    norm_mlp_out,
    norm_query,
    norm_key,
):
    size = lax.axis_size("fsdp")
    chips = size // 2
    me = lax.axis_index("fsdp")
    core = me % 2
    core_arg = core.astype(jnp.int32).reshape(1)
    tok_rows, width = tokens.shape
    shard = w_query.shape[0]
    q_cols, kv_cols = w_query.shape[1], w_key_value.shape[1]
    qkv_cols = q_cols + kv_cols
    gu_cols, ff = w_gate_up.shape[1], w_down.shape[0] * size
    down_rows = w_down.shape[0]
    head = kv_cols // 2
    hshard = norm_query.shape[0]

    gathered = jnp.zeros((SLOTS, gu_cols + 3 * width), BF16)
    column = 0
    zero = jnp.zeros((), BF16)
    for part, first in ((w_gate_up, 0), (w_down, 0), (w_down, SLOTS), (w_output, 0)):
        high, wide = part.shape
        after = gathered.shape[1] - column - wide
        rows = (-first, SLOTS - high + first, 0)
        gathered = gathered + lax.pad(part, zero, (rows, (column, after, 0)))
        column += wide
    mlp_full = lax.all_gather(gathered, "fsdp", axis=0, tiled=True)

    tiles = qkv_cols // LANES
    chunk = 64
    gain_row = jnp.zeros((1, LANES), BF16)
    gain_count = 0
    for part in (norm_attn_in, norm_attn_out, norm_mlp_in, norm_mlp_out, norm_query, norm_key):
        wide = part.shape[0]
        gain_row = gain_row + jnp.pad(part[None], ((0, 0), (gain_count, LANES - gain_count - wide)))
        gain_count += wide
    pack = jnp.concatenate(
        [
            jnp.concatenate([w_query, w_key_value], axis=1).reshape(shard * tiles, LANES),
            jnp.pad(gain_row, ((0, chunk - shard * tiles - 1), (0, 0))),
        ],
        axis=0,
    )
    own = spread(pack).reshape(chips * chunk, LANES)
    peer = swap_cores(own)

    key_reach = (WINDOW + tok_rows - 2) // tok_rows
    first_token = me * tok_rows
    q_index, q_seq, q_pos, q_live = token_layout(seq_start, seq_len, first_token, tok_rows)
    k_index, k_seq, k_pos, k_live = token_layout(
        seq_start, seq_len, first_token - key_reach * tok_rows, (key_reach + 1) * tok_rows
    )
    live = q_live.astype(F32)[:, None]
    q_seq, k_seq = q_seq[:, None], k_seq[None, :]
    inv_freq = theta_base ** (-2.0 * jnp.arange(head // 2, dtype=F32) / head)
    angles = q_pos.astype(F32)[:, None] * inv_freq[None, :]
    cos_vals, sin_vals = jnp.cos(angles), jnp.sin(angles)

    raw, query_low, own_kv, gains, head_gains, attn_weights = call(
        before_attention,
        (
            shape((tok_rows, qkv_cols), F32),
            shape((tok_rows, q_cols), BF16),
            shape((tok_rows, kv_cols), BF16),
            shape((8, width), F32),
            shape((8, head), F32),
            shape((2, chips * shard, qkv_cols), BF16),
        ),
        (core_arg, tokens, own, peer, cos_vals, sin_vals),
        scratch=(pltpu.VMEM((loose_rows(chips, chunk), LANES), F32),),
        specs=[SCALAR] + [WHOLE] * 5,
    )
    kv_near = shifted(own_kv, "fsdp", 1)
    kv_far = shifted(own_kv, "fsdp", 2)
    heads_low, log_total, spread_flat, spread_core = call(
        attention,
        (
            shape((tok_rows, q_cols), BF16),
            shape((tok_rows, LANES), F32),
            shape((width, size * SLOTS), BF16),
            shape((2, width, width // 2), BF16),
        ),
        (core_arg, query_low, kv_far, kv_near, own_kv, q_seq, k_seq),
        specs=[SCALAR] + [WHOLE] * 6,
        flops=20e9,
    )

    tile = 512
    blocks, strips = 8, chips // 8
    down_at = shard * gu_cols // LANES
    out_at = down_at + down_rows * (width // LANES)
    chunk_rows = out_at + 6 * SLOTS
    chunk_shape = (blocks, strips, chunk_rows, LANES)
    gain_grads, mixed, d_state, d_heads, low_own, d_gate_up, own_down, own_out, send = call(
        feed_forward,
        (
            shape((8, width), F32),
            shape((tok_rows, width), BF16),
            shape((tok_rows, width), F32),
            shape((tok_rows, q_cols), BF16),
            shape((tok_rows, width // 2), BF16),
            shape((tok_rows, gu_cols), BF16),
            shape((blocks, strips, out_at - down_at, LANES), BF16),
            shape((blocks, strips, 6 * SLOTS, LANES), BF16),
            shape(chunk_shape, BF16),
        ),
        (
            core_arg, live, gains, tokens, out_grad, heads_low, spread_flat, spread_core, mlp_full,
        ),
        scratch=(
            pltpu.VMEM((gu_cols // tile, size * SLOTS, tile), BF16),
            pltpu.VMEM((size * SLOTS, 3 * width), BF16),
            pltpu.VMEM((ff, width), BF16),
            pltpu.VMEM((tok_rows, ff), F32),
            pltpu.VMEM((tok_rows, ff), F32),
            pltpu.VMEM((tok_rows, ff), BF16),
            pltpu.VMEM((tok_rows, width), F32),
            pltpu.VMEM((tok_rows, width), F32),
            pltpu.VMEM((tok_rows, width), F32),
            pltpu.VMEM((tok_rows, size * SLOTS), F32),
            pltpu.VMEM((tok_rows, size * SLOTS), BF16),
            pltpu.VMEM((tok_rows, width), BF16),
            pltpu.VMEM((width // 2, tok_rows), BF16),
            pltpu.VMEM((tok_rows, width), BF16),
            pltpu.VMEM((loose_rows(chips, down_at), LANES), F32),
            pltpu.VMEM((blocks, strips, 2, SLOTS, width), F32),
            pltpu.VMEM((tile // (2 * down_rows) // strips, strips, 2, down_rows, width), BF16),
            pltpu.VMEM((width, size * SLOTS), BF16),
            pltpu.VMEM((2, width, width // 2), BF16),
            pltpu.VMEM((tok_rows, width), BF16),
            pltpu.VMEM((tok_rows, width), F32),
            pltpu.VMEM((tok_rows, q_cols), BF16),
            pltpu.VMEM((tok_rows, width // 2), BF16),
            pltpu.VMEM((tok_rows, gu_cols), BF16),
            pltpu.VMEM((blocks, strips, out_at - down_at, LANES), BF16),
            pltpu.VMEM((blocks, strips, 6 * SLOTS, LANES), BF16),
            pltpu.VMEM(chunk_shape, BF16),
            pltpu.VMEM((tok_rows, width), BF16),
            pltpu.VMEM((tok_rows, width), BF16),
            pltpu.VMEM((tok_rows, q_cols), BF16),
            pltpu.SemaphoreType.DMA((gu_cols // tile,)),
            pltpu.SemaphoreType.DMA((7,)),
            pltpu.SemaphoreType.DMA((9,)),
        ),
        specs=[SCALAR] + [WHOLE] * 2 + [AWAY] * 6,
        out_specs=(WHOLE,) + (AWAY,) * 8,
        flops=12e9,
    )
    arrived = swap_cores(send)

    d_query, d_own, d_near, d_far = call(
        attention_back,
        (
            shape((tok_rows, q_cols), F32),
            shape((tok_rows, kv_cols), F32),
            shape((tok_rows, kv_cols), BF16),
            shape((tok_rows, kv_cols), BF16),
        ),
        (query_low, kv_far, kv_near, own_kv, d_heads, log_total, q_seq, k_seq),
        scratch=(
            pltpu.VMEM(((key_reach + 1) * tok_rows, head), F32),
            pltpu.VMEM(((key_reach + 1) * tok_rows, head), F32),
        ),
        specs=[WHOLE] * 8,
        flops=20e9,
    )
    near = shifted(d_near, "fsdp", -1)
    far = shifted(d_far, "fsdp", -2)
    arrived, far_started = lax.optimization_barrier((arrived, d_far))
    both_mlp = call(
        own_gradients,
        shape(chunk_shape, BF16),
        (low_own, d_gate_up, own_down, own_out, arrived),
        scratch=(
            pltpu.VMEM(chunk_shape, BF16),
            pltpu.VMEM(chunk_shape, BF16),
            pltpu.VMEM((tok_rows, gu_cols), BF16),
            pltpu.VMEM((blocks, strips, out_at - down_at, LANES), BF16),
            pltpu.VMEM((blocks, strips, 6 * SLOTS, LANES), BF16),
            pltpu.VMEM((width // 2, tok_rows), BF16),
            pltpu.VMEM((loose_rows(chips, down_at), LANES), F32),
            pltpu.SemaphoreType.DMA((gu_cols // tile,)),
            pltpu.SemaphoreType.DMA((2,)),
            pltpu.SemaphoreType.DMA((blocks,)),
            pltpu.SemaphoreType.DMA((blocks,)),
        ),
        specs=[WHOLE] + [AWAY] * 4,
        out_specs=AWAY,
        flops=12e9,
        vmem=62 * 1024 * 1024,
    )
    both_mlp, near, far = lax.optimization_barrier((both_mlp, near, far))
    mlp_parts = exchange(both_mlp.reshape(chips, chunk_rows, LANES))
    tokens_grad, keep, send = call(
        after_attention,
        (
            shape((tok_rows, width), BF16),
            shape((chips * chunk, LANES), BF16),
            shape((chips * chunk, LANES), BF16),
        ),
        (
            core_arg, raw, d_query, d_own, near, far, attn_weights, tokens, gains,
            head_gains, cos_vals, sin_vals, d_state, gain_grads,
        ),
        scratch=(
            pltpu.VMEM((tok_rows, qkv_cols), BF16),
            pltpu.VMEM((loose_rows(chips, chunk), LANES), F32),
        ),
        specs=[SCALAR] + [WHOLE] * 13,
        flops=20e9,
        vmem=62 * 1024 * 1024,
    )
    both = (keep.astype(F32) + swap_cores(send).astype(F32)).astype(BF16)
    line = lax.psum_scatter(
        both, "fsdp", scatter_dimension=0, axis_index_groups=line_groups(size), tiled=True
    )
    line, mlp_parts = lax.optimization_barrier((line, mlp_parts))
    attn_parts = lax.all_to_all(
        line.reshape(chips // LINE, chunk, LANES),
        "fsdp",
        split_axis=0,
        concat_axis=0,
        tiled=True,
        axis_index_groups=plane_groups(size),
    )
    share_attn = jnp.sum(attn_parts.astype(F32), axis=0)
    share_qkv = share_attn[: shard * tiles].reshape(shard, tiles * LANES)
    share_gains = share_attn[shard * tiles, :gain_count]

    share_mlp = jnp.sum(mlp_parts.astype(F32), axis=0)
    share_gate_up = share_mlp[:down_at].reshape(shard, gu_cols)
    share_down = (
        share_mlp[down_at:out_at]
        .reshape(width // LANES, down_rows, LANES)
        .transpose(1, 0, 2)
        .reshape(down_rows, width)
    )
    share_output = (
        share_mlp[out_at : out_at + SLOTS * (width // LANES)]
        .reshape(width // LANES, SLOTS, LANES)
        .transpose(1, 0, 2)
        .reshape(SLOTS, width)
    )
    return (
        mixed,
        tokens_grad,
        share_qkv[:, :q_cols],
        share_qkv[:, q_cols:],
        share_output,
        share_gate_up,
        share_down,
        share_gains[:shard],
        share_gains[shard : 2 * shard],
        share_gains[2 * shard : 3 * shard],
        share_gains[3 * shard : 4 * shard],
        share_gains[4 * shard : 4 * shard + hshard],
        share_gains[4 * shard + hshard :],
    )


def solution(mesh):
    placed = (
        P("fsdp", None),
        P("fsdp", None),
        P(),
        P(),
        P("fsdp", None),
        P("fsdp", None),
        P("fsdp", None),
        P("fsdp", None),
        P("fsdp", None),
        P("fsdp"),
        P("fsdp"),
        P("fsdp"),
        P("fsdp"),
        P("fsdp"),
        P("fsdp"),
    )
    return jax.shard_map(
        on_device,
        mesh=mesh,
        in_specs=placed,
        out_specs=(
            P("fsdp", None),
            P("fsdp", None),
            P("fsdp", None),
            P("fsdp", None),
            P("fsdp", None),
            P("fsdp", None),
            P("fsdp", None),
            P("fsdp"),
            P("fsdp"),
            P("fsdp"),
            P("fsdp"),
            P("fsdp"),
            P("fsdp"),
        ),
        check_vma=False,
    )
```

```python
import jax
import jax.numpy as jnp
from jax import lax
from jax.experimental import pallas as pl
from jax.experimental.pallas import tpu as pltpu
from jax.sharding import PartitionSpec as P

WINDOW = 512


epsilon = 1e-06
theta_base = 10000.0
query_scale = 0.0625


def shifted(block, axis, distance):
    devices = range(lax.axis_size(axis))
    route = [(i - distance, i) for i in devices if i - distance in devices]
    return lax.ppermute(block, axis, route)


def token_layout(seq_start, seq_len, first_token, token_count):
    indices = first_token + jnp.arange(token_count, dtype=jnp.int32)
    offsets = indices[:, None] - seq_start[None, :]
    inside = (offsets >= 0) & (offsets < seq_len[None, :])
    live_mask = jnp.any(inside, axis=1)
    seq_numbers = jnp.arange(seq_start.shape[0], dtype=jnp.int32)
    seq_id = jnp.sum(jnp.where(inside, seq_numbers[None, :], 0), axis=1)
    seq_id = jnp.where(live_mask, seq_id, -1)
    positions = jnp.sum(jnp.where(inside, offsets, 0), axis=1)
    return (indices, seq_id, positions, live_mask)


BF16 = jnp.bfloat16
F32 = jnp.float32
SLOTS = 8
MASKED = -1e30
ODD = 1
VMEM_BYTES = 56 * 1024 * 1024
LANES = 128


def same_core_groups(size):
    return [[2 * chip + core for chip in range(size // 2)] for core in range(2)]


LINE = 4


def line_groups(size):
    planes = size // 2 // LINE
    return [
        [2 * (plane * LINE + x) + core for x in range(LINE)]
        for plane in range(planes)
        for core in range(2)
    ]


def plane_groups(size):
    planes = size // 2 // LINE
    return [
        [2 * (plane * LINE + x) + core for plane in range(planes)]
        for x in range(LINE)
        for core in range(2)
    ]


def line_first(place, chips):
    planes = chips // LINE
    return lax.rem(place, planes) * LINE + lax.div(place, planes)


def swap_cores(block):
    size = lax.axis_size("fsdp")
    return lax.ppermute(block, "fsdp", [(i, i ^ 1) for i in range(size)])


def exchange(blocks):
    return lax.all_to_all(
        blocks,
        "fsdp",
        split_axis=0,
        concat_axis=0,
        tiled=True,
        axis_index_groups=same_core_groups(lax.axis_size("fsdp")),
    )


def spread(block):
    chips = lax.axis_size("fsdp") // 2
    return exchange(jnp.broadcast_to(block[None], (chips,) + block.shape))


def call(kernel, outs, ins, scratch=(), specs=None, flops=4e9, out_specs=None, vmem=VMEM_BYTES):
    return pl.pallas_call(
        kernel,
        out_shape=outs,
        in_specs=specs,
        **({} if out_specs is None else {"out_specs": out_specs}),
        scratch_shapes=list(scratch),
        compiler_params=pltpu.CompilerParams(vmem_limit_bytes=vmem),
        cost_estimate=pl.CostEstimate(
            flops=int(flops), bytes_accessed=8_000_000, transcendentals=0
        ),
    )(*ins)


SCALAR = pl.BlockSpec(memory_space=pltpu.SMEM)
WHOLE = pl.BlockSpec(memory_space=pltpu.VMEM)
AWAY = pl.BlockSpec(memory_space=pl.ANY)


def shape(dims, kind):
    return jax.ShapeDtypeStruct(dims, kind)


def dot(left, right):
    return jnp.dot(left, right, preferred_element_type=F32)


def dot_nt(left, right):
    return lax.dot_general(left, right, (((1,), (1,)), ((), ())), preferred_element_type=F32)


def dot_tn(left, right):
    return lax.dot_general(left, right, (((0,), (0,)), ((), ())), preferred_element_type=F32)


def normed(values):
    scale = lax.rsqrt(jnp.mean(values * values, axis=-1, keepdims=True) + epsilon)
    return values * scale, scale


def normed_back(cot, unit, scale, gain):
    weighted = cot * gain
    inner = jnp.mean(weighted * unit, axis=-1, keepdims=True)
    return scale * (weighted - unit * inner), jnp.sum(cot * unit, axis=0, keepdims=True)


def ones_where(mask):
    return jnp.where(mask, 1.0, 0.0).astype(BF16)


def pick_flat(rows, count, per):
    place = lax.broadcasted_iota(jnp.int32, (1, count), 1)
    device, slot = lax.shift_right_logical(place, 3), place & (SLOTS - 1)
    source = jnp.where(slot < per, device * per + slot, -1)
    return ones_where(lax.broadcasted_iota(jnp.int32, (rows, count), 0) == source)


def pick_core(rows, chips, per, core, lines=False):
    place = lax.broadcasted_iota(jnp.int32, (1, chips * per), 1)
    row, chip = lax.div(place, chips), lax.rem(place, chips)
    if lines:
        chip = line_first(chip, chips)
    source = (2 * chip + core) * per + row
    return ones_where(lax.broadcasted_iota(jnp.int32, (rows, chips * per), 0) == source)


def pick_chip(rows, chips, per, core, lines=False):
    chip = lax.broadcasted_iota(jnp.int32, (1, chips), 1)
    if lines:
        chip = line_first(chip, chips)
    low = (2 * chip + core) * per
    natural = lax.broadcasted_iota(jnp.int32, (rows, chips), 0)
    return ones_where((natural >= low) & (natural < low + per))


def gain_mask(first, per, rows, columns):
    row = lax.broadcasted_iota(jnp.int32, (rows, columns), 0)
    column = lax.broadcasted_iota(jnp.int32, (rows, columns), 1)
    return row == first + lax.rem(column, per)


def turned(values, cos, sin):
    half = values.shape[-1] // 2
    first, second = values[:, :half], values[:, half:]
    return jnp.concatenate([first * cos - second * sin, second * cos + first * sin], axis=1)


def before_attention(
    core_ref, tok, own, peer, cos, sin, raw, query_low, own_kv, gains, head_gains, weights, loose
):
    core = core_ref[0]
    width = tok.shape[1]
    kv_cols = own_kv.shape[1]
    head = kv_cols // 2
    q_cols = query_low.shape[1]
    columns = q_cols + kv_cols
    tiles = columns // LANES
    per, per_head = width // LANES, head // LANES
    chips = weights.shape[1] // per
    chunk = own.shape[0] // chips
    wide = jnp.zeros((width, LANES), F32)
    narrow = jnp.zeros((head, LANES), F32)
    stride = chunk + ODD
    for which, (block, parity) in enumerate(((own, core), (peer, 1 - core))):
        for chip in range(chips):
            loose[chip * stride : chip * stride + chunk, :] = block[
                chip * chunk : (chip + 1) * chunk, :
            ].astype(F32)
        for row in range(per):
            for tile in range(tiles):
                weights[
                    which, row * chips : (row + 1) * chips, tile * LANES : (tile + 1) * LANES
                ] = loose[pl.ds(row * tiles + tile, chips, stride=stride), :].astype(BF16)
        found = loose[pl.ds(per * tiles, chips, stride=stride), :].astype(BF16)
        wide += dot(pick_chip(width, chips, per, parity), found)
        narrow += dot(pick_chip(head, chips, per_head, parity), found)
    wide, narrow = jnp.transpose(wide)[:32], jnp.transpose(narrow)[:32]
    for which in range(4):
        mask = gain_mask(which * per, per, 32, width)
        gains[which : which + 1, :] = jnp.sum(jnp.where(mask, wide, 0.0), 0, keepdims=True)
    for which in range(2):
        mask = gain_mask(4 * per + which * per_head, per_head, 32, head)
        head_gains[which : which + 1, :] = jnp.sum(jnp.where(mask, narrow, 0.0), 0, keepdims=True)
    unit, _ = normed(tok[...].astype(F32))
    low = (unit * gains[0:1, :]).astype(BF16)
    raw[...] = dot(dot(low, pick_core(width, chips, per, core)).astype(BF16), weights[0]) + dot(
        dot(low, pick_core(width, chips, per, 1 - core)).astype(BF16), weights[1]
    )
    for index in range(q_cols // head):
        span = slice(index * head, (index + 1) * head)
        unit, _ = normed(raw[:, span])
        query_low[:, span] = turned(unit * head_gains[0:1, :], cos[...], sin[...]).astype(BF16)
    unit, _ = normed(raw[:, q_cols : q_cols + head])
    own_kv[:, :head] = turned(unit * head_gains[1:2, :], cos[...], sin[...]).astype(BF16)
    own_kv[:, head:] = raw[:, q_cols + head :].astype(BF16)


def visible(q_seq, k_seq):
    queries, keys = q_seq.shape[0], k_seq.shape[1]
    row = lax.broadcasted_iota(jnp.int32, (queries, keys), 0)
    column = lax.broadcasted_iota(jnp.int32, (queries, keys), 1)
    distance = row - column + (keys - queries)
    same = (q_seq[...] == k_seq[...]) & (q_seq[...] >= 0)
    return (same & (distance >= 0) & (distance < WINDOW)) | (distance == 0)


def attention(
    core_ref, query_low, kv_far, kv_near, kv_own, q_seq, k_seq,
    heads_low, log_total, spread_flat, spread_core,
):
    core = core_ref[0]
    width, per_core = spread_core.shape[1:]
    per = width // LANES
    spread_flat[...] = pick_flat(width, spread_flat.shape[1], per)
    for which, parity in enumerate((core, 1 - core)):
        spread_core[which] = pick_core(width, per_core // per, per, parity)
    head = kv_own.shape[1] // 2
    parts = (kv_far, kv_near, kv_own)
    keys = jnp.concatenate([part[:, :head] for part in parts], axis=0)
    values = jnp.concatenate([part[:, head:] for part in parts], axis=0)
    allowed = visible(q_seq, k_seq)
    for index in range(query_low.shape[1] // head):
        span = slice(index * head, (index + 1) * head)
        scores = dot_nt(query_low[:, span], keys) * query_scale
        scores = jnp.where(allowed, scores, MASKED)
        top = jnp.max(scores, axis=-1, keepdims=True)
        terms = jnp.exp(scores - top)
        total = jnp.sum(terms, axis=-1, keepdims=True)
        probs = (terms * (1.0 / total)).astype(BF16)
        heads_low[:, span] = dot(probs, values).astype(BF16)
        log_total[:, index : index + 1] = top + jnp.log(total)


def feed_forward(
    core_ref, live, gains, tok_in, out_grad_in, heads_in, spread_flat_in, spread_core_in, full,
    gain_grads, mixed_out, d_state_out, d_heads_out, low_own_out, d_gate_up_out, own_down_out,
    own_out_out, send_out,
    weights, rest, down, act, act_slope, hidden, proj, state, total, back, low_flat, low, turned_low,
    low_branch, loose, loose_out, turn_down, spread_flat, spread_core, mixed, d_state, d_heads,
    low_own, d_gate_up, own_down, own_out, send, tok, out_grad, heads_low,
    weight_sem, rest_sem, out_sem,
):
    core = core_ref[0]
    tiles, tile = weights.shape[0], weights.shape[2]
    half = tiles // 2
    width = state.shape[1]
    q_cols = heads_low.shape[1]
    per = width // LANES
    blocks, strips, down_rows = send.shape[0], send.shape[1], turn_down.shape[3]
    chips = blocks * strips
    tile_chips = tile // (2 * down_rows)
    tile_rows = tile // down_rows * SLOTS
    columns_at = tiles * tile

    def weight_copy(index):
        return pltpu.make_async_copy(
            full.at[:, pl.ds(pl.multiple_of(index * tile, tile), tile)],
            weights.at[index],
            weight_sem.at[index],
        )

    def rest_copy(which, first, last):
        return pltpu.make_async_copy(
            full.at[:, columns_at + first : columns_at + last],
            rest.at[:, first:last],
            rest_sem.at[which],
        )

    out_copy = rest_copy(0, 2 * width, 3 * width)
    down_copy = rest_copy(1, 0, 2 * width)
    flat_copy = pltpu.make_async_copy(spread_flat_in, spread_flat, rest_sem.at[2])
    core_copy = pltpu.make_async_copy(spread_core_in, spread_core, rest_sem.at[3])
    heads_copy = pltpu.make_async_copy(heads_in, heads_low, rest_sem.at[4])
    tok_copy = pltpu.make_async_copy(tok_in, tok, rest_sem.at[5])
    grad_copy = pltpu.make_async_copy(out_grad_in, out_grad, rest_sem.at[6])
    heads_copy.start()
    out_copy.start()
    tok_copy.start()
    flat_copy.start()
    down_copy.start()
    for index in range(half):
        weight_copy(index).start()
        weight_copy(half + index).start()
    core_copy.start()
    grad_copy.start()
    leaving = []

    def leave(source, target):
        leaving.append(pltpu.make_async_copy(source, target, out_sem.at[len(leaving)]))
        leaving[-1].start()

    heads_copy.wait()
    out_copy.wait()
    w_out = rest[:, 2 * width :]
    proj[...] = dot(heads_low[...], w_out)
    tok_copy.wait()
    unit, _ = normed(proj[...])
    state[...] = tok[...].astype(F32) + unit * gains[1:2, :]
    unit, scale = normed(state[...])
    low[...] = (unit * gains[2:3, :]).astype(BF16)
    flat_copy.wait()
    low_flat[...] = dot(low[...], spread_flat[...]).astype(BF16)
    total[...] = jnp.zeros_like(total)
    down_copy.wait()

    def down_tile(index):
        return down[pl.ds(pl.multiple_of(index * tile, tile), tile)]

    def forward(index, carry):
        columns = pl.ds(pl.multiple_of(index * tile, tile), tile)
        stored = rest[pl.ds(pl.multiple_of(index * tile_rows, tile_rows), tile_rows), : 2 * width]
        stored = stored.astype(F32).reshape(tile_rows // SLOTS, SLOTS, 2 * width)
        down[pl.ds(pl.multiple_of(index * tile, tile), tile)] = (
            jnp.concatenate([stored[:, :, :width], stored[:, :, width:]], axis=1)
            .reshape(tile, width)
            .astype(BF16)
        )
        weight_copy(index).wait()
        weight_copy(half + index).wait()
        gate = dot(low_flat[...], weights[index])
        up = dot(low_flat[...], weights[half + index])
        square = gate * gate
        bend = jnp.tanh(gate * (0.7978845608028654 * (1.0 + 0.044715 * square)))
        rise = 0.5 * (1.0 + bend)
        gelu = gate * rise
        slope = rise + 0.5 * gate * (1.0 - bend * bend) * (
            0.7978845608028654 * (1.0 + 0.134145 * square)
        )
        act[:, columns] = gelu
        act_slope[:, columns] = up * slope
        hidden[:, columns] = (gelu * up).astype(BF16)
        total[...] += dot(hidden[:, columns], down_tile(index))
        return carry

    lax.fori_loop(0, half, forward, 0, unroll=True)
    core_copy.wait()
    low_own[...] = dot(low[...], spread_core[0]).astype(BF16)
    turned_low[...] = jnp.transpose(dot(low[...], spread_core[1])).astype(BF16)
    leave(low_own, low_own_out)

    branch_unit, branch_scale = normed(total[...])
    mixed[...] = ((state[...] + branch_unit * gains[3:4, :]) * live[...]).astype(BF16)
    leave(mixed, mixed_out)
    grad_copy.wait()
    cotangent = out_grad[...].astype(F32) * live[...]
    d_branch, gain_grads[3:4, :] = normed_back(
        cotangent, branch_unit, branch_scale, gains[3:4, :]
    )
    low_branch[...] = d_branch.astype(BF16)
    back[...] = jnp.zeros_like(back)

    row_tiles = tiles * tile // LANES
    chunk = per * row_tiles

    def place(start, grad):
        place_rows(loose, dot(turned_low[...], grad), start, per, chips, row_tiles)

    down_at = chunk
    out_at = down_at + down_rows * (width // LANES)

    def backward(index, carry):
        columns = pl.ds(pl.multiple_of(index * tile, tile), tile)
        d_hidden = dot_nt(low_branch[...], down_tile(index))
        d_gate = (d_hidden * act_slope[:, columns]).astype(BF16)
        d_up = (d_hidden * act[:, columns]).astype(BF16)
        d_gate_up[:, columns] = d_gate
        d_gate_up[:, pl.ds(pl.multiple_of((half + index) * tile, tile), tile)] = d_up
        back[...] += dot_nt(d_gate, weights[index]) + dot_nt(d_up, weights[half + index])
        place(index * (tile // LANES), d_gate)
        place((half + index) * (tile // LANES), d_up)
        turn_down[...] = (
            dot_tn(hidden[:, columns], low_branch[...])
            .astype(BF16)
            .reshape(tile_chips // strips, strips, 2, down_rows, width)
        )
        tall = pl.ds(index * (tile_chips // strips), tile_chips // strips)
        for part in range(width // LANES):
            top = part * down_rows
            lanes = slice(part * LANES, (part + 1) * LANES)
            own_down[tall, :, top : top + down_rows, :] = turn_down[:, :, core, :, lanes]
            send[tall, :, down_at + top : down_at + top + down_rows, :] = turn_down[
                :, :, 1 - core, :, lanes
            ]
        return carry

    lax.fori_loop(0, half, backward, 0, unroll=True)
    leave(d_gate_up, d_gate_up_out)
    leave(own_down, own_down_out)

    def pack(block, carry):
        for strip in range(strips):
            send[block, strip, :chunk, :] = loose_chunk(loose, block * strips + strip, chunk).astype(
                BF16
            )
        return carry

    lax.fori_loop(0, blocks, pack, 0)
    leave(send.at[:, :, :out_at, :], send_out.at[:, :, :out_at, :])

    d_low = dot_nt(back[...].astype(BF16), spread_flat[...])
    d_norm, gain_grads[2:3, :] = normed_back(d_low, unit, scale, gains[2:3, :])
    d_state[...] = cotangent + d_norm
    leave(d_state, d_state_out)
    proj_unit, proj_scale = normed(proj[...])
    d_proj, gain_grads[1:2, :] = normed_back(d_state[...], proj_unit, proj_scale, gains[1:2, :])
    proj_low = d_proj.astype(BF16)
    loose_out[...] = dot_tn(heads_low[...], proj_low).reshape(blocks, strips, 2, SLOTS, width)
    out_tiles = width // LANES
    for target, parity, start in ((own_out, core, 0), (send, 1 - core, out_at)):
        for part in range(out_tiles // 2 + 1):
            lanes = [slice(i * LANES, (i + 1) * LANES) for i in (2 * part, 2 * part + 1)]
            pair = [
                loose_out[:, :, parity, :, lane]
                if lane.stop <= width
                else jnp.zeros((blocks, strips, SLOTS, LANES), F32)
                for lane in lanes
            ]
            top = start + 2 * part * SLOTS
            target[:, :, top : top + 2 * SLOTS, :] = jnp.concatenate(pair, axis=2).astype(BF16)
    leave(own_out, own_out_out)
    leave(send.at[:, :, out_at:, :], send_out.at[:, :, out_at:, :])
    d_heads[...] = dot_nt(proj_low, w_out).astype(BF16)
    leave(d_heads, d_heads_out)
    for copy in leaving:
        copy.wait()


def place_rows(loose, block, start, per, chips, row_tiles):
    stride = per * row_tiles + ODD
    for row in range(per):
        for part in range(block.shape[1] // LANES):
            loose[pl.ds(row * row_tiles + start + part, chips, stride=stride), :] = block[
                row * chips : (row + 1) * chips, part * LANES : (part + 1) * LANES
            ]


def loose_rows(chips, chunk):
    return -(-(chips + 1) * (chunk + ODD) // SLOTS) * SLOTS


def loose_chunk(loose, chip, chunk):
    return loose[pl.ds(chip * (chunk + ODD), chunk), :]


def own_gradients(
    low_own, d_gate_up_in, own_down_in, own_out_in, arrived, both_out,
    both, other, d_gate_up, own_down, own_out, turned_low, loose, tile_sem, in_sem, arrived_sem, both_sem,
):
    tile = 512
    steps = d_gate_up.shape[1] // tile

    def tile_copy(index):
        span = pl.ds(pl.multiple_of(index * tile, tile), tile)
        return pltpu.make_async_copy(
            d_gate_up_in.at[:, span], d_gate_up.at[:, span], tile_sem.at[index]
        )

    for index in range(steps):
        tile_copy(index).start()
    copies = [
        pltpu.make_async_copy(own_down_in, own_down, in_sem.at[0]),
        pltpu.make_async_copy(own_out_in, own_out, in_sem.at[1]),
    ]

    def arrival(block):
        return pltpu.make_async_copy(arrived.at[block], other.at[block], arrived_sem.at[block])

    for copy in copies:
        copy.start()
    blocks, strips, down_size = own_down.shape[:3]
    for block in range(blocks):
        arrival(block).start()
    chips = blocks * strips
    per = low_own.shape[1] // chips
    row_tiles = d_gate_up.shape[1] // LANES
    chunk = per * row_tiles
    turned_low[...] = jnp.transpose(low_own[...].astype(F32)).astype(BF16)

    def place(index, carry):
        tile_copy(index).wait()
        grad = d_gate_up[:, pl.ds(pl.multiple_of(index * tile, tile), tile)]
        block = dot(turned_low[...], grad)
        place_rows(loose, block, index * (tile // LANES), per, chips, row_tiles)
        return carry

    lax.fori_loop(0, steps, place, 0)
    for copy in copies:
        copy.wait()

    def leave(block):
        return pltpu.make_async_copy(both.at[block], both_out.at[block], both_sem.at[block])

    def pack(block, carry):
        arrival(block).wait()
        for strip in range(strips):
            both[block, strip, :chunk, :] = (
                loose_chunk(loose, block * strips + strip, chunk)
                + other[block, strip, :chunk, :].astype(F32)
            ).astype(BF16)
        low, high = chunk, chunk + down_size
        both[block, :, low:high, :] = (
            own_down[block].astype(F32) + other[block, :, low:high, :].astype(F32)
        ).astype(BF16)
        both[block, :, high:, :] = (
            own_out[block].astype(F32) + other[block, :, high:, :].astype(F32)
        ).astype(BF16)
        leave(block).start()
        return carry

    lax.fori_loop(0, blocks, pack, 0)
    for block in range(blocks):
        leave(block).wait()


def attention_back(
    query_low, kv_far, kv_near, kv_own, d_heads, log_total, q_seq, k_seq,
    d_query, d_own, d_near, d_far, sum_keys, sum_values,
):
    head = kv_own.shape[1] // 2
    rows = kv_own.shape[0]
    parts = (kv_far, kv_near, kv_own)
    keys = jnp.concatenate([part[:, :head] for part in parts], axis=0)
    values = jnp.concatenate([part[:, head:] for part in parts], axis=0)
    allowed = visible(q_seq, k_seq)
    for index in range(query_low.shape[1] // head):
        span = slice(index * head, (index + 1) * head)
        scores = dot_nt(query_low[:, span], keys) * query_scale
        scores = jnp.where(allowed, scores, MASKED)
        probs = jnp.exp(scores - log_total[:, index : index + 1])
        d_probs = dot_nt(d_heads[:, span], values)
        inner = jnp.sum(probs * d_probs, axis=-1, keepdims=True)
        d_scores = (probs * (d_probs - inner)).astype(BF16)
        d_query[:, span] = (dot(d_scores, keys) * query_scale).astype(BF16)
        key_term = dot_tn(d_scores, query_low[:, span]) * query_scale
        value_term = dot_tn(probs.astype(BF16), d_heads[:, span])
        if index == 0:
            sum_keys[...] = key_term
            sum_values[...] = value_term
        else:
            sum_keys[...] += key_term
            sum_values[...] += value_term
    for target, start in ((d_far, 0), (d_near, rows), (d_own, 2 * rows)):
        target[:, :head] = sum_keys[start : start + rows, :].astype(target.dtype)
        target[:, head:] = sum_values[start : start + rows, :].astype(target.dtype)


def after_attention(
    core_ref, raw, d_query, d_own, near, far, weights, tok, gains, head_gains, cos, sin,
    d_state, gain_grads, tokens_grad, keep, send, low, loose,
):
    core = core_ref[0]
    width = tok.shape[1]
    q_cols, kv_cols = d_query.shape[1], d_own.shape[1]
    head = kv_cols // 2
    tiles = (q_cols + kv_cols) // LANES
    per, per_head = width // LANES, head // LANES
    chips = weights.shape[1] // per
    chunk = keep.shape[0] // chips
    cosine, minus_sine = cos[...], -sin[...]
    query_gain_grad = jnp.zeros((1, head), F32)
    for index in range(q_cols // head):
        span = slice(index * head, (index + 1) * head)
        unit, scale = normed(raw[:, span])
        cot = turned(d_query[:, span].astype(F32), cosine, minus_sine)
        d_raw, part = normed_back(cot, unit, scale, head_gains[0:1, :])
        query_gain_grad += part
        low[:, span] = d_raw.astype(BF16)
    d_kv = d_own[...].astype(F32) + near[...].astype(F32) + far[...].astype(F32)
    unit, scale = normed(raw[:, q_cols : q_cols + head])
    cot = turned(d_kv[:, :head], cosine, minus_sine)
    d_raw, key_gain_grad = normed_back(cot, unit, scale, head_gains[1:2, :])
    low[:, q_cols : q_cols + head] = d_raw.astype(BF16)
    low[:, q_cols + head :] = d_kv[:, head:].astype(BF16)

    selectors = [pick_core(width, chips, per, parity) for parity in (core, 1 - core)]
    d_low = jnp.zeros(tok.shape, F32)
    for which, selector in enumerate(selectors):
        part = dot_nt(low[...], weights[which])
        high = part.astype(BF16)
        rounding = (part - high.astype(F32)).astype(BF16)
        d_low += dot_nt(high, selector) + dot_nt(rounding, selector)
    unit, scale = normed(tok[...].astype(F32))
    d_norm, in_gain_grad = normed_back(d_low, unit, scale, gains[0:1, :])
    tokens_grad[...] = (d_state[...] + d_norm).astype(BF16)

    wide = jnp.zeros((LANES, width), F32)
    vectors = [in_gain_grad] + [gain_grads[i : i + 1, :] for i in range(1, 4)]
    for which, vector in enumerate(vectors):
        wide = jnp.where(gain_mask(which * per, per, LANES, width), vector, wide)
    narrow = jnp.zeros((LANES, head), F32)
    for which, vector in enumerate((query_gain_grad, key_gain_grad)):
        mask = gain_mask(4 * per + which * per_head, per_head, LANES, head)
        narrow = jnp.where(mask, vector, narrow)
    wide, narrow = wide.astype(BF16), narrow.astype(BF16)
    attn_low = (unit * gains[0:1, :]).astype(BF16)
    stride = chunk + ODD
    for row in range(per * tiles + 1, chunk):
        loose[pl.ds(row, chips, stride=stride), :] = jnp.zeros((chips, LANES), F32)
    for target, parity in ((keep, core), (send, 1 - core)):
        extra = dot(wide, pick_chip(width, chips, per, parity, lines=True)) + dot(
            narrow, pick_chip(head, chips, per_head, parity, lines=True)
        )
        selector = pick_core(width, chips, per, parity, lines=True)
        loose[pl.ds(per * tiles, chips, stride=stride), :] = jnp.transpose(extra)
        block = dot_tn(dot(attn_low, selector).astype(BF16), low[...])
        for row in range(per):
            for tile in range(tiles):
                loose[pl.ds(row * tiles + tile, chips, stride=stride), :] = block[
                    row * chips : (row + 1) * chips, tile * LANES : (tile + 1) * LANES
                ]
        for chip in range(chips):
            target[chip * chunk : (chip + 1) * chunk, :] = loose_chunk(loose, chip, chunk).astype(BF16)


def on_device(
    tokens,
    out_grad,
    seq_start,
    seq_len,
    w_query,
    w_key_value,
    w_output,
    w_gate_up,
    w_down,
    norm_attn_in,
    norm_attn_out,
    norm_mlp_in,
    norm_mlp_out,
    norm_query,
    norm_key,
):
    size = lax.axis_size("fsdp")
    chips = size // 2
    me = lax.axis_index("fsdp")
    core = me % 2
    core_arg = core.astype(jnp.int32).reshape(1)
    tok_rows, width = tokens.shape
    shard = w_query.shape[0]
    q_cols, kv_cols = w_query.shape[1], w_key_value.shape[1]
    qkv_cols = q_cols + kv_cols
    gu_cols, ff = w_gate_up.shape[1], w_down.shape[0] * size
    down_rows = w_down.shape[0]
    head = kv_cols // 2
    hshard = norm_query.shape[0]

    gathered = jnp.zeros((SLOTS, gu_cols + 3 * width), BF16)
    column = 0
    zero = jnp.zeros((), BF16)
    for part, first in ((w_gate_up, 0), (w_down, 0), (w_down, SLOTS), (w_output, 0)):
        high, wide = part.shape
        after = gathered.shape[1] - column - wide
        rows = (-first, SLOTS - high + first, 0)
        gathered = gathered + lax.pad(part, zero, (rows, (column, after, 0)))
        column += wide
    mlp_full = lax.all_gather(gathered, "fsdp", axis=0, tiled=True)

    tiles = qkv_cols // LANES
    chunk = 64
    gain_row = jnp.zeros((1, LANES), BF16)
    gain_count = 0
    for part in (norm_attn_in, norm_attn_out, norm_mlp_in, norm_mlp_out, norm_query, norm_key):
        wide = part.shape[0]
        gain_row = gain_row + jnp.pad(part[None], ((0, 0), (gain_count, LANES - gain_count - wide)))
        gain_count += wide
    pack = jnp.concatenate(
        [
            jnp.concatenate([w_query, w_key_value], axis=1).reshape(shard * tiles, LANES),
            jnp.pad(gain_row, ((0, chunk - shard * tiles - 1), (0, 0))),
        ],
        axis=0,
    )
    own = spread(pack).reshape(chips * chunk, LANES)
    peer = swap_cores(own)

    key_reach = (WINDOW + tok_rows - 2) // tok_rows
    first_token = me * tok_rows
    q_index, q_seq, q_pos, q_live = token_layout(seq_start, seq_len, first_token, tok_rows)
    k_index, k_seq, k_pos, k_live = token_layout(
        seq_start, seq_len, first_token - key_reach * tok_rows, (key_reach + 1) * tok_rows
    )
    live = q_live.astype(F32)[:, None]
    q_seq, k_seq = q_seq[:, None], k_seq[None, :]
    inv_freq = theta_base ** (-2.0 * jnp.arange(head // 2, dtype=F32) / head)
    angles = q_pos.astype(F32)[:, None] * inv_freq[None, :]
    cos_vals, sin_vals = jnp.cos(angles), jnp.sin(angles)

    raw, query_low, own_kv, gains, head_gains, attn_weights = call(
        before_attention,
        (
            shape((tok_rows, qkv_cols), F32),
            shape((tok_rows, q_cols), BF16),
            shape((tok_rows, kv_cols), BF16),
            shape((8, width), F32),
            shape((8, head), F32),
            shape((2, chips * shard, qkv_cols), BF16),
        ),
        (core_arg, tokens, own, peer, cos_vals, sin_vals),
        scratch=(pltpu.VMEM((loose_rows(chips, chunk), LANES), F32),),
        specs=[SCALAR] + [WHOLE] * 5,
    )
    kv_near = shifted(own_kv, "fsdp", 1)
    kv_far = shifted(own_kv, "fsdp", 2)
    heads_low, log_total, spread_flat, spread_core = call(
        attention,
        (
            shape((tok_rows, q_cols), BF16),
            shape((tok_rows, LANES), F32),
            shape((width, size * SLOTS), BF16),
            shape((2, width, width // 2), BF16),
        ),
        (core_arg, query_low, kv_far, kv_near, own_kv, q_seq, k_seq),
        specs=[SCALAR] + [WHOLE] * 6,
        flops=20e9,
    )

    tile = 512
    blocks, strips = 8, chips // 8
    down_at = shard * gu_cols // LANES
    out_at = down_at + down_rows * (width // LANES)
    chunk_rows = out_at + 6 * SLOTS
    chunk_shape = (blocks, strips, chunk_rows, LANES)
    gain_grads, mixed, d_state, d_heads, low_own, d_gate_up, own_down, own_out, send = call(
        feed_forward,
        (
            shape((8, width), F32),
            shape((tok_rows, width), BF16),
            shape((tok_rows, width), F32),
            shape((tok_rows, q_cols), BF16),
            shape((tok_rows, width // 2), BF16),
            shape((tok_rows, gu_cols), BF16),
            shape((blocks, strips, out_at - down_at, LANES), BF16),
            shape((blocks, strips, 6 * SLOTS, LANES), BF16),
            shape(chunk_shape, BF16),
        ),
        (
            core_arg, live, gains, tokens, out_grad, heads_low, spread_flat, spread_core, mlp_full,
        ),
        scratch=(
            pltpu.VMEM((gu_cols // tile, size * SLOTS, tile), BF16),
            pltpu.VMEM((size * SLOTS, 3 * width), BF16),
            pltpu.VMEM((ff, width), BF16),
            pltpu.VMEM((tok_rows, ff), F32),
            pltpu.VMEM((tok_rows, ff), F32),
            pltpu.VMEM((tok_rows, ff), BF16),
            pltpu.VMEM((tok_rows, width), F32),
            pltpu.VMEM((tok_rows, width), F32),
            pltpu.VMEM((tok_rows, width), F32),
            pltpu.VMEM((tok_rows, size * SLOTS), F32),
            pltpu.VMEM((tok_rows, size * SLOTS), BF16),
            pltpu.VMEM((tok_rows, width), BF16),
            pltpu.VMEM((width // 2, tok_rows), BF16),
            pltpu.VMEM((tok_rows, width), BF16),
            pltpu.VMEM((loose_rows(chips, down_at), LANES), F32),
            pltpu.VMEM((blocks, strips, 2, SLOTS, width), F32),
            pltpu.VMEM((tile // (2 * down_rows) // strips, strips, 2, down_rows, width), BF16),
            pltpu.VMEM((width, size * SLOTS), BF16),
            pltpu.VMEM((2, width, width // 2), BF16),
            pltpu.VMEM((tok_rows, width), BF16),
            pltpu.VMEM((tok_rows, width), F32),
            pltpu.VMEM((tok_rows, q_cols), BF16),
            pltpu.VMEM((tok_rows, width // 2), BF16),
            pltpu.VMEM((tok_rows, gu_cols), BF16),
            pltpu.VMEM((blocks, strips, out_at - down_at, LANES), BF16),
            pltpu.VMEM((blocks, strips, 6 * SLOTS, LANES), BF16),
            pltpu.VMEM(chunk_shape, BF16),
            pltpu.VMEM((tok_rows, width), BF16),
            pltpu.VMEM((tok_rows, width), BF16),
            pltpu.VMEM((tok_rows, q_cols), BF16),
            pltpu.SemaphoreType.DMA((gu_cols // tile,)),
            pltpu.SemaphoreType.DMA((7,)),
            pltpu.SemaphoreType.DMA((9,)),
        ),
        specs=[SCALAR] + [WHOLE] * 2 + [AWAY] * 6,
        out_specs=(WHOLE,) + (AWAY,) * 8,
        flops=12e9,
    )
    arrived = swap_cores(send)

    d_query, d_own, d_near, d_far = call(
        attention_back,
        (
            shape((tok_rows, q_cols), BF16),
            shape((tok_rows, kv_cols), BF16),
            shape((tok_rows, kv_cols), BF16),
            shape((tok_rows, kv_cols), BF16),
        ),
        (query_low, kv_far, kv_near, own_kv, d_heads, log_total, q_seq, k_seq),
        scratch=(
            pltpu.VMEM(((key_reach + 1) * tok_rows, head), F32),
            pltpu.VMEM(((key_reach + 1) * tok_rows, head), F32),
        ),
        specs=[WHOLE] * 8,
        flops=20e9,
    )
    near = shifted(d_near, "fsdp", -1)
    far = shifted(d_far, "fsdp", -2)
    arrived, far_started = lax.optimization_barrier((arrived, d_far))
    both_mlp = call(
        own_gradients,
        shape(chunk_shape, BF16),
        (low_own, d_gate_up, own_down, own_out, arrived),
        scratch=(
            pltpu.VMEM(chunk_shape, BF16),
            pltpu.VMEM(chunk_shape, BF16),
            pltpu.VMEM((tok_rows, gu_cols), BF16),
            pltpu.VMEM((blocks, strips, out_at - down_at, LANES), BF16),
            pltpu.VMEM((blocks, strips, 6 * SLOTS, LANES), BF16),
            pltpu.VMEM((width // 2, tok_rows), BF16),
            pltpu.VMEM((loose_rows(chips, down_at), LANES), F32),
            pltpu.SemaphoreType.DMA((gu_cols // tile,)),
            pltpu.SemaphoreType.DMA((2,)),
            pltpu.SemaphoreType.DMA((blocks,)),
            pltpu.SemaphoreType.DMA((blocks,)),
        ),
        specs=[WHOLE] + [AWAY] * 4,
        out_specs=AWAY,
        flops=12e9,
        vmem=62 * 1024 * 1024,
    )
    both_mlp, near, far = lax.optimization_barrier((both_mlp, near, far))
    mlp_parts = exchange(both_mlp.reshape(chips, chunk_rows, LANES))
    tokens_grad, keep, send = call(
        after_attention,
        (
            shape((tok_rows, width), BF16),
            shape((chips * chunk, LANES), BF16),
            shape((chips * chunk, LANES), BF16),
        ),
        (
            core_arg, raw, d_query, d_own, near, far, attn_weights, tokens, gains,
            head_gains, cos_vals, sin_vals, d_state, gain_grads,
        ),
        scratch=(
            pltpu.VMEM((tok_rows, qkv_cols), BF16),
            pltpu.VMEM((loose_rows(chips, chunk), LANES), F32),
        ),
        specs=[SCALAR] + [WHOLE] * 13,
        flops=20e9,
        vmem=62 * 1024 * 1024,
    )
    both = (keep.astype(F32) + swap_cores(send).astype(F32)).astype(BF16)
    line = lax.psum_scatter(
        both, "fsdp", scatter_dimension=0, axis_index_groups=line_groups(size), tiled=True
    )
    line, mlp_parts = lax.optimization_barrier((line, mlp_parts))
    attn_parts = lax.all_to_all(
        line.reshape(chips // LINE, chunk, LANES),
        "fsdp",
        split_axis=0,
        concat_axis=0,
        tiled=True,
        axis_index_groups=plane_groups(size),
    )
    share_attn = jnp.sum(attn_parts.astype(F32), axis=0)
    share_qkv = share_attn[: shard * tiles].reshape(shard, tiles * LANES)
    share_gains = share_attn[shard * tiles, :gain_count]

    share_mlp = jnp.sum(mlp_parts.astype(F32), axis=0)
    share_gate_up = share_mlp[:down_at].reshape(shard, gu_cols)
    share_down = (
        share_mlp[down_at:out_at]
        .reshape(width // LANES, down_rows, LANES)
        .transpose(1, 0, 2)
        .reshape(down_rows, width)
    )
    share_output = (
        share_mlp[out_at : out_at + SLOTS * (width // LANES)]
        .reshape(width // LANES, SLOTS, LANES)
        .transpose(1, 0, 2)
        .reshape(SLOTS, width)
    )
    return (
        mixed,
        tokens_grad,
        share_qkv[:, :q_cols],
        share_qkv[:, q_cols:],
        share_output,
        share_gate_up,
        share_down,
        share_gains[:shard],
        share_gains[shard : 2 * shard],
        share_gains[2 * shard : 3 * shard],
        share_gains[3 * shard : 4 * shard],
        share_gains[4 * shard : 4 * shard + hshard],
        share_gains[4 * shard + hshard :],
    )


def solution(mesh):
    placed = (
        P("fsdp", None),
        P("fsdp", None),
        P(),
        P(),
        P("fsdp", None),
        P("fsdp", None),
        P("fsdp", None),
        P("fsdp", None),
        P("fsdp", None),
        P("fsdp"),
        P("fsdp"),
        P("fsdp"),
        P("fsdp"),
        P("fsdp"),
        P("fsdp"),
    )
    return jax.shard_map(
        on_device,
        mesh=mesh,
        in_specs=placed,
        out_specs=(
            P("fsdp", None),
            P("fsdp", None),
            P("fsdp", None),
            P("fsdp", None),
            P("fsdp", None),
            P("fsdp", None),
            P("fsdp", None),
            P("fsdp"),
            P("fsdp"),
            P("fsdp"),
            P("fsdp"),
            P("fsdp"),
            P("fsdp"),
        ),
        check_vma=False,
    )
```
